32 devices in a mesh: parts: 2 (over x), leaf: 16 (over z, y, core).
Axes of the slice: x: 2, y: 2, z: 4, core: 2. Of those that a mesh axis runs over, the one named last changes fastest.
Arguments:
- right_side: float32 [32, 65536], P(None, ('parts', 'leaf')), parts along dimension 1, may hold values from -16 to 16
- near_pairs: int32 [2, 2048], P(None, ('parts', 'leaf')), parts along dimension 1, may hold values from 0 to 15, as said below
- near_count: int32 [32], P(('parts', 'leaf')), parts along dimension 0, may hold values from 8 to 64, as said below
- near_blocks: bfloat16 [2048, 256, 256], P(('parts', 'leaf')), parts along dimension 0, may hold values from -1 to 2
- far_pairs: int32 [2, 4096], P(None, ('parts', 'leaf')), parts along dimension 1, may hold values from 0 to 127, as said below
- coupling: bfloat16 [4096, 1024], P(('parts', 'leaf')), parts along dimension 0, may hold values from -0.21875 to 0.21875
- cluster_basis: bfloat16 [256, 32, 256], P(('parts', 'leaf')), parts along dimension 0, may hold values from -0.375 to 0.375
- cluster_slot: int32 [256], P('parts'), parts along dimension 0, may hold values from 0 to 127, as said below
Outputs:
- solution_field: float32 [32, 65536], P(None, ('parts', 'leaf')), parts along dimension 1
- residual: float32 [32, 65536], P(None, ('parts', 'leaf')), parts along dimension 1
- hessenberg: float32 [128, 32], P('parts'), parts along dimension 0
The draws below stay inside these ranges and needn't reach their ends.
There are 2 independent parts, one for each index of `parts`. The reference program is written for one: setup_inputs(seed, part) draws one part's arguments, and reference() takes and returns one part's arrays. A program takes and returns all parts, laid end to end along the dimension named above; each array names one. Nothing has to cross between parts.
Inputs may be any that keep to these rules, and one draw needn't show every extreme that they name: `near_pairs`: A device's first 8 slots pair each of its clusters with itself; in every other slot the second entry exceeds the first. Entries below 8 name the device's own clusters, higher ones the next device's clusters, which the last device never names. `near_count`: some device has exactly 64 live slots. `far_pairs`: the first number of a pair is smaller than the second. Through cluster_slot, exactly one end of each of a device's far pairs is a cluster stored on that device and the other end is stored on another device; of one device's far pairs at most 9 have their other end on any one given device, and exactly 9 for some. `cluster_slot`: each number appears once.
All inputs are finite; a program needn't handle non-finite values.
Results may differ from the reference program's by a relative error of at most 0.0078.
Values may be sent and summed in bfloat16 or wider, within the bound.
No kernel may reach another device: no remote copies, remote signals or barrier semaphores. Data moves between devices by JAX's collectives and lax.ppermute only.
A program may use at most 64 MiB of HBM per device.

```python
import jax
import jax.numpy as jnp
from jax import lax

P_SIZE = 256
R = 32
K = 32
CL_DEV = 8
NB = 64
FP = 128
NCL = 128
NFAR = 2048
N_LEAF = 16


def slot_table(key):
    clusters = CL_DEV * N_LEAF
    return jax.random.permutation(jax.random.fold_in(key, 97), clusters).astype(jnp.int32)


def draw_right_side(key, part):
    key = jax.random.fold_in(key, 15)
    rows = CL_DEV * N_LEAF * P_SIZE
    device = jnp.arange(rows, dtype=jnp.int32) // (CL_DEV * P_SIZE)
    ramp = device.astype(jnp.float32) / (N_LEAF - 1)
    values = jnp.clip(jax.random.normal(key, (R, rows), jnp.float32), -5.0, 5.0)
    scale = 1.0 + 2.0 * ramp
    return (values * scale[None, :]).astype(jnp.float32)


def draw_cluster_slot(key, part):
    slots = slot_table(key)
    return slots


def draw_near_pairs(key, part):
    key = jax.random.fold_in(key, 11)
    total = NB * N_LEAF
    first_key, second_key, third_key = jax.random.split(key, 3)
    slot_ids = jnp.arange(total, dtype=jnp.int32)
    device = slot_ids // NB
    local = slot_ids % NB
    last = device == N_LEAF - 1
    row_any = jax.random.randint(first_key, (total,), 0, CL_DEV)
    row_last = jax.random.randint(second_key, (total,), 0, CL_DEV - 1)
    row_ids = jnp.where(last, row_last, row_any)
    limit = jnp.where(last, CL_DEV, 2 * CL_DEV)
    offset = jax.random.randint(third_key, (total,), 0, 1048576)
    col_ids = row_ids + 1 + offset % (limit - 1 - row_ids)
    own = local < CL_DEV
    row_ids = jnp.where(own, local, row_ids)
    col_ids = jnp.where(own, local, col_ids)
    return jnp.stack([row_ids, col_ids], axis=0).astype(jnp.int32)


def draw_near_count(key, part):
    key = jax.random.fold_in(key, 12)
    first_key, second_key, third_key = jax.random.split(key, 3)
    first = jax.random.randint(first_key, (N_LEAF,), CL_DEV, NB + 1)
    second = jax.random.randint(second_key, (N_LEAF,), CL_DEV, NB + 1)
    counts = jnp.minimum(first, second)
    busiest = jax.random.randint(third_key, (), 0, N_LEAF)
    counts = jnp.where(jnp.arange(N_LEAF, dtype=jnp.int32) == busiest, NB, counts)
    return counts.astype(jnp.int32)


def draw_near_blocks(key, part):
    key = jax.random.fold_in(key, 13)
    total = NB * N_LEAF
    spread = 0.16 / P_SIZE ** 0.5
    noise = jnp.clip(jax.random.normal(key, (total, P_SIZE, P_SIZE), jnp.float32), -5.0, 5.0) * spread
    own = jnp.arange(total, dtype=jnp.int32) % NB < CL_DEV
    diagonal = jnp.eye(P_SIZE, dtype=jnp.float32)[None, :, :] * own.astype(jnp.float32)[:, None, None]
    return (noise + diagonal).astype(jnp.bfloat16)


def draw_far_pairs(key, part):
    slots = slot_table(key)
    key = jax.random.fold_in(key, 14)
    clusters = CL_DEV * N_LEAF
    per_peer = (FP + N_LEAF - 2) // (N_LEAF - 1)
    order_key, offset_key, own_key, other_key = jax.random.split(key, 4)
    order = jax.vmap(lambda k: jax.random.permutation(k, FP))(jax.random.split(order_key, N_LEAF))
    offsets = jax.vmap(lambda k: jax.random.permutation(k, N_LEAF - 1))(jax.random.split(offset_key, N_LEAF))
    group = (order // per_peer).astype(jnp.int32)
    step = jnp.take_along_axis(offsets.astype(jnp.int32), group, axis=1) + 1
    device = jnp.arange(N_LEAF, dtype=jnp.int32)[:, None]
    target = (device + step) % N_LEAF
    own_local = jax.random.randint(own_key, (N_LEAF, FP), 0, CL_DEV)
    other_local = jax.random.randint(other_key, (N_LEAF, FP), 0, CL_DEV)
    own_store = (device * CL_DEV + own_local).reshape(-1)
    other_store = (target * CL_DEV + other_local).reshape(-1)
    inverse = jnp.zeros((clusters,), jnp.int32).at[slots].set(jnp.arange(clusters, dtype=jnp.int32))
    first_geo = inverse[own_store]
    second_geo = inverse[other_store]
    lower = jnp.minimum(first_geo, second_geo)
    upper = jnp.maximum(first_geo, second_geo)
    return jnp.stack([lower, upper], axis=0).astype(jnp.int32)


def block_scale(rng, shape, pieces, smallest, high):
    level, own = 1.0, jax.random.fold_in(rng, 6)
    for position, blocks in pieces:
        draws = jnp.exp(jax.random.uniform(jax.random.fold_in(own, position), (blocks,), jnp.float32, smallest / len(pieces), high / len(pieces)))
        level = level * jnp.repeat(draws, shape[position] // blocks).reshape([-1 if axis == position else 1 for axis in range(len(shape))])
    return level


def gaussian(rng, extent, scale, most, cuts=(), held_as=jnp.bfloat16):
    entries = scale * jax.random.normal(rng, extent, jnp.float32)
    if cuts:
        entries = entries * block_scale(rng, extent, cuts, -0.22, 0.18)
    return jnp.clip(entries, -most, most).astype(held_as)


def setup_inputs(seed: int = 0, part: int = 0) -> dict:
    arg_keys = jax.random.split(jax.random.key(seed), 9)
    own_keys = jax.random.split(jax.random.fold_in(arg_keys[8], part), 9)
    return {
        "right_side": draw_right_side(jax.random.fold_in(jax.random.fold_in(arg_keys[8], part), 71), part),
        "near_pairs": draw_near_pairs(jax.random.fold_in(jax.random.fold_in(arg_keys[8], part), 71), part),
        "near_count": draw_near_count(jax.random.fold_in(jax.random.fold_in(arg_keys[8], part), 71), part),
        "near_blocks": draw_near_blocks(jax.random.fold_in(jax.random.fold_in(arg_keys[8], part), 71), part),
        "far_pairs": draw_far_pairs(jax.random.fold_in(jax.random.fold_in(arg_keys[8], part), 71), part),
        "coupling": gaussian(own_keys[5], (NFAR, K * K), (25 * K) ** -0.5, 0.21875, ((0, 16),)),
        "cluster_basis": gaussian(own_keys[6], (NCL, K, P_SIZE), P_SIZE ** -0.5, 0.375, ((0, 16),)),
        "cluster_slot": draw_cluster_slot(jax.random.fold_in(jax.random.fold_in(arg_keys[8], part), 71), part),
    }


highest = lax.Precision.HIGHEST

def near_product(field_bf, near_pairs, near_count, near_blocks):
    clusters = CL_DEV * N_LEAF
    columns = jnp.transpose(field_bf.reshape(R, clusters, P_SIZE).astype(jnp.float32), (1, 0, 2))
    columns = jnp.concatenate([columns, jnp.zeros((CL_DEV, R, P_SIZE), jnp.float32)], axis=0)
    window_ids = jnp.arange(2 * CL_DEV, dtype=jnp.int32)

    def per_device(total, device):
        first = (device * CL_DEV).astype(jnp.int32)
        slot_first = (device * NB).astype(jnp.int32)
        window = lax.dynamic_slice_in_dim(columns, first, 2 * CL_DEV, 0)
        row_ids = lax.dynamic_slice_in_dim(near_pairs[0], slot_first, NB, 0)
        col_ids = lax.dynamic_slice_in_dim(near_pairs[1], slot_first, NB, 0)
        blocks = lax.dynamic_slice_in_dim(near_blocks, slot_first, NB, 0).astype(jnp.float32)
        live = (jnp.arange(NB, dtype=jnp.int32) < near_count[device]).astype(jnp.float32)
        row_hot = (row_ids[:, None] == window_ids[None, :]).astype(jnp.float32) * live[:, None]
        col_hot = (col_ids[:, None] == window_ids[None, :]).astype(jnp.float32) * live[:, None]
        rows_in = window[row_ids]
        cols_in = window[col_ids]
        to_rows = jnp.einsum('sab,srb->sra', blocks, cols_in, precision=highest)
        to_cols = jnp.einsum('sab,sra->srb', blocks, rows_in, precision=highest)
        piece = jnp.einsum('sw,sra->wra', row_hot, to_rows, precision=highest)
        piece = piece + jnp.einsum('sw,srb->wrb', col_hot, to_cols, precision=highest)
        current = lax.dynamic_slice_in_dim(total, first, 2 * CL_DEV, 0)
        total = lax.dynamic_update_slice_in_dim(total, current + piece, first, 0)
        return (total, None)
    start = jnp.zeros((clusters + CL_DEV, R, P_SIZE), jnp.float32)
    total, unused = lax.scan(per_device, start, jnp.arange(N_LEAF, dtype=jnp.int32))
    return total[:clusters]

def far_product(field_bf, cluster_basis, far_pairs, coupling, cluster_slot):
    clusters = CL_DEV * N_LEAF
    fields = field_bf.reshape(R, clusters, P_SIZE).astype(jnp.float32)
    basis_wide = cluster_basis.astype(jnp.float32)
    projection = jnp.einsum('ckp,rcp->ckr', basis_wide, fields, precision=highest)
    projection = lax.optimization_barrier(projection.astype(jnp.bfloat16)).astype(jnp.float32)
    ends_a = cluster_slot[far_pairs[0]]
    ends_b = cluster_slot[far_pairs[1]]
    blocks = coupling.reshape(-1, K, K).astype(jnp.float32)
    to_a = jnp.einsum('pkl,plr->pkr', blocks, projection[ends_b], precision=highest)
    to_b = jnp.einsum('pkl,pkr->plr', blocks, projection[ends_a], precision=highest)
    sums = jax.ops.segment_sum(jnp.concatenate([to_a, to_b], axis=0), jnp.concatenate([ends_a, ends_b], axis=0), num_segments=clusters)
    sums = lax.optimization_barrier(sums.astype(jnp.bfloat16)).astype(jnp.float32)
    return jnp.einsum('ckp,ckr->crp', basis_wide, sums, precision=highest)

def apply_operator(field, near_pairs, near_count, near_blocks, far_pairs, coupling, cluster_basis, cluster_slot):
    field_bf = lax.optimization_barrier(field.astype(jnp.bfloat16))
    result = near_product(field_bf, near_pairs, near_count, near_blocks)
    result = result + far_product(field_bf, cluster_basis, far_pairs, coupling, cluster_slot)
    return jnp.transpose(result, (1, 0, 2)).reshape(R, -1)

def reference(right_side, near_pairs, near_count, near_blocks, far_pairs, coupling, cluster_basis, cluster_slot):

    def operate(field):
        return apply_operator(field, near_pairs, near_count, near_blocks, far_pairs, coupling, cluster_basis, cluster_slot)
    gram_start = jnp.dot(right_side, right_side.T, precision=highest)
    lower_start = jnp.linalg.cholesky(gram_start)
    krylov_zero = jax.scipy.linalg.solve_triangular(lower_start, right_side, lower=True)
    image_zero = operate(krylov_zero)
    projected = jnp.dot(krylov_zero, image_zero.T, precision=highest)
    update = image_zero - jnp.dot(projected.T, krylov_zero, precision=highest)
    gram_next = jnp.dot(update, update.T, precision=highest)
    lower_next = jnp.linalg.cholesky(gram_next)
    krylov_one = jax.scipy.linalg.solve_triangular(lower_next, update, lower=True)
    image_one = operate(krylov_one)
    hessenberg = jnp.concatenate([projected, lower_next], axis=0)
    basis_all = jnp.concatenate([krylov_zero, krylov_one], axis=0)
    images = jnp.concatenate([image_zero, image_one], axis=0)
    normal = jnp.dot(images, images.T, precision=highest)
    target = jnp.dot(images, right_side.T, precision=highest)
    weights = jax.scipy.linalg.cho_solve((jnp.linalg.cholesky(normal), True), target)
    solution_field = jnp.dot(weights.T, basis_all, precision=highest)
    residual = right_side - jnp.dot(weights.T, images, precision=highest)
    return (solution_field, residual, hessenberg)
```

```python
import functools

import jax
import jax.numpy as jnp
from jax import lax
from jax.experimental import pallas as pl
from jax.experimental.pallas import tpu as pltpu
from jax.sharding import PartitionSpec as P

PANEL = 256
R = 32
K = 32
GROUP = 8
highest = lax.Precision.HIGHEST
VMEM = pltpu.VMEM
SMEM = pltpu.SMEM
TN = (((0,), (0,)), ((), ()))
NT = (((1,), (1,)), ((), ()))
f32 = jnp.float32
bf16 = jnp.bfloat16


def spec(space):
    return pl.BlockSpec(memory_space=space)


def call(kernel, outs, ins, spaces, scratch=(), limit=40, flops=10**8, moved=10**6):
    return pl.pallas_call(
        kernel,
        out_shape=outs,
        in_specs=[spec(s) for s in spaces],
        out_specs=jax.tree.map(lambda _: spec(VMEM), outs),
        scratch_shapes=list(scratch),
        compiler_params=pltpu.CompilerParams(vmem_limit_bytes=limit << 20),
        cost_estimate=pl.CostEstimate(flops=flops, bytes_accessed=moved, transcendentals=0),
    )(*ins)


def dot(x, y):
    return jnp.dot(x, y, preferred_element_type=f32)


def dot_nt(x, y):
    return lax.dot_general(x, y, NT, preferred_element_type=f32)


def exact_nt(x, y):
    return lax.dot_general(x, y, NT, precision=highest, preferred_element_type=f32)


def split_rows(x):
    high = x.astype(bf16)
    low = (x - high.astype(f32)).astype(bf16)
    return jnp.concatenate([high, low], axis=0)


def join_rows(x):
    return x[:R] + x[R:]


def lane_group(shape):
    return lax.broadcasted_iota(jnp.int32, shape, 1) // K


def project(fields, basis, clusters):
    group = lane_group((2 * R, clusters * K))
    total = jnp.zeros((2 * R, clusters * K), f32)
    for c in range(clusters):
        total = total + jnp.where(group == c, dot_nt(fields[c], basis), 0.0)
    return split_rows(join_rows(total))


def start_kernel(right_ref, basis_ref, field_ref, proj_ref):
    clusters = field_ref.shape[0]
    fields = []
    for c in range(clusters):
        field = split_rows(right_ref[:, c * PANEL : (c + 1) * PANEL])
        field_ref[c] = field
        fields.append(field)
    proj_ref[...] = project(fields, basis_ref[...], clusters)


def couple_kernel(bits, pairs_ref, slots_ref, me_ref, coupling_ref, out_ref):
    clusters = out_ref.shape[2] // K
    me = me_ref[0]
    out_ref[...] = jnp.zeros_like(out_ref)
    group = lane_group((K, clusters * K))

    def one(f, carry):
        first = slots_ref[pairs_ref[0, f]]
        second = slots_ref[pairs_ref[1, f]]
        first_home, second_home = first // clusters, second // clusters
        own = (first_home == me).astype(jnp.int32)
        apart = (first_home + second_home - me) ^ me
        place = jnp.int32(0)
        for b in range(bits):
            place = place + (((apart >> b) & 1) << (bits - 1 - b))
        block = jnp.concatenate([coupling_ref[f]] * clusters, axis=1)
        block = jnp.where(group == second % clusters, block.astype(f32), 0.0).astype(bf16)
        rows = pl.ds(pl.multiple_of((first % clusters) * K, K), K)
        where = own * (1 << bits) + place
        out_ref[where, rows, :] = out_ref[where, rows, :] + block
        return carry

    lax.fori_loop(0, pairs_ref.shape[1], one, 0)


def send_kernel(coupled_ref, proj_ref, out_ref):
    devices = out_ref.shape[0]
    proj = proj_ref[...]
    for d in range(devices):
        value = dot(proj, coupled_ref[devices + d]) + dot_nt(proj, coupled_ref[d])
        out_ref[d] = join_rows(value)


def near_specs(nb, group):
    return pl.BlockSpec((group, PANEL, PANEL), lambda g, pairs, count: (jnp.minimum(g, (count[0] - 1) // group), 0, 0))


def whole(shape):
    return pl.BlockSpec(shape, lambda g, pairs, count: (0,) * len(shape))


def near_cols_kernel(pairs_ref, count_ref, blocks_ref, field_ref, own_ref, next_ref, total):
    g = pl.program_id(0)
    clusters = field_ref.shape[0]

    @pl.when(g == 0)
    def _():
        total[...] = jnp.zeros_like(total)

    @pl.when(g * GROUP < count_ref[0])
    def _():
        for u in range(GROUP):
            s = g * GROUP + u
            i = pairs_ref[0, s]
            j = jnp.where(s < count_ref[0], pairs_ref[1, s], 2 * clusters)
            total[j] = total[j] + join_rows(dot(field_ref[i], blocks_ref[u]))

    @pl.when(g == pl.num_programs(0) - 1)
    def _():
        own_ref[...] = total[:clusters]
        next_ref[...] = total[clusters : 2 * clusters]


def near_rows_kernel(pairs_ref, count_ref, blocks_ref, field_ref, after_ref, begun_ref, out_ref, window, total):
    g = pl.program_id(0)
    clusters = field_ref.shape[0]

    @pl.when(g == 0)
    def _():
        window[:clusters] = field_ref[...]
        window[clusters:] = after_ref[...]
        total[:clusters] = begun_ref[...]

    @pl.when(g * GROUP < count_ref[0])
    def _():
        for u in range(GROUP):
            s = g * GROUP + u
            i = jnp.where(s < count_ref[0], pairs_ref[0, s], clusters)
            j = pairs_ref[1, s]
            total[i] = total[i] + join_rows(dot_nt(window[j], blocks_ref[u]))

    @pl.when(g == pl.num_programs(0) - 1)
    def _():
        out_ref[...] = total[:clusters]


def near_call(kernel, outs, near_pairs, near_count, near_blocks, arrays, scratch):
    nb = near_blocks.shape[0]
    return pl.pallas_call(
        kernel,
        out_shape=outs,
        grid_spec=pltpu.PrefetchScalarGridSpec(
            num_scalar_prefetch=2,
            grid=(nb // GROUP,),
            in_specs=[near_specs(nb, GROUP)] + [whole(a.shape) for a in arrays],
            out_specs=jax.tree.map(lambda o: whole(o.shape), outs),
            scratch_shapes=scratch,
        ),
        compiler_params=pltpu.CompilerParams(
            vmem_limit_bytes=24 << 20, dimension_semantics=("arbitrary",)
        ),
        cost_estimate=pl.CostEstimate(
            flops=nb * 64 * PANEL * PANEL * 2, bytes_accessed=nb * PANEL * PANEL * 2, transcendentals=0
        ),
    )(near_pairs, near_count, near_blocks, *arrays)


def far_fields(coupled_ref, gathered_refs, reduced_refs, basis):
    devices = coupled_ref.shape[0] // 2
    total = jnp.zeros((2 * R, basis.shape[0]), f32)
    place = 0
    for ref in gathered_refs:
        for d in range(ref.shape[0]):
            proj = ref[d]
            total = total + dot(proj, coupled_ref[place]) + dot_nt(proj, coupled_ref[devices + place])
            place += 1
    sums = join_rows(total)
    for ref in reduced_refs:
        sums = sums + ref[0]
    sums = split_rows(sums)
    group = lane_group(sums.shape)
    zero = jnp.zeros_like(sums)
    return lambda c: join_rows(dot(jnp.where(group == c, sums, zero), basis))


def finish_one_kernel(coupled_ref, near_ref, back_ref, low_ref, high_ref, kept_ref, got_ref, basis_ref,
                      image_ref, field_ref, proj_ref):
    clusters = near_ref.shape[0]
    basis = basis_ref[...]
    far = far_fields(coupled_ref, (low_ref, high_ref), (kept_ref, got_ref), basis)
    fields = []
    for c in range(clusters):
        image = near_ref[c] + back_ref[c] + far(c)
        image_ref[c] = image
        field = split_rows(image)
        field_ref[c] = field
        fields.append(field)
    proj_ref[...] = project(fields, basis, clusters)


def finish_two_kernel(coupled_ref, near_ref, back_ref, low_ref, high_ref, kept_ref, got_ref, basis_ref,
                      right_ref, image_ref, second_ref, gram_ref):
    clusters = near_ref.shape[0]
    basis = basis_ref[...]
    far = far_fields(coupled_ref, (low_ref, high_ref), (kept_ref, got_ref), basis)
    gram = jnp.zeros((4 * R, 4 * R), f32)
    for c in range(clusters):
        second = near_ref[c] + back_ref[c] + far(c)
        second_ref[c] = second
        right = right_ref[:, c * PANEL : (c + 1) * PANEL]
        rows = jnp.concatenate([right, image_ref[c], second, jnp.zeros_like(second)], axis=0)
        gram = gram + exact_nt(rows, rows)
    gram_ref[...] = gram[: 3 * R]


def column(x, k):
    return jnp.broadcast_to(x[:, k : k + 1], x.shape)


def last_kernel(kept_ref, got_ref, right_ref, image_ref, second_ref, field_ref, residual_ref, hessenberg_ref):
    clusters = image_ref.shape[0]
    gram = kept_ref[...] + got_ref[...]
    lanes = lax.broadcasted_iota(jnp.int32, (2 * R, 4 * R), 1)
    rows = lax.broadcasted_iota(jnp.int32, (2 * R, 4 * R), 0)
    system = gram[R : 3 * R]
    lower = gram[: 2 * R]
    lower = jnp.where(lanes < 2 * R, lower, jnp.where(lanes - 2 * R == rows, 1.0, 0.0))
    for k in range(2 * R):
        pivot = system[k : k + 1]
        inverse = 1.0 / pivot[:, R + k : R + k + 1]
        pivot = pivot * inverse
        factor = column(system, R + k)
        system = jnp.where(rows == k, pivot, system - factor * pivot)
        top = lower[k : k + 1]
        top = top * lax.rsqrt(top[:, k : k + 1])
        down = column(lower, k)
        scaled = lower - (down / top[:, k : k + 1]) * top
        lower = jnp.where(rows == k, top, jnp.where(rows > k, scaled, lower))
    weights = system[:, :R]
    inverse_zero = lower[:R, 2 * R : 3 * R]
    cross = lower[:R, R : 2 * R]
    corner = lower[R:, R : 2 * R]
    hessenberg_ref[:R] = exact_nt(cross, inverse_zero)
    hessenberg_ref[R:] = exact_nt(inverse_zero, corner)
    for c in range(clusters):
        right = right_ref[:, c * PANEL : (c + 1) * PANEL]
        image = image_ref[c]
        second = second_ref[c]

        def combine(x, y):
            stacked = jnp.concatenate([x, y], axis=0)
            return lax.dot_general(weights, stacked, TN, precision=highest, preferred_element_type=f32)

        field_ref[:, c * PANEL : (c + 1) * PANEL] = combine(right, image)
        residual_ref[:, c * PANEL : (c + 1) * PANEL] = right - combine(image, second)


def body(right_side, near_pairs, near_count, near_blocks, far_pairs, coupling, cluster_basis, cluster_slot):
    devices = lax.axis_size("leaf")
    bits = devices.bit_length() - 1
    clusters = cluster_basis.shape[0]
    me = lax.axis_index("leaf").astype(jnp.int32).reshape(1)
    basis = cluster_basis.reshape(clusters * K, PANEL)
    sds = jax.ShapeDtypeStruct

    def across(x, bit):
        return lax.ppermute(x, "leaf", [(i, i ^ bit) for i in range(devices)])

    def shift(x, by):
        return lax.ppermute(x, "leaf", [(i, i + by) for i in range(devices) if 0 <= i + by < devices])

    panels = sds((clusters, R, PANEL), f32)
    split = sds((clusters, 2 * R, PANEL), bf16)
    rank = sds((2 * R, clusters * K), bf16)

    field, proj = call(start_kernel, (split, rank), (right_side, basis), (VMEM, VMEM))
    coupled = call(
        functools.partial(couple_kernel, bits),
        sds((2 * devices, clusters * K, clusters * K), bf16),
        (far_pairs, cluster_slot, me, coupling.reshape(-1, K, K)),
        (SMEM, SMEM, SMEM, VMEM),
    )

    def exchange(field, proj):
        gathered = proj[None]
        after = shift(field, -1)
        sent = call(send_kernel, sds((devices, R, clusters * K), f32), (coupled, proj), (VMEM, VMEM))
        own, following = near_call(
            near_cols_kernel, (panels, panels), near_pairs, near_count, near_blocks, (field,),
            [pltpu.VMEM((2 * clusters + 1, R, PANEL), f32)],
        )
        back = shift(following, 1)
        got_gather = got_sent = None
        for b in range(bits):
            if b > 0:
                gathered = jnp.concatenate([gathered, got_gather], axis=0)
                sent = sent[: devices >> b] + got_sent
            got_gather = across(gathered, devices >> (b + 1))
            got_sent = across(sent[devices >> (b + 1) :], 1 << b)
        near = near_call(
            near_rows_kernel, panels, near_pairs, near_count, near_blocks, (field, after, own),
            [pltpu.VMEM((2 * clusters, 2 * R, PANEL), bf16), pltpu.VMEM((clusters + 1, R, PANEL), f32)],
        )
        return (coupled, near, back, gathered, got_gather, sent[:1], got_sent, basis)

    parts = exchange(field, proj)
    image, field, proj = call(finish_one_kernel, (panels, split, rank), parts, [VMEM] * 8)
    parts = exchange(field, proj)
    second, gram = call(
        finish_two_kernel, (panels, sds((3 * R, 4 * R), f32)), parts + (right_side, image), [VMEM] * 10
    )
    got = None
    for b in range(bits):
        if b > 0:
            gram = gram + got
        got = across(gram, 1 << b)
    wide = sds(right_side.shape, f32)
    return call(
        last_kernel, (wide, wide, sds((2 * R, R), f32)), (gram, got, right_side, image, second), [VMEM] * 5
    )


def solution(mesh):
    in_specs = (
        P(None, ("parts", "leaf")),
        P(None, ("parts", "leaf")),
        P(("parts", "leaf")),
        P(("parts", "leaf"), None, None),
        P(None, ("parts", "leaf")),
        P(("parts", "leaf"), None),
        P(("parts", "leaf"), None, None),
        P("parts"),
    )
    out_specs = (P(None, ("parts", "leaf")), P(None, ("parts", "leaf")), P("parts", None))
    return jax.shard_map(body, mesh=mesh, in_specs=in_specs, out_specs=out_specs, check_vma=False)
```

```python
import functools

import jax
import jax.numpy as jnp
from jax import lax
from jax.experimental import pallas as pl
from jax.experimental.pallas import tpu as pltpu
from jax.sharding import PartitionSpec as P

PANEL = 256
R = 32
K = 32
GROUP = 8
highest = lax.Precision.HIGHEST
VMEM = pltpu.VMEM
SMEM = pltpu.SMEM
TN = (((0,), (0,)), ((), ()))
NT = (((1,), (1,)), ((), ()))
f32 = jnp.float32
bf16 = jnp.bfloat16


def spec(space):
    return pl.BlockSpec(memory_space=space)


def call(kernel, outs, ins, spaces, scratch=(), limit=40, flops=10**8, moved=10**6):
    return pl.pallas_call(
        kernel,
        out_shape=outs,
        in_specs=[spec(s) for s in spaces],
        out_specs=jax.tree.map(lambda _: spec(VMEM), outs),
        scratch_shapes=list(scratch),
        compiler_params=pltpu.CompilerParams(vmem_limit_bytes=limit << 20),
        cost_estimate=pl.CostEstimate(flops=flops, bytes_accessed=moved, transcendentals=0),
    )(*ins)


def dot(x, y):
    return jnp.dot(x, y, preferred_element_type=f32)


def dot_nt(x, y):
    return lax.dot_general(x, y, NT, preferred_element_type=f32)


def exact_nt(x, y):
    return lax.dot_general(x, y, NT, precision=highest, preferred_element_type=f32)


def split_rows(x):
    high = x.astype(bf16)
    low = (x - high.astype(f32)).astype(bf16)
    return jnp.concatenate([high, low], axis=0)


def join_rows(x):
    return x[:R] + x[R:]


def lane_group(shape):
    return lax.broadcasted_iota(jnp.int32, shape, 1) // K


def project(fields, basis, clusters):
    group = lane_group((2 * R, clusters * K))
    total = jnp.zeros((2 * R, clusters * K), f32)
    for c in range(clusters):
        total = total + jnp.where(group == c, dot_nt(fields[c], basis), 0.0)
    return join_rows(total).astype(bf16)


def start_kernel(right_ref, basis_ref, field_ref, proj_ref):
    clusters = field_ref.shape[0]
    fields = []
    for c in range(clusters):
        field = split_rows(right_ref[:, c * PANEL : (c + 1) * PANEL])
        field_ref[c] = field
        fields.append(field)
    proj_ref[...] = project(fields, basis_ref[...], clusters)


def places(devices):
    bits = devices.bit_length() - 1
    order = [0] + list(range(bits - 1, 0, -1))
    place = [sum(((d >> b) & 1) << (bits - 1 - t) for t, b in enumerate(order)) for d in range(devices)]
    return order, place


def couple_kernel(order, me_ref, pairs_hbm, slots_hbm, coupling_ref, out_ref, wide, pairs_ref, slots_ref, sems):
    clusters = out_ref.shape[2] // K
    pairs = coupling_ref.shape[0] // K
    me = me_ref[0]
    copies = [
        pltpu.make_async_copy(pairs_hbm, pairs_ref, sems.at[0]),
        pltpu.make_async_copy(slots_hbm, slots_ref, sems.at[1]),
    ]
    for copy in copies:
        copy.start()
    out_ref[...] = jnp.zeros_like(out_ref)
    rows = lax.broadcasted_iota(jnp.int32, (K, clusters * K), 0)
    lanes = lax.broadcasted_iota(jnp.int32, (K, clusters * K), 1)
    spread = jnp.where(lanes % K == rows, 1.0, 0.0).astype(bf16)
    wide[...] = dot(coupling_ref[...], spread).astype(bf16)
    group = lanes // K
    for copy in copies:
        copy.wait()

    def one(f):
        first = slots_ref[pairs_ref[0, f]]
        second = slots_ref[pairs_ref[1, f]]
        first_home, second_home = first // clusters, second // clusters
        own = (first_home == me).astype(jnp.int32)
        apart = (first_home + second_home - me) ^ me
        place = jnp.int32(0)
        for t, b in enumerate(order):
            place = place + (((apart >> b) & 1) << (len(order) - 1 - t))
        block = wide[pl.ds(pl.multiple_of(f * K, K), K), :]
        block = jnp.where(group == second % clusters, block, jnp.zeros_like(block))
        here = pl.ds(pl.multiple_of((first % clusters) * K, K), K)
        where = own * (1 << len(order)) + place
        out_ref[where, here, :] = out_ref[where, here, :] + block

    def some(step, carry):
        for u in range(4):
            one(step * 4 + u)
        return carry

    lax.fori_loop(0, pairs // 4, some, 0)


def send_kernel(coupled_ref, proj_ref, out_ref):
    devices = out_ref.shape[0]
    proj = proj_ref[...]
    for d in range(devices):
        out_ref[d] = dot(proj, coupled_ref[devices + d]) + dot_nt(proj, coupled_ref[d])


def near_specs(nb, group):
    return pl.BlockSpec((group, PANEL, PANEL), lambda g, pairs, count: (jnp.minimum(g, (count[0] - 1) // group), 0, 0))


def whole(shape):
    return pl.BlockSpec(shape, lambda g, pairs, count: (0,) * len(shape))


def near_cols_kernel(pairs_ref, count_ref, blocks_ref, field_ref, own_ref, next_ref, total):
    g = pl.program_id(0)
    clusters = field_ref.shape[0]

    @pl.when(g == 0)
    def _():
        total[...] = jnp.zeros_like(total)

    @pl.when(g * GROUP < count_ref[0])
    def _():
        for u in range(GROUP):
            s = g * GROUP + u
            i = pairs_ref[0, s]
            j = jnp.where(s < count_ref[0], pairs_ref[1, s], 2 * clusters)
            total[j] = total[j] + join_rows(dot(field_ref[i], blocks_ref[u]))

    @pl.when(g == pl.num_programs(0) - 1)
    def _():
        own_ref[...] = total[:clusters]
        next_ref[...] = total[clusters : 2 * clusters].astype(bf16)


def near_rows_kernel(pairs_ref, count_ref, blocks_ref, field_ref, after_ref, begun_ref, out_ref, window, total):
    g = pl.program_id(0)
    clusters = field_ref.shape[0]

    @pl.when(g == 0)
    def _():
        window[:clusters] = field_ref[...]
        window[clusters:] = after_ref[...]
        total[:clusters] = begun_ref[...]

    @pl.when(g * GROUP < count_ref[0])
    def _():
        for u in range(GROUP):
            s = g * GROUP + u
            i = jnp.where(s < count_ref[0], pairs_ref[0, s], clusters)
            j = pairs_ref[1, s]
            total[i] = total[i] + join_rows(dot_nt(window[j], blocks_ref[u]))

    @pl.when(g == pl.num_programs(0) - 1)
    def _():
        out_ref[...] = total[:clusters]


def near_call(kernel, outs, near_pairs, near_count, near_blocks, arrays, scratch):
    nb = near_blocks.shape[0]
    return pl.pallas_call(
        kernel,
        out_shape=outs,
        grid_spec=pltpu.PrefetchScalarGridSpec(
            num_scalar_prefetch=2,
            grid=(nb // GROUP,),
            in_specs=[near_specs(nb, GROUP)] + [whole(a.shape) for a in arrays],
            out_specs=jax.tree.map(lambda o: whole(o.shape), outs),
            scratch_shapes=scratch,
        ),
        compiler_params=pltpu.CompilerParams(
            vmem_limit_bytes=24 << 20, dimension_semantics=("arbitrary",)
        ),
        cost_estimate=pl.CostEstimate(
            flops=nb * 64 * PANEL * PANEL * 2, bytes_accessed=nb * PANEL * PANEL * 2, transcendentals=0
        ),
    )(near_pairs, near_count, near_blocks, *arrays)


def far_fields(place, coupled_ref, low_ref, high_ref, kept_ref, got_ref, basis):
    devices = coupled_ref.shape[0] // 2
    sums = kept_ref[0] + got_ref[0].astype(f32)
    order = places(devices)[0]
    for g in range(devices):
        proj = low_ref[g] if g < devices // 2 else high_ref[g - devices // 2]
        apart = sum(((g >> t) & 1) << b for t, b in enumerate(order))
        sums = sums + dot(proj, coupled_ref[place[apart]]) + dot_nt(proj, coupled_ref[devices + place[apart]])
    sums = split_rows(sums)
    group = lane_group(sums.shape)
    zero = jnp.zeros_like(sums)
    return lambda c: join_rows(dot(jnp.where(group == c, sums, zero), basis))


def finish_one_kernel(place, coupled_ref, near_ref, back_ref, low_ref, high_ref, kept_ref, got_ref, basis_ref,
                      image_ref, field_ref, proj_ref):
    clusters = near_ref.shape[0]
    basis = basis_ref[...]
    far = far_fields(place, coupled_ref, low_ref, high_ref, kept_ref, got_ref, basis)
    fields = []
    for c in range(clusters):
        image = near_ref[c] + back_ref[c].astype(f32) + far(c)
        image_ref[c] = image
        field = split_rows(image)
        field_ref[c] = field
        fields.append(field)
    proj_ref[...] = project(fields, basis, clusters)


def finish_two_kernel(place, coupled_ref, near_ref, back_ref, low_ref, high_ref, kept_ref, got_ref, basis_ref,
                      right_ref, image_ref, second_ref, gram_ref):
    clusters = near_ref.shape[0]
    basis = basis_ref[...]
    far = far_fields(place, coupled_ref, low_ref, high_ref, kept_ref, got_ref, basis)
    gram = jnp.zeros((2 * R, 4 * R), f32)
    corner = jnp.zeros((R, 4 * R), f32)
    zero = jnp.zeros((R, PANEL), f32)
    for c in range(clusters):
        second = near_ref[c] + back_ref[c].astype(f32) + far(c)
        second_ref[c] = second
        right = right_ref[:, c * PANEL : (c + 1) * PANEL]
        image = image_ref[c]
        gram = gram + exact_nt(
            jnp.concatenate([image, second], axis=0), jnp.concatenate([right, image, second, zero], axis=0)
        )
        corner = corner + exact_nt(right, jnp.concatenate([zero, zero, right, zero], axis=0))
    lanes = lax.broadcasted_iota(jnp.int32, (R, 4 * R), 1)
    gram_ref[:R] = jnp.where(lanes // R == 2, corner, gram[:R])
    gram_ref[R:] = gram[R:]


def lane(x, k):
    return jnp.broadcast_to(x[:, k : k + 1], x.shape)


def last_kernel(kept_ref, got_ref, right_ref, image_ref, second_ref, field_ref, residual_ref, hessenberg_ref):
    clusters = image_ref.shape[0]
    gram = kept_ref[...] + got_ref[...]
    top, bottom = gram[:R], gram[R:]
    lanes = lax.broadcasted_iota(jnp.int32, (2 * R, 4 * R), 1)
    rows = lax.broadcasted_iota(jnp.int32, (2 * R, 4 * R), 0)
    wide = jnp.zeros((R, R), f32)
    first_first, image_first = top[:, 2 * R : 3 * R], top[:, :R]
    image_image, second_first, second_image = top[:, R : 2 * R], bottom[:, :R], bottom[:, R : 2 * R]
    second_second = bottom[:, 2 * R : 3 * R]
    system = jnp.concatenate(
        [
            jnp.concatenate([image_image, second_image.T, image_first, wide], axis=1),
            jnp.concatenate([second_image, second_second, second_first, wide], axis=1),
        ],
        axis=0,
    )
    lower = jnp.concatenate(
        [
            jnp.concatenate([first_first, image_first.T, wide, wide], axis=1),
            jnp.concatenate([image_first, image_image, wide, wide], axis=1),
        ],
        axis=0,
    )
    lower = jnp.where(lanes - 2 * R == rows, 1.0, lower)

    def two(matrix, k):
        p, q = matrix[k : k + 1], matrix[k + 1 : k + 2]
        a, b, c, d = lane(p, k), lane(p, k + 1), lane(q, k), lane(q, k + 1)
        scale = 1.0 / (a * d - b * c)
        p_new, q_new = (d * p - b * q) * scale, (a * q - c * p) * scale
        rest = matrix - lane(matrix, k) * p_new - lane(matrix, k + 1) * q_new
        return p, q, a, c, p_new, q_new, rest

    for k in range(0, 2 * R, 2):
        p, q, a, c, p_new, q_new, rest = two(system, k)
        system = jnp.where(rows == k, p_new, jnp.where(rows == k + 1, q_new, rest))
        p, q, a, c, p_new, q_new, rest = two(lower, k)
        lower = jnp.where(rows > k + 1, rest, jnp.where(rows == k + 1, q - c / a * p, lower))
    diagonal = jnp.sum(jnp.where(lanes == rows, lower, 0.0), axis=1, keepdims=True)
    lower = lower * lax.rsqrt(diagonal)
    weights = system.T[2 * R : 3 * R, : 2 * R]
    inverse_zero = lower[:R, 2 * R : 3 * R]
    hessenberg_ref[:R] = exact_nt(lower[:R, R : 2 * R], inverse_zero)
    hessenberg_ref[R:] = exact_nt(inverse_zero, lower[R:, R : 2 * R])
    for c in range(clusters):
        here = slice(c * PANEL, (c + 1) * PANEL)
        right, image, second = right_ref[:, here], image_ref[c], second_ref[c]

        def combine(x, y):
            return jnp.dot(
                weights, jnp.concatenate([x, y], axis=0), precision=highest, preferred_element_type=f32
            )

        field_ref[:, here] = combine(right, image)
        residual_ref[:, here] = right - combine(image, second)


def body(right_side, near_pairs, near_count, near_blocks, far_pairs, coupling, cluster_basis, cluster_slot):
    devices = lax.axis_size("leaf")
    order, place = places(devices)
    clusters = cluster_basis.shape[0]
    me = lax.axis_index("leaf").astype(jnp.int32).reshape(1)
    basis = cluster_basis.reshape(clusters * K, PANEL)
    sds = jax.ShapeDtypeStruct

    def across(x, b):
        return lax.ppermute(x, "leaf", [(i, i ^ (1 << b)) for i in range(devices)])

    def shift(x, by):
        return lax.ppermute(x, "leaf", [(i, i + by) for i in range(devices) if 0 <= i + by < devices])

    panels = sds((clusters, R, PANEL), f32)
    split = sds((clusters, 2 * R, PANEL), bf16)
    rank = sds((R, clusters * K), bf16)

    field, proj = call(start_kernel, (split, rank), (right_side, basis), (VMEM, VMEM))
    coupled = call(
        functools.partial(couple_kernel, order),
        sds((2 * devices, clusters * K, clusters * K), bf16),
        (me, far_pairs, cluster_slot, coupling.reshape(-1, K)),
        (SMEM, pl.ANY, pl.ANY, VMEM),
        [
            pltpu.VMEM((coupling.shape[0] * K, clusters * K), bf16),
            pltpu.SMEM(far_pairs.shape, jnp.int32),
            pltpu.SMEM(cluster_slot.shape, jnp.int32),
            pltpu.SemaphoreType.DMA((2,)),
        ],
    )

    def exchange(field, proj):
        after = shift(field, -1)
        sums = call(send_kernel, sds((devices, R, clusters * K), f32), (coupled, proj), (VMEM, VMEM))
        own, following = near_call(
            near_cols_kernel, (panels, sds(panels.shape, bf16)), near_pairs, near_count, near_blocks, (field,),
            [pltpu.VMEM((2 * clusters + 1, R, PANEL), f32)],
        )
        back = shift(following, 1)
        gathered = proj[None]
        for t, b in enumerate(order):
            held, half = gathered.shape[0], sums.shape[0] // 2
            got = across(jnp.concatenate([gathered, sums[half:].astype(bf16)], axis=0), b)
            sums, got_gathered, got_sums = sums[:half], got[:held], got[held:]
            if t < len(order) - 1:
                gathered = jnp.concatenate([gathered, got_gathered], axis=0)
                sums = sums + got_sums.astype(f32)
        near = near_call(
            near_rows_kernel, panels, near_pairs, near_count, near_blocks, (field, after, own),
            [pltpu.VMEM((2 * clusters, 2 * R, PANEL), bf16), pltpu.VMEM((clusters + 1, R, PANEL), f32)],
        )
        return (coupled, near, back, gathered, got_gathered, sums, got_sums, basis)

    parts = exchange(field, proj)
    image, field, proj = call(
        functools.partial(finish_one_kernel, place), (panels, split, rank), parts, [VMEM] * 8
    )
    parts = exchange(field, proj)
    second, gram = call(
        functools.partial(finish_two_kernel, place), (panels, sds((2 * R, 4 * R), f32)), parts + (right_side, image),
        [VMEM] * 10,
    )
    got = None
    for t, b in enumerate(order):
        if t > 0:
            gram = gram + got
        got = across(gram, b)
    wide = sds(right_side.shape, f32)
    return call(
        last_kernel, (wide, wide, sds((2 * R, R), f32)), (gram, got, right_side, image, second), [VMEM] * 5
    )


def solution(mesh):
    in_specs = (
        P(None, ("parts", "leaf")),
        P(None, ("parts", "leaf")),
        P(("parts", "leaf")),
        P(("parts", "leaf"), None, None),
        P(None, ("parts", "leaf")),
        P(("parts", "leaf"), None),
        P(("parts", "leaf"), None, None),
        P("parts"),
    )
    out_specs = (P(None, ("parts", "leaf")), P(None, ("parts", "leaf")), P("parts", None))
    return jax.shard_map(body, mesh=mesh, in_specs=in_specs, out_specs=out_specs, check_vma=False)
```

```python
import functools

import jax
import jax.numpy as jnp
from jax import lax
from jax.experimental import pallas as pl
from jax.experimental.pallas import tpu as pltpu
from jax.sharding import PartitionSpec as P

PANEL = 256
R = 32
K = 32
GROUP = 8
highest = lax.Precision.HIGHEST
VMEM = pltpu.VMEM
SMEM = pltpu.SMEM
TN = (((0,), (0,)), ((), ()))
NT = (((1,), (1,)), ((), ()))
f32 = jnp.float32
bf16 = jnp.bfloat16


def spec(space):
    return pl.BlockSpec(memory_space=space)


def call(kernel, outs, ins, spaces, scratch=(), limit=40, flops=10**8, moved=10**6):
    return pl.pallas_call(
        kernel,
        out_shape=outs,
        in_specs=[spec(s) for s in spaces],
        out_specs=jax.tree.map(lambda _: spec(VMEM), outs),
        scratch_shapes=list(scratch),
        compiler_params=pltpu.CompilerParams(vmem_limit_bytes=limit << 20),
        cost_estimate=pl.CostEstimate(flops=flops, bytes_accessed=moved, transcendentals=0),
    )(*ins)


def dot(x, y):
    return jnp.dot(x, y, preferred_element_type=f32)


def dot_nt(x, y):
    return lax.dot_general(x, y, NT, preferred_element_type=f32)


def exact_nt(x, y):
    return lax.dot_general(x, y, NT, precision=highest, preferred_element_type=f32)


def split_rows(x):
    high = x.astype(bf16)
    low = (x - high.astype(f32)).astype(bf16)
    return jnp.concatenate([high, low], axis=0)


def join_rows(x):
    return x[:R] + x[R:]


def lane_group(shape):
    return lax.broadcasted_iota(jnp.int32, shape, 1) // K


def project(fields, basis):
    clusters = fields.shape[0] // (2 * R)
    all_pairs = dot_nt(fields, basis)
    group = lane_group((2 * R, clusters * K))
    total = jnp.zeros((2 * R, clusters * K), f32)
    for c in range(clusters):
        total = total + jnp.where(group == c, all_pairs[c * 2 * R : (c + 1) * 2 * R], 0.0)
    return join_rows(total)


def expand(sums, basis):
    group = lane_group(sums.shape)
    zero = jnp.zeros_like(sums)
    spread = [jnp.where(group == c, sums, zero) for c in range(sums.shape[1] // K)]
    return dot(jnp.concatenate(spread, axis=0), basis)


def start_kernel(right_hbm, basis_hbm, field_ref, proj_ref, near_proj_ref, cross_ref, right_ref, basis_ref, sems):
    clusters = field_ref.shape[0]
    copies = [
        pltpu.make_async_copy(basis_hbm, basis_ref, sems.at[0]),
        pltpu.make_async_copy(right_hbm, right_ref, sems.at[1]),
    ]
    for copy in copies:
        copy.start()
    copies[0].wait()
    basis = basis_ref[...]
    cross = dot_nt(basis, basis)
    same = lane_group(cross.shape) == lax.broadcasted_iota(jnp.int32, cross.shape, 0) // K
    cross_ref[...] = jnp.where(same, cross, 0.0)
    copies[1].wait()
    for c in range(clusters):
        field_ref[c] = split_rows(right_ref[:, c * PANEL : (c + 1) * PANEL])
    proj = project(field_ref[...].reshape(clusters * 2 * R, PANEL), basis)
    proj_ref[...] = proj.astype(bf16)
    near_proj_ref[...] = proj


def places(devices):
    bits = devices.bit_length() - 1
    order = [0] + list(range(bits - 1, 0, -1))
    place = [sum(((d >> b) & 1) << (bits - 1 - t) for t, b in enumerate(order)) for d in range(devices)]
    return order, place


def couple_kernel(order, me_ref, pairs_hbm, slots_hbm, coupling_ref, out_ref, wide, pairs_ref, slots_ref, sems):
    clusters = out_ref.shape[2] // K
    pairs = coupling_ref.shape[0] // K
    me = me_ref[0]
    copies = [
        pltpu.make_async_copy(pairs_hbm, pairs_ref, sems.at[0]),
        pltpu.make_async_copy(slots_hbm, slots_ref, sems.at[1]),
    ]
    for copy in copies:
        copy.start()
    out_ref[...] = jnp.zeros_like(out_ref)
    rows = lax.broadcasted_iota(jnp.int32, (K, clusters * K), 0)
    lanes = lax.broadcasted_iota(jnp.int32, (K, clusters * K), 1)
    spread = jnp.where(lanes % K == rows, 1.0, 0.0).astype(bf16)
    wide[...] = dot(coupling_ref[...], spread).astype(bf16)
    group = lanes // K
    for copy in copies:
        copy.wait()

    def one(f):
        first = slots_ref[pairs_ref[0, f]]
        second = slots_ref[pairs_ref[1, f]]
        first_home, second_home = first // clusters, second // clusters
        own = (first_home == me).astype(jnp.int32)
        apart = (first_home + second_home - me) ^ me
        place = jnp.int32(0)
        for t, b in enumerate(order):
            place = place + (((apart >> b) & 1) << (len(order) - 1 - t))
        block = wide[pl.ds(pl.multiple_of(f * K, K), K), :]
        block = jnp.where(group == second % clusters, block, jnp.zeros_like(block))
        here = pl.ds(pl.multiple_of((first % clusters) * K, K), K)
        where = own * (1 << len(order)) + place
        out_ref[where, here, :] = out_ref[where, here, :] + block

    def some(step, carry):
        for u in range(4):
            one(step * 4 + u)
        return carry

    lax.fori_loop(0, pairs // 4, some, 0)


def send(coupled_ref, proj, payload_ref, kept_ref):
    half = kept_ref.shape[0]
    payload_ref[0] = proj
    for d in range(2 * half):
        value = dot(proj, coupled_ref[2 * half + d]) + dot_nt(proj, coupled_ref[d])
        if d < half:
            kept_ref[d] = value
        else:
            payload_ref[1 + d - half] = value.astype(bf16)


def send_kernel(coupled_ref, proj_ref, payload_ref, kept_ref):
    send(coupled_ref, proj_ref[...], payload_ref, kept_ref)


def near_specs(nb, group):
    return pl.BlockSpec((group, PANEL, PANEL), lambda g, pairs, count: (jnp.minimum(g, (count[0] - 1) // group), 0, 0))


def whole(shape):
    return pl.BlockSpec(shape, lambda g, pairs, count: (0,) * len(shape))


def near_cols_kernel(pairs_ref, count_ref, blocks_ref, field_ref, own_ref, next_ref, total):
    g = pl.program_id(0)
    clusters = field_ref.shape[0]

    @pl.when(g == 0)
    def _():
        total[...] = jnp.zeros_like(total)

    @pl.when(g * GROUP < count_ref[0])
    def _():
        for u in range(GROUP):
            s = g * GROUP + u
            i = pairs_ref[0, s]
            j = jnp.where(s < count_ref[0], pairs_ref[1, s], 2 * clusters)
            total[j] = total[j] + join_rows(dot(field_ref[i], blocks_ref[u]))

    @pl.when(g == pl.num_programs(0) - 1)
    def _():
        own_ref[...] = total[:clusters]
        next_ref[...] = total[clusters : 2 * clusters].astype(bf16)


def near_rows_kernel(pairs_ref, count_ref, blocks_ref, field_ref, after_ref, begun_ref, back_ref, basis_ref,
                     out_ref, proj_ref, window, total):
    g = pl.program_id(0)
    clusters = field_ref.shape[0]

    @pl.when(g == 0)
    def _():
        window[:clusters] = field_ref[...]
        window[clusters:] = after_ref[...]
        total[:clusters] = begun_ref[...] + back_ref[...].astype(f32)

    @pl.when(g * GROUP < count_ref[0])
    def _():
        for u in range(GROUP):
            s = g * GROUP + u
            i = jnp.where(s < count_ref[0], pairs_ref[0, s], clusters)
            j = pairs_ref[1, s]
            total[i] = total[i] + join_rows(dot_nt(window[j], blocks_ref[u]))

    @pl.when(g == pl.num_programs(0) - 1)
    def _():
        near = total[:clusters]
        out_ref[...] = near
        split = jnp.concatenate([split_rows(near[c]) for c in range(clusters)], axis=0)
        proj_ref[...] = project(split, basis_ref[...])


def near_call(kernel, outs, near_pairs, near_count, near_blocks, arrays, scratch):
    nb = near_blocks.shape[0]
    return pl.pallas_call(
        kernel,
        out_shape=outs,
        grid_spec=pltpu.PrefetchScalarGridSpec(
            num_scalar_prefetch=2,
            grid=(nb // GROUP,),
            in_specs=[near_specs(nb, GROUP)] + [whole(a.shape) for a in arrays],
            out_specs=jax.tree.map(lambda o: whole(o.shape), outs),
            scratch_shapes=scratch,
        ),
        compiler_params=pltpu.CompilerParams(
            vmem_limit_bytes=24 << 20, dimension_semantics=("arbitrary",)
        ),
        cost_estimate=pl.CostEstimate(
            flops=nb * 64 * PANEL * PANEL * 2, bytes_accessed=nb * PANEL * PANEL * 2, transcendentals=0
        ),
    )(near_pairs, near_count, near_blocks, *arrays)


def far_sums(place, coupled_ref, low_ref, high_ref, kept_ref, got_ref):
    devices = coupled_ref.shape[0] // 2
    sums = kept_ref[0]
    for piece in range(got_ref.shape[0]):
        sums = sums + got_ref[piece].astype(f32)
    order = places(devices)[0]
    for g in range(devices):
        proj = low_ref[g] if g < devices // 2 else high_ref[g - devices // 2]
        apart = sum(((g >> t) & 1) << b for t, b in enumerate(order))
        sums = sums + dot(proj, coupled_ref[place[apart]]) + dot_nt(proj, coupled_ref[devices + place[apart]])
    return split_rows(sums)


def exact(x, y):
    return jnp.dot(x, y, precision=highest, preferred_element_type=f32)


def turn_kernel(place, coupled_ref, low_ref, high_ref, kept_ref, got_ref, near_proj_ref, cross_ref,
                sums_ref, proj_ref, payload_ref, next_ref):
    sums = far_sums(place, coupled_ref, low_ref, high_ref, kept_ref, got_ref)
    sums_ref[...] = sums
    proj = near_proj_ref[...] + exact(join_rows(sums.astype(f32)), cross_ref[...])
    proj_ref[...] = proj
    send(coupled_ref, proj.astype(bf16), payload_ref, next_ref)


def image_kernel(near_ref, sums_ref, basis_ref, image_ref, field_ref):
    far = expand(sums_ref[...], basis_ref[...])
    for c in range(near_ref.shape[0]):
        image = near_ref[c] + join_rows(far[c * 2 * R : (c + 1) * 2 * R])
        image_ref[c] = image
        field_ref[c] = split_rows(image)


def second_kernel(near_ref, sums_ref, basis_ref, image_ref):
    far = expand(sums_ref[...], basis_ref[...])
    for c in range(near_ref.shape[0]):
        image_ref[c] = near_ref[c] + join_rows(far[c * 2 * R : (c + 1) * 2 * R])


def gram_one_kernel(right_ref, image_ref, gram_ref):
    gram = jnp.zeros((R, 4 * R), f32)
    corner = jnp.zeros((R, 4 * R), f32)
    zero = jnp.zeros((R, PANEL), f32)
    for c in range(image_ref.shape[0]):
        right, image = right_ref[:, c * PANEL : (c + 1) * PANEL], image_ref[c]
        gram = gram + exact_nt(image, jnp.concatenate([right, image, zero, zero], axis=0))
        corner = corner + exact_nt(right, jnp.concatenate([zero, zero, right, zero], axis=0))
    gram_ref[...] = gram + corner


def gram_two_kernel(right_ref, image_ref, near_ref, gram_ref):
    gram = jnp.zeros((R, 4 * R), f32)
    zero = jnp.zeros((R, PANEL), f32)
    for c in range(image_ref.shape[0]):
        right, near = right_ref[:, c * PANEL : (c + 1) * PANEL], near_ref[c]
        gram = gram + exact_nt(near, jnp.concatenate([right, image_ref[c], near, zero], axis=0))
    gram_ref[...] = gram


def tail_kernel(place, coupled_ref, low_ref, high_ref, kept_ref, got_ref, near_proj_ref, cross_ref,
                right_proj_ref, image_proj_ref, early_ref, gram_ref, sums_ref, out_ref):
    sums = far_sums(place, coupled_ref, low_ref, high_ref, kept_ref, got_ref)
    sums_ref[...] = sums
    sums = join_rows(sums.astype(f32))
    half = near_proj_ref[...] + 0.5 * exact(sums, cross_ref[...])
    known = jnp.concatenate([right_proj_ref[...], image_proj_ref[...], half, jnp.zeros_like(half)], axis=0)
    out_ref[:R] = early_ref[...]
    added = exact_nt(sums, known)
    mirror = exact_nt(half, jnp.concatenate([jnp.zeros_like(sums)] * 2 + [sums, jnp.zeros_like(sums)], axis=0))
    out_ref[R:] = gram_ref[...] + added + mirror


def lane(x, k):
    return jnp.broadcast_to(x[:, k : k + 1], x.shape)


def last_kernel(kept_ref, got_ref, right_ref, image_ref, second_ref, field_ref, residual_ref, hessenberg_ref):
    clusters = image_ref.shape[0]
    gram = kept_ref[...] + got_ref[...]
    top, bottom = gram[:R], gram[R:]
    lanes = lax.broadcasted_iota(jnp.int32, (2 * R, 4 * R), 1)
    rows = lax.broadcasted_iota(jnp.int32, (2 * R, 4 * R), 0)
    wide = jnp.zeros((R, R), f32)
    first_first, image_first = top[:, 2 * R : 3 * R], top[:, :R]
    image_image, second_first, second_image = top[:, R : 2 * R], bottom[:, :R], bottom[:, R : 2 * R]
    second_second = bottom[:, 2 * R : 3 * R]
    system = jnp.concatenate(
        [
            jnp.concatenate([image_image, second_image.T, image_first, wide], axis=1),
            jnp.concatenate([second_image, second_second, second_first, wide], axis=1),
        ],
        axis=0,
    )
    lower = jnp.concatenate(
        [
            jnp.concatenate([first_first, image_first.T, wide, wide], axis=1),
            jnp.concatenate([image_first, image_image, wide, wide], axis=1),
        ],
        axis=0,
    )
    lower = jnp.where(lanes - 2 * R == rows, 1.0, lower)

    def two(matrix, k):
        p, q = matrix[k : k + 1], matrix[k + 1 : k + 2]
        a, b, c, d = lane(p, k), lane(p, k + 1), lane(q, k), lane(q, k + 1)
        scale = 1.0 / (a * d - b * c)
        p_new, q_new = (d * p - b * q) * scale, (a * q - c * p) * scale
        rest = matrix - lane(matrix, k) * p_new - lane(matrix, k + 1) * q_new
        return p, q, a, c, p_new, q_new, rest

    for k in range(0, 2 * R, 2):
        p, q, a, c, p_new, q_new, rest = two(system, k)
        system = jnp.where(rows == k, p_new, jnp.where(rows == k + 1, q_new, rest))
        p, q, a, c, p_new, q_new, rest = two(lower, k)
        lower = jnp.where(rows > k + 1, rest, jnp.where(rows == k + 1, q - c / a * p, lower))
    diagonal = jnp.sum(jnp.where(lanes == rows, lower, 0.0), axis=1, keepdims=True)
    lower = lower * lax.rsqrt(diagonal)
    weights = system.T[2 * R : 3 * R, : 2 * R]
    inverse_zero = lower[:R, 2 * R : 3 * R]
    hessenberg_ref[:R] = exact_nt(lower[:R, R : 2 * R], inverse_zero)
    hessenberg_ref[R:] = exact_nt(inverse_zero, lower[R:, R : 2 * R])
    for c in range(clusters):
        here = slice(c * PANEL, (c + 1) * PANEL)
        right, image, second = right_ref[:, here], image_ref[c], second_ref[c]

        def combine(x, y):
            return jnp.dot(
                weights, jnp.concatenate([x, y], axis=0), precision=highest, preferred_element_type=f32
            )

        field_ref[:, here] = combine(right, image)
        residual_ref[:, here] = right - combine(image, second)


def body(right_side, near_pairs, near_count, near_blocks, far_pairs, coupling, cluster_basis, cluster_slot):
    devices = lax.axis_size("leaf")
    order, place = places(devices)
    clusters = cluster_basis.shape[0]
    me = lax.axis_index("leaf").astype(jnp.int32).reshape(1)
    basis = cluster_basis.reshape(clusters * K, PANEL)
    sds = jax.ShapeDtypeStruct

    def across(x, b):
        return lax.ppermute(x, "leaf", [(i, i ^ (1 << b)) for i in range(devices)])

    def shift(x, by):
        return lax.ppermute(x, "leaf", [(i, i + by) for i in range(devices) if 0 <= i + by < devices])

    panels = sds((clusters, R, PANEL), f32)
    narrow = sds((clusters, R, PANEL), bf16)
    split = sds((clusters, 2 * R, PANEL), bf16)
    rank = sds((R, clusters * K), bf16)
    rank_wide = sds((R, clusters * K), f32)
    rank_split = sds((2 * R, clusters * K), bf16)
    square = sds((clusters * K, clusters * K), f32)
    half = devices // 2
    payload_out = sds((1 + half, R, clusters * K), bf16)
    kept_out = sds((half, R, clusters * K), f32)
    barrier = lax.optimization_barrier

    field, proj, right_proj, cross = call(
        start_kernel, (split, rank, rank_wide, square), (right_side, basis), (pltpu.HBM, pltpu.HBM),
        [pltpu.VMEM(right_side.shape, f32), pltpu.VMEM(basis.shape, bf16), pltpu.SemaphoreType.DMA((2,))],
    )
    coupled = call(
        functools.partial(couple_kernel, order),
        sds((2 * devices, clusters * K, clusters * K), bf16),
        (me, far_pairs, cluster_slot, coupling.reshape(-1, K)),
        (SMEM, pltpu.HBM, pltpu.HBM, VMEM),
        [
            pltpu.VMEM((coupling.shape[0] * K, clusters * K), bf16),
            pltpu.SMEM(far_pairs.shape, jnp.int32),
            pltpu.SMEM(cluster_slot.shape, jnp.int32),
            pltpu.SemaphoreType.DMA((2,)),
        ],
    )

    def exchange(make_field, payload, sums):
        for t, b in enumerate(order):
            if t > 0:
                held, half = gathered.shape[0], sums.shape[0] // 2
                payload = jnp.concatenate([gathered, sums[half:].astype(bf16)], axis=0)
                sums = sums[:half]
            else:
                gathered, held = payload[:1], 1
            if t == 2:
                payload, own = barrier((payload, own))
            got = across(payload, b)
            if t == 0:
                image, field, got = make_field(got)
                after = shift(field, -1)
                own, following = near_call(
                    near_cols_kernel, (panels, narrow), near_pairs, near_count, near_blocks, (field,),
                    [pltpu.VMEM((2 * clusters + 1, R, PANEL), f32)],
                )
                back = shift(following, 1)
            if t == len(order) - 2:
                after, got = barrier((after, got))
            got_gathered, got_sums = got[:held], got[held:]
            if t < len(order) - 1:
                gathered = jnp.concatenate([gathered, got_gathered], axis=0)
                sums = sums + got_sums.astype(f32)
        near, near_proj = near_call(
            near_rows_kernel, (panels, rank_wide), near_pairs, near_count, near_blocks,
            (field, after, own, back, basis),
            [pltpu.VMEM((2 * clusters, 2 * R, PANEL), bf16), pltpu.VMEM((clusters + 1, R, PANEL), f32)],
        )
        return image, near, (coupled, gathered, got_gathered, sums, got_sums, near_proj, cross)

    def first_field(got):
        ready, got = barrier((field, got))
        return right_side, ready, got

    payload, sums = call(send_kernel, (payload_out, kept_out), (coupled, proj), (VMEM, VMEM))
    unused, near, parts = exchange(first_field, payload, sums)
    far, image_proj, payload, sums = call(
        functools.partial(turn_kernel, place), (rank_split, rank_wide, payload_out, kept_out), parts, [VMEM] * 7
    )

    def second_field(got):
        ready, got = barrier((far, got))
        return *call(image_kernel, (panels, split), (near, ready, basis), [VMEM] * 3), got

    image, near_two, parts = exchange(second_field, payload, sums)
    early = call(gram_one_kernel, sds((R, 4 * R), f32), (right_side, image), [VMEM] * 2)
    gram = call(gram_two_kernel, sds((R, 4 * R), f32), (right_side, image, near_two), [VMEM] * 3)
    far, gram = call(
        functools.partial(tail_kernel, place), (rank_split, sds((2 * R, 4 * R), f32)),
        parts + (right_proj, image_proj, early, gram), [VMEM] * 11,
    )
    got = None
    for t, b in enumerate(order):
        if t > 0:
            gram = gram + got
        if t == 2:
            gram, second = barrier((gram, second))
        got = across(gram, b)
        if t == 0:
            far, got = barrier((far, got))
            second = call(second_kernel, panels, (near_two, far, basis), [VMEM] * 3)
    wide = sds(right_side.shape, f32)
    return call(
        last_kernel, (wide, wide, sds((2 * R, R), f32)), (gram, got, right_side, image, second), [VMEM] * 5
    )


def solution(mesh):
    in_specs = (
        P(None, ("parts", "leaf")),
        P(None, ("parts", "leaf")),
        P(("parts", "leaf")),
        P(("parts", "leaf"), None, None),
        P(None, ("parts", "leaf")),
        P(("parts", "leaf"), None),
        P(("parts", "leaf"), None, None),
        P("parts"),
    )
    out_specs = (P(None, ("parts", "leaf")), P(None, ("parts", "leaf")), P("parts", None))
    return jax.shard_map(body, mesh=mesh, in_specs=in_specs, out_specs=out_specs, check_vma=False)
```

```python
import functools

import jax
import jax.numpy as jnp
from jax import lax
from jax.experimental import pallas as pl
from jax.experimental.pallas import tpu as pltpu
from jax.sharding import PartitionSpec as P

PANEL = 256
R = 32
K = 32
GROUP = 8
highest = lax.Precision.HIGHEST
VMEM = pltpu.VMEM
SMEM = pltpu.SMEM
TN = (((0,), (0,)), ((), ()))
NT = (((1,), (1,)), ((), ()))
f32 = jnp.float32
bf16 = jnp.bfloat16


def spec(space):
    return pl.BlockSpec(memory_space=space)


def call(kernel, outs, ins, spaces, scratch=(), limit=40, flops=10**8, moved=10**6, placed=None):
    return pl.pallas_call(
        kernel,
        out_shape=outs,
        in_specs=[spec(s) for s in spaces],
        out_specs=jax.tree.map(lambda _: spec(VMEM), outs) if placed is None else tuple(map(spec, placed)),
        scratch_shapes=list(scratch),
        compiler_params=pltpu.CompilerParams(vmem_limit_bytes=limit << 20),
        cost_estimate=pl.CostEstimate(flops=flops, bytes_accessed=moved, transcendentals=0),
    )(*ins)


def dot(x, y):
    return jnp.dot(x, y, preferred_element_type=f32)


def dot_nt(x, y):
    return lax.dot_general(x, y, NT, preferred_element_type=f32)


def exact_nt(x, y):
    return lax.dot_general(x, y, NT, precision=highest, preferred_element_type=f32)


def split_rows(x):
    high = x.astype(bf16)
    low = (x - high.astype(f32)).astype(bf16)
    return jnp.concatenate([high, low], axis=0)


def join_rows(x):
    return x[:R] + x[R:]


def lane_group(shape):
    return lax.broadcasted_iota(jnp.int32, shape, 1) // K


def project(fields, basis):
    clusters = fields.shape[0] // (2 * R)
    all_pairs = dot_nt(fields, basis)
    group = lane_group((2 * R, clusters * K))
    total = jnp.zeros((2 * R, clusters * K), f32)
    for c in range(clusters):
        total = total + jnp.where(group == c, all_pairs[c * 2 * R : (c + 1) * 2 * R], 0.0)
    return join_rows(total)


def expand(sums, basis):
    group = lane_group(sums.shape)
    zero = jnp.zeros_like(sums)
    spread = [jnp.where(group == c, sums, zero) for c in range(sums.shape[1] // K)]
    return dot(jnp.concatenate(spread, axis=0), basis)


def places(devices):
    bits = devices.bit_length() - 1
    order = [0] + list(range(bits - 1, 0, -1))
    place = [sum(((d >> b) & 1) << (bits - 1 - t) for t, b in enumerate(order)) for d in range(devices)]
    return order, place


def couple(order, me, pairs_ref, slots_ref, wide_ref, out_ref):
    clusters = out_ref.shape[2] // K
    pairs = wide_ref.shape[0] // K
    group = lane_group((K, clusters * K))

    def one(f):
        first = slots_ref[pairs_ref[0, f]]
        second = slots_ref[pairs_ref[1, f]]
        first_home, second_home = first // clusters, second // clusters
        own = (first_home == me).astype(jnp.int32)
        apart = (first_home + second_home - me) ^ me
        place = jnp.int32(0)
        for t, b in enumerate(order):
            place = place + (((apart >> b) & 1) << (len(order) - 1 - t))
        block = wide_ref[pl.ds(f, K, stride=pairs), :]
        block = jnp.concatenate([block] * (clusters * K // block.shape[1]), axis=1)
        block = jnp.where(group == second % clusters, block, 0.0).astype(bf16)
        here = pl.ds(pl.multiple_of((first % clusters) * K, K), K)
        where = own * (1 << len(order)) + place
        out_ref[where, here, :] = out_ref[where, here, :] + block

    def some(step, carry):
        for u in range(8):
            one(step * 8 + u)
        return carry

    lax.fori_loop(0, pairs // 8, some, 0)


def open_kernel(order, me_ref, pairs_hbm, slots_hbm, coupling_hbm, right_hbm, basis_hbm, near_hbm, blocks_hbm,
                near_pairs_ref, blocks_ref, field_ref, near_proj_ref, cross_ref, coupled_ref, payload_ref, kept_ref,
                pairs_ref, slots_ref, coupling_ref, right_ref, basis_ref, wide_ref, sems):
    clusters = field_ref.shape[0]
    moves = [(coupling_hbm, coupling_ref), (basis_hbm, basis_ref), (right_hbm, right_ref),
             (pairs_hbm, pairs_ref), (slots_hbm, slots_ref), (near_hbm, near_pairs_ref), (blocks_hbm, blocks_ref)]
    copies = [pltpu.make_async_copy(*move, sems.at[i]) for i, move in enumerate(moves)]
    for copy in copies:
        copy.start()
    coupled_ref[...] = jnp.zeros_like(coupled_ref)
    copies[0].wait()
    pairs = coupling_ref.shape[0]
    lanes_held = 128
    rows = lax.broadcasted_iota(jnp.int32, (lanes_held, lanes_held), 0)
    lanes = lax.broadcasted_iota(jnp.int32, (lanes_held, lanes_held), 1)
    tiles = coupling_ref.shape[1] // lanes_held
    flat = jnp.concatenate(
        [coupling_ref[:, t * lanes_held : (t + 1) * lanes_held] for t in range(tiles)], axis=0
    )
    each = lanes_held // K
    for u in range(each):
        spread = jnp.where((lanes % K == rows % K) & (rows // K == u), 1.0, 0.0).astype(bf16)
        value = dot(flat, spread)
        for t in range(tiles):
            wide_ref[(t * each + u) * pairs : (t * each + u + 1) * pairs] = value[t * pairs : (t + 1) * pairs]
    copies[1].wait()
    basis = basis_ref[...]
    cross = dot_nt(basis, basis)
    same = lane_group(cross.shape) == lax.broadcasted_iota(jnp.int32, cross.shape, 0) // K
    cross = jnp.where(same, cross, 0.0)
    high = cross.astype(bf16)
    cross_ref[0] = high
    cross_ref[1] = (cross - high.astype(f32)).astype(bf16)
    copies[2].wait()
    for c in range(clusters):
        field_ref[c] = split_rows(right_ref[:, c * PANEL : (c + 1) * PANEL])
    proj = project(field_ref[...].reshape(clusters * 2 * R, PANEL), basis)
    near_proj_ref[...] = proj
    copies[3].wait()
    copies[4].wait()
    copies[5].wait()
    couple(order, me_ref[0], pairs_ref, slots_ref, wide_ref, coupled_ref)
    proj = proj.astype(bf16)
    devices = coupled_ref.shape[0] // 2
    send(lambda d: dot(proj, coupled_ref[devices + d]) + dot_nt(proj, coupled_ref[d]), payload_ref, kept_ref, proj)
    copies[6].wait()


def send(products, payload_ref, kept_ref, proj):
    half = kept_ref.shape[0]
    payload_ref[0] = proj
    for d in range(2 * half):
        if d < half:
            kept_ref[d] = products(d)
        else:
            payload_ref[1 + d - half] = products(d).astype(bf16)


def near_specs(nb, group):
    return pl.BlockSpec((group, PANEL, PANEL), lambda g, pairs, count: (jnp.minimum(g, (count[0] - 1) // group), 0, 0))


def whole(shape):
    return pl.BlockSpec(shape, lambda g, pairs, count: (0,) * len(shape))


def near_cols_kernel(pairs_ref, count_ref, blocks_ref, field_ref, own_ref, next_ref, total):
    g = pl.program_id(0)
    clusters = field_ref.shape[0]

    @pl.when(g == 0)
    def _():
        total[...] = jnp.zeros_like(total)

    @pl.when(g * GROUP < count_ref[0])
    def _():
        for u in range(GROUP):
            s = g * GROUP + u
            i = pairs_ref[0, s]
            j = jnp.where(s < count_ref[0], pairs_ref[1, s], 2 * clusters)
            total[j] = total[j] + join_rows(dot(field_ref[i], blocks_ref[u]))

    @pl.when(g == pl.num_programs(0) - 1)
    def _():
        own_ref[...] = total[:clusters]
        next_ref[...] = total[clusters : 2 * clusters].astype(bf16)


def near_rows_kernel(pairs_ref, count_ref, blocks_ref, field_ref, after_ref, begun_ref, back_ref, basis_ref,
                     out_ref, proj_ref, window, total):
    g = pl.program_id(0)
    clusters = field_ref.shape[0]

    @pl.when(g == 0)
    def _():
        window[:clusters] = field_ref[...]
        window[clusters:] = after_ref[...]
        total[:clusters] = begun_ref[...] + back_ref[...].astype(f32)

    @pl.when(g * GROUP < count_ref[0])
    def _():
        for u in range(GROUP):
            s = g * GROUP + u
            i = jnp.where(s < count_ref[0], pairs_ref[0, s], clusters)
            j = pairs_ref[1, s]
            total[i] = total[i] + join_rows(dot_nt(window[j], blocks_ref[u]))

    @pl.when(g == pl.num_programs(0) - 1)
    def _():
        near = total[:clusters]
        out_ref[...] = near
        split = jnp.concatenate([split_rows(near[c]) for c in range(clusters)], axis=0)
        proj_ref[...] = project(split, basis_ref[...])


def near_call(kernel, outs, near_pairs, near_count, near_blocks, arrays, scratch):
    nb = near_blocks.shape[0]
    return pl.pallas_call(
        kernel,
        out_shape=outs,
        grid_spec=pltpu.PrefetchScalarGridSpec(
            num_scalar_prefetch=2,
            grid=(nb // GROUP,),
            in_specs=[near_specs(nb, GROUP)] + [whole(a.shape) for a in arrays],
            out_specs=jax.tree.map(lambda o: whole(o.shape), outs),
            scratch_shapes=scratch,
        ),
        compiler_params=pltpu.CompilerParams(
            vmem_limit_bytes=24 << 20, dimension_semantics=("arbitrary",)
        ),
        cost_estimate=pl.CostEstimate(
            flops=nb * 64 * PANEL * PANEL * 2, bytes_accessed=nb * PANEL * PANEL * 2, transcendentals=0
        ),
    )(near_pairs, near_count, near_blocks, *arrays)


def merge_kernel(coupled_ref, out_ref):
    devices = out_ref.shape[0]
    for d in range(devices):
        out_ref[d] = coupled_ref[d] + coupled_ref[devices + d].T


def far_sums(place, merged_ref, low_ref, high_ref, kept_ref, got_ref):
    devices = merged_ref.shape[0]
    sums = kept_ref[0]
    for piece in range(got_ref.shape[0]):
        sums = sums + got_ref[piece].astype(f32)
    order = places(devices)[0]
    for g in range(devices):
        proj = low_ref[g] if g < devices // 2 else high_ref[g - devices // 2]
        apart = sum(((g >> t) & 1) << b for t, b in enumerate(order))
        sums = sums + dot(proj, merged_ref[place[apart]])
    return split_rows(sums)


def across_clusters(sums, cross_ref):
    return join_rows(dot(sums, cross_ref[0])) + dot(sums[:R], cross_ref[1])


def turn_kernel(place, merged_ref, low_ref, high_ref, kept_ref, got_ref, near_proj_ref, cross_ref,
                sums_ref, proj_ref, payload_ref, next_ref):
    sums = far_sums(place, merged_ref, low_ref, high_ref, kept_ref, got_ref)
    sums_ref[...] = sums
    proj = near_proj_ref[...] + across_clusters(sums, cross_ref)
    proj_ref[...] = proj
    proj = proj.astype(bf16)
    send(lambda d: dot_nt(proj, merged_ref[d]), payload_ref, next_ref, proj)


def image_kernel(near_ref, sums_ref, basis_ref, image_ref, field_ref):
    far = expand(sums_ref[...], basis_ref[...])
    for c in range(near_ref.shape[0]):
        image = near_ref[c] + join_rows(far[c * 2 * R : (c + 1) * 2 * R])
        image_ref[c] = image
        field_ref[c] = split_rows(image)


def second_kernel(near_ref, sums_ref, basis_ref, image_ref):
    far = expand(sums_ref[...], basis_ref[...])
    for c in range(near_ref.shape[0]):
        image_ref[c] = near_ref[c] + join_rows(far[c * 2 * R : (c + 1) * 2 * R])


def gram_one_kernel(right_ref, image_ref, gram_ref):
    gram = jnp.zeros((R, 4 * R), f32)
    corner = jnp.zeros((R, 4 * R), f32)
    zero = jnp.zeros((R, PANEL), f32)
    for c in range(image_ref.shape[0]):
        right, image = right_ref[:, c * PANEL : (c + 1) * PANEL], image_ref[c]
        gram = gram + exact_nt(image, jnp.concatenate([right, image, zero, zero], axis=0))
        corner = corner + exact_nt(right, jnp.concatenate([zero, zero, right, zero], axis=0))
    gram_ref[...] = gram + corner


def gram_two_kernel(right_ref, image_ref, near_ref, gram_ref):
    gram = jnp.zeros((R, 4 * R), f32)
    zero = jnp.zeros((R, PANEL), f32)
    for c in range(image_ref.shape[0]):
        right, near = right_ref[:, c * PANEL : (c + 1) * PANEL], near_ref[c]
        gram = gram + exact_nt(near, jnp.concatenate([right, image_ref[c], near, zero], axis=0))
    gram_ref[...] = gram


def tail_kernel(place, merged_ref, low_ref, high_ref, kept_ref, got_ref, near_proj_ref, cross_ref,
                right_proj_ref, image_proj_ref, early_ref, gram_ref, sums_ref, out_ref):
    sums = far_sums(place, merged_ref, low_ref, high_ref, kept_ref, got_ref)
    sums_ref[...] = sums
    half = near_proj_ref[...] + 0.5 * across_clusters(sums, cross_ref)
    sums = join_rows(sums.astype(f32))
    known = jnp.concatenate([right_proj_ref[...], image_proj_ref[...], half, jnp.zeros_like(half)], axis=0)
    out_ref[:R] = early_ref[...]
    added = exact_nt(sums, known)
    mirror = exact_nt(half, jnp.concatenate([jnp.zeros_like(sums)] * 2 + [sums, jnp.zeros_like(sums)], axis=0))
    out_ref[R:] = gram_ref[...] + added + mirror


TALL = 8


def lane(x, k):
    return jnp.broadcast_to(x[:, k : k + 1], x.shape)


def eliminate(wide, late, k):
    block, at = k // TALL, k % TALL
    rows = lax.broadcasted_iota(jnp.int32, wide[block].shape, 0)
    both = [wide] if late is None or block < len(wide) // 2 else [wide, late]
    columns = [[lane(x, k + j) for x in wide[block:]] for j in range(4)]
    m = [[columns[j][0][at + i : at + i + 1] for j in range(4)] for i in range(4)]
    scale = 1.0 / (m[0][0] * m[1][1] - m[0][1] * m[1][0])
    first = {j: (m[1][1] * m[0][j] - m[0][1] * m[1][j]) * scale for j in (2, 3)}
    second = {j: (m[0][0] * m[1][j] - m[1][0] * m[0][j]) * scale for j in (2, 3)}
    s = {(i, j): m[i][j] - (m[i][0] * first[j] + m[i][1] * second[j]) for i in (2, 3) for j in (2, 3)}
    after = 1.0 / (s[2, 2] * s[3, 3] - s[2, 3] * s[3, 2])
    ratio, last_ratio = m[1][0] / m[0][0], s[3, 2] / s[2, 2]
    for part in both:
        p = [part[block][at + i : at + i + 1] for i in range(4)]
        y0 = (m[1][1] * p[0] - m[0][1] * p[1]) * scale
        y1 = (m[0][0] * p[1] - m[1][0] * p[0]) * scale
        r2 = p[2] - (m[2][0] * y0 + m[2][1] * y1)
        r3 = p[3] - (m[3][0] * y0 + m[3][1] * y1)
        x2 = (s[3, 3] * r2 - s[2, 3] * r3) * after
        x3 = (s[2, 2] * r3 - s[3, 2] * r2) * after
        x0 = y0 - (first[2] * x2 + first[3] * x3)
        x1 = y1 - (second[2] * x2 + second[3] * x3)
        own = [p[0], p[1] - ratio * p[0], r2, r3 - last_ratio * r2]
        for i in range(block, len(wide)):
            c = [column[i - block] for column in columns]
            rest = part[i] - ((c[0] * x0 + c[1] * x1) + (c[2] * x2 + c[3] * x3))
            if i == block:
                rest = jnp.where(rows > at + 3, rest, part[i])
                for t in range(1, 4):
                    rest = jnp.where(rows == at + t, own[t], rest)
            part[i] = rest


def last_kernel(kept_ref, got_ref, right_ref, image_ref, second_ref, field_ref, residual_ref, hessenberg_ref):
    clusters = image_ref.shape[0]
    gram = kept_ref[...] + got_ref[...]
    top, bottom = gram[:R], gram[R:]
    lanes = lax.broadcasted_iota(jnp.int32, (2 * R, 4 * R), 1)
    rows = lax.broadcasted_iota(jnp.int32, (2 * R, 4 * R), 0)
    wide = jnp.zeros((R, R), f32)
    first_first, image_first = top[:, 2 * R : 3 * R], top[:, :R]
    image_image, second_first, second_image = top[:, R : 2 * R], bottom[:, :R], bottom[:, R : 2 * R]
    second_second = bottom[:, 2 * R : 3 * R]
    system = jnp.concatenate(
        [
            jnp.concatenate([image_image, second_image.T, image_first, wide], axis=1),
            jnp.concatenate([second_image, second_second, second_first, wide], axis=1),
        ],
        axis=0,
    )
    lower = jnp.concatenate(
        [
            jnp.concatenate([first_first, image_first.T, wide, wide], axis=1),
            jnp.concatenate([image_first, image_image, wide, wide], axis=1),
        ],
        axis=0,
    )
    lower = jnp.where(lanes - 2 * R == rows, 1.0, lower)
    system = jnp.where(lanes - 3 * R == rows, 1.0, system)
    late = jnp.where(lanes + R == rows, 1.0, 0.0)

    def blocks(x):
        return [x[i : i + TALL] for i in range(0, 2 * R, TALL)]

    system, lower, late = blocks(system), blocks(lower), blocks(late)
    for k in range(0, 2 * R, 4):
        eliminate(system, late, k)
        eliminate(lower, None, k)
    system, lower, late = (jnp.concatenate(x, axis=0) for x in (system, lower, late))

    def diagonal(x):
        return jnp.sum(jnp.where(lanes == rows, x, 0.0), axis=1, keepdims=True)

    lower = lower * lax.rsqrt(diagonal(lower))
    scaled = system[:, 2 * R : 3 * R] / diagonal(system)
    inverse = jnp.concatenate([system[:, 3 * R :], late[:, :R]], axis=1)
    weights = lax.dot_general(scaled, inverse, TN, precision=highest, preferred_element_type=f32)
    inverse_zero = lower[:R, 2 * R : 3 * R]
    hessenberg_ref[:, :R] = exact_nt(inverse_zero, lower[:R, R : 2 * R])
    hessenberg_ref[:, R:] = lax.dot_general(
        lower[R:, R : 2 * R], inverse_zero, NT, precision=highest, preferred_element_type=f32
    )
    none = jnp.zeros((R, R), f32)
    mix = jnp.concatenate(
        [jnp.concatenate([weights, none], axis=1), jnp.concatenate([none, weights], axis=1)], axis=0
    )
    mix_high = mix.astype(bf16)
    mix_both = jnp.concatenate([mix_high, (mix - mix_high.astype(f32)).astype(bf16)], axis=0)
    for c in range(clusters):
        here = slice(c * PANEL, (c + 1) * PANEL)
        right = right_ref[:, here]
        stacked = jnp.concatenate([right, image_ref[c], second_ref[c]], axis=0)
        high = stacked.astype(bf16)
        low = (stacked - high.astype(f32)).astype(bf16)
        both = dot(mix_both, high)
        value = both[: 2 * R] + both[2 * R :] + dot(mix_high, low)
        field_ref[:, here] = value[:R]
        residual_ref[:, here] = right - value[R:]


def body(right_side, near_pairs, near_count, near_blocks, far_pairs, coupling, cluster_basis, cluster_slot):
    devices = lax.axis_size("leaf")
    order, place = places(devices)
    clusters = cluster_basis.shape[0]
    me = lax.axis_index("leaf").astype(jnp.int32).reshape(1)
    basis = cluster_basis.reshape(clusters * K, PANEL)
    sds = jax.ShapeDtypeStruct

    def across(x, b):
        return lax.ppermute(x, "leaf", [(i, i ^ (1 << b)) for i in range(devices)])

    def shift(x, by):
        return lax.ppermute(x, "leaf", [(i, i + by) for i in range(devices) if 0 <= i + by < devices])

    panels = sds((clusters, R, PANEL), f32)
    narrow = sds((clusters, R, PANEL), bf16)
    split = sds((clusters, 2 * R, PANEL), bf16)
    rank_wide = sds((R, clusters * K), f32)
    rank_split = sds((2 * R, clusters * K), bf16)
    half = devices // 2
    payload_out = sds((1 + half, R, clusters * K), bf16)
    kept_out = sds((half, R, clusters * K), f32)
    barrier = lax.optimization_barrier

    def in_hbm(x):
        return pltpu.with_memory_space_constraint(x, pltpu.HBM)

    near_pairs, near_blocks, field, right_proj, cross, coupled, payload, sums = call(
        functools.partial(open_kernel, order),
        (sds(near_pairs.shape, jnp.int32), sds(near_blocks.shape, bf16), split, rank_wide, sds((2, clusters * K, clusters * K), bf16),
         sds((2 * devices, clusters * K, clusters * K), bf16), payload_out, kept_out),
        (me, in_hbm(far_pairs), in_hbm(cluster_slot), in_hbm(coupling), in_hbm(right_side), in_hbm(basis),
         in_hbm(near_pairs), in_hbm(near_blocks)),
        [SMEM] + [pltpu.HBM] * 7,
        [
            pltpu.SMEM(far_pairs.shape, jnp.int32),
            pltpu.SMEM(cluster_slot.shape, jnp.int32),
            pltpu.VMEM(coupling.shape, bf16),
            pltpu.VMEM(right_side.shape, f32),
            pltpu.VMEM(basis.shape, bf16),
            pltpu.VMEM((coupling.shape[0] * K, 128), f32),
            pltpu.SemaphoreType.DMA((7,)),
        ],
        placed=[SMEM] + [VMEM] * 7,
    )

    def exchange(make_field, payload, sums, merged):
        for t, b in enumerate(order):
            if t > 0:
                held, half = gathered.shape[0], sums.shape[0] // 2
                payload = jnp.concatenate([gathered, sums[half:].astype(bf16)], axis=0)
                sums = sums[:half]
            else:
                gathered, held = payload[:1], 1
            if t == 2:
                payload, own = barrier((payload, own))
            if t == 3 and merged is None:
                payload, merged = barrier((payload, made))
            got = across(payload, b)
            if t == 0:
                image, field, got = make_field(got)
                after = shift(field, -1)
                own, following = near_call(
                    near_cols_kernel, (panels, narrow), near_pairs, near_count, near_blocks, (field,),
                    [pltpu.VMEM((2 * clusters + 1, R, PANEL), f32)],
                )
                back = shift(following, 1)
            if t == 1 and merged is None:
                ready, got = barrier((coupled, got))
                made = call(
                    merge_kernel, sds((devices, clusters * K, clusters * K), bf16), (ready,), [VMEM]
                )
            if t == len(order) - 2:
                after, got = barrier((after, got))
            got_gathered, got_sums = got[:held], got[held:]
            if t < len(order) - 1:
                gathered = jnp.concatenate([gathered, got_gathered], axis=0)
                sums = sums + got_sums.astype(f32)
        near, near_proj = near_call(
            near_rows_kernel, (panels, rank_wide), near_pairs, near_count, near_blocks,
            (field, after, own, back, basis),
            [pltpu.VMEM((2 * clusters, 2 * R, PANEL), bf16), pltpu.VMEM((clusters + 1, R, PANEL), f32)],
        )
        return image, near, (merged, gathered, got_gathered, sums, got_sums, near_proj, cross)

    def first_field(got):
        ready, got = barrier((field, got))
        return right_side, ready, got

    unused, near, parts = exchange(first_field, payload, sums, None)
    far, image_proj, payload, sums = call(
        functools.partial(turn_kernel, place), (rank_split, rank_wide, payload_out, kept_out), parts, [VMEM] * 7
    )

    def second_field(got):
        ready, got = barrier((far, got))
        return *call(image_kernel, (panels, split), (near, ready, basis), [VMEM] * 3), got

    image, near_two, parts = exchange(second_field, payload, sums, parts[0])
    early = call(gram_one_kernel, sds((R, 4 * R), f32), (right_side, image), [VMEM] * 2)
    gram = call(gram_two_kernel, sds((R, 4 * R), f32), (right_side, image, near_two), [VMEM] * 3)
    far, gram = call(
        functools.partial(tail_kernel, place), (rank_split, sds((2 * R, 4 * R), f32)),
        parts + (right_proj, image_proj, early, gram), [VMEM] * 11,
    )
    got = None
    for t, b in enumerate(order):
        if t > 0:
            gram = gram + got
        if t == 2:
            gram, second = barrier((gram, second))
        got = across(gram, b)
        if t == 0:
            far, got = barrier((far, got))
            second = call(second_kernel, panels, (near_two, far, basis), [VMEM] * 3)
    wide = sds(right_side.shape, f32)
    solution_field, residual, hessenberg = call(
        last_kernel, (wide, wide, sds((R, 2 * R), f32)), (gram, got, right_side, image, second), [VMEM] * 5
    )
    return solution_field, residual, hessenberg.T


def solution(mesh):
    in_specs = (
        P(None, ("parts", "leaf")),
        P(None, ("parts", "leaf")),
        P(("parts", "leaf")),
        P(("parts", "leaf"), None, None),
        P(None, ("parts", "leaf")),
        P(("parts", "leaf"), None),
        P(("parts", "leaf"), None, None),
        P("parts"),
    )
    out_specs = (P(None, ("parts", "leaf")), P(None, ("parts", "leaf")), P("parts", None))
    return jax.shard_map(body, mesh=mesh, in_specs=in_specs, out_specs=out_specs, check_vma=False)
```

```python
import functools

import jax
import jax.numpy as jnp
from jax import lax
from jax.experimental import pallas as pl
from jax.experimental.pallas import tpu as pltpu
from jax.sharding import PartitionSpec as P

PANEL = 256
R = 32
K = 32
GROUP = 32
highest = lax.Precision.HIGHEST
VMEM = pltpu.VMEM
SMEM = pltpu.SMEM
TN = (((0,), (0,)), ((), ()))
NT = (((1,), (1,)), ((), ()))
f32 = jnp.float32
bf16 = jnp.bfloat16


def spec(space):
    return pl.BlockSpec(memory_space=space)


def call(kernel, outs, ins, spaces, scratch=(), limit=24, flops=10**8, moved=10**6, placed=None):
    return pl.pallas_call(
        kernel,
        out_shape=outs,
        in_specs=[spec(s) for s in spaces],
        out_specs=jax.tree.map(lambda _: spec(VMEM), outs) if placed is None else tuple(map(spec, placed)),
        scratch_shapes=list(scratch),
        compiler_params=pltpu.CompilerParams(vmem_limit_bytes=limit << 20),
        cost_estimate=pl.CostEstimate(flops=flops, bytes_accessed=moved, transcendentals=0),
    )(*ins)


def dot(x, y):
    return jnp.dot(x, y, preferred_element_type=f32)


def dot_nt(x, y):
    return lax.dot_general(x, y, NT, preferred_element_type=f32)


def exact_nt(x, y):
    return lax.dot_general(x, y, NT, precision=highest, preferred_element_type=f32)


def split_rows(x):
    high = x.astype(bf16)
    low = (x - high.astype(f32)).astype(bf16)
    return jnp.concatenate([high, low], axis=0)


def join_rows(x):
    return x[:R] + x[R:]


def lane_group(shape):
    return lax.broadcasted_iota(jnp.int32, shape, 1) // K


def project(fields, basis):
    clusters = fields.shape[0] // (2 * R)
    all_pairs = dot_nt(fields, basis)
    group = lane_group((2 * R, clusters * K))
    total = jnp.zeros((2 * R, clusters * K), f32)
    for c in range(clusters):
        total = total + jnp.where(group == c, all_pairs[c * 2 * R : (c + 1) * 2 * R], 0.0)
    return join_rows(total)


def expand(sums, basis):
    group = lane_group(sums.shape)
    zero = jnp.zeros_like(sums)
    spread = [jnp.where(group == c, sums, zero) for c in range(sums.shape[1] // K)]
    return dot(jnp.concatenate(spread, axis=0), basis)


def rounds(devices):
    bits = devices.bit_length() - 1
    return [1] + [(1 << b) | 1 for b in range(bits - 1, 0, -1)]


def places(devices):
    steps = rounds(devices)
    place = [0] * devices
    for p in range(devices):
        apart = 0
        for t, step in enumerate(steps):
            if (p >> (len(steps) - 1 - t)) & 1:
                apart ^= step
        place[apart] = p
    return place


def couple(me, pairs_ref, slots_ref, table_ref, wide_ref, out_ref):
    clusters = out_ref.shape[2] // K
    devices = out_ref.shape[0] // 2
    pairs = pairs_ref.shape[1]
    group = lane_group((K, clusters * K))
    shift = clusters.bit_length() - 1
    assert clusters == 1 << shift
    steps = rounds(devices)
    for home in range(devices):
        apart = home ^ me
        parity = apart
        for b in range(1, len(steps)):
            parity = parity ^ (apart >> b)
        place = (parity & 1) << (len(steps) - 1)
        for t, step in enumerate(steps[1:], 1):
            bit = step.bit_length() - 1
            place = place + (((apart >> bit) & 1) << (len(steps) - 1 - t))
        table_ref[home] = place

    def one(f):
        first = slots_ref[pairs_ref[0, f]]
        second = slots_ref[pairs_ref[1, f]]
        first_home, second_home = first >> shift, second >> shift
        own = first_home == me
        where = jnp.where(own, devices, 0) + table_ref[jnp.where(own, second_home, first_home)]
        block = wide_ref[pl.ds(f, K, stride=pairs), :]
        block = jnp.concatenate([block] * (clusters * K // block.shape[1]), axis=1)
        block = jnp.where(group == (second & (clusters - 1)), block, 0.0).astype(bf16)
        here = pl.ds(pl.multiple_of((first & (clusters - 1)) * K, K), K)
        out_ref[where, here, :] = out_ref[where, here, :] + block

    def some(step, carry):
        for u in range(8):
            one(step * 8 + u)
        return carry

    lax.fori_loop(0, pairs // 8, some, 0)


def open_kernel(me_ref, pairs_hbm, slots_hbm, coupling_hbm, right_hbm, basis_hbm, near_hbm, blocks_hbm,
                near_pairs_ref, blocks_ref, field_ref, near_proj_ref, coupled_ref, payload_ref,
                pairs_ref, slots_ref, table_ref, coupling_ref, right_ref, basis_ref, wide_ref, sems):
    clusters = field_ref.shape[0]
    moves = [(coupling_hbm, coupling_ref), (basis_hbm, basis_ref), (right_hbm, right_ref),
             (pairs_hbm, pairs_ref), (slots_hbm, slots_ref), (near_hbm, near_pairs_ref), (blocks_hbm, blocks_ref)]
    copies = [pltpu.make_async_copy(*move, sems.at[i]) for i, move in enumerate(moves)]
    for copy in copies:
        copy.start()
    coupled_ref[...] = jnp.zeros_like(coupled_ref)
    copies[0].wait()
    pairs = coupling_ref.shape[0]
    lanes_held = 128
    rows = lax.broadcasted_iota(jnp.int32, (lanes_held, lanes_held), 0)
    lanes = lax.broadcasted_iota(jnp.int32, (lanes_held, lanes_held), 1)
    tiles = coupling_ref.shape[1] // lanes_held
    flat = jnp.concatenate(
        [coupling_ref[:, t * lanes_held : (t + 1) * lanes_held] for t in range(tiles)], axis=0
    )
    each = lanes_held // K
    for u in range(each):
        spread = jnp.where((lanes % K == rows % K) & (rows // K == u), 1.0, 0.0).astype(bf16)
        value = dot(flat, spread)
        for t in range(tiles):
            wide_ref[(t * each + u) * pairs : (t * each + u + 1) * pairs] = value[t * pairs : (t + 1) * pairs]
    copies[1].wait()
    basis = basis_ref[...]
    copies[2].wait()
    for c in range(clusters):
        field_ref[c] = split_rows(right_ref[:, c * PANEL : (c + 1) * PANEL])
    proj = project(field_ref[...].reshape(clusters * 2 * R, PANEL), basis)
    near_proj_ref[...] = proj
    copies[3].wait()
    copies[4].wait()
    copies[5].wait()
    couple(me_ref[0], pairs_ref, slots_ref, table_ref, wide_ref, coupled_ref)
    proj = proj.astype(bf16)
    devices = coupled_ref.shape[0] // 2
    send(
        lambda d: dot(proj, coupled_ref[devices + d]) + dot_nt(proj, coupled_ref[d]),
        payload_ref, proj, devices, True,
    )
    copies[6].wait()


def send(products, payload_ref, proj, devices, both):
    payload_ref[0] = proj
    half = devices // 2
    for d in range(half, devices):
        value = products(d)
        high = value.astype(bf16)
        payload_ref[1 + d - half] = high
        if both:
            payload_ref[1 + d] = (value - high.astype(f32)).astype(bf16)


def keep_one_kernel(coupled_ref, payload_ref, basis_ref, right_ref, kept_ref, cross_ref, corner_ref):
    devices = coupled_ref.shape[0] // 2
    proj = payload_ref[0]
    for d in range(devices // 2):
        kept_ref[d] = dot(proj, coupled_ref[devices + d]) + dot_nt(proj, coupled_ref[d])
    basis = basis_ref[...]
    cross = dot_nt(basis, basis)
    same = lane_group(cross.shape) == lax.broadcasted_iota(jnp.int32, cross.shape, 0) // K
    cross = jnp.where(same, cross, 0.0)
    high = cross.astype(bf16)
    cross_ref[0] = high
    cross_ref[1] = (cross - high.astype(f32)).astype(bf16)
    corner = jnp.zeros((R, 4 * R), f32)
    zero = jnp.zeros((R, PANEL), f32)
    for c in range(right_ref.shape[1] // PANEL):
        right = right_ref[:, c * PANEL : (c + 1) * PANEL]
        corner = corner + exact_nt(right, jnp.concatenate([zero, zero, right, zero], axis=0))
    corner_ref[...] = corner


def keep_two_kernel(turned_ref, payload_ref, kept_ref):
    proj = payload_ref[0]
    for d in range(kept_ref.shape[0]):
        kept_ref[d] = dot(proj, turned_ref[d])


def near_loop(count_ref, one):
    def group(g, carry):
        for u in range(GROUP):
            one(g * GROUP + u)
        return carry

    lax.fori_loop(0, (count_ref[0] + GROUP - 1) // GROUP, group, 0)


def near_cols_kernel(pairs_ref, count_ref, blocks_ref, field_ref, own_ref, next_ref, total):
    clusters = field_ref.shape[0]
    total[...] = jnp.zeros_like(total)

    def one(s):
        i = pairs_ref[0, s]
        j = jnp.where(s < count_ref[0], pairs_ref[1, s], 2 * clusters)
        total[j] = total[j] + join_rows(dot(field_ref[i], blocks_ref[s]))

    near_loop(count_ref, one)
    own_ref[...] = total[:clusters]
    next_ref[...] = total[clusters : 2 * clusters].astype(bf16)


def near_rows_kernel(pairs_ref, count_ref, blocks_ref, field_ref, after_ref, begun_ref, back_ref, basis_ref,
                     out_ref, proj_ref, window, total):
    clusters = field_ref.shape[0]
    window[:clusters] = field_ref[...]
    window[clusters:] = after_ref[...]
    total[:clusters] = begun_ref[...] + back_ref[...].astype(f32)
    total[clusters] = jnp.zeros_like(total[clusters])

    def one(s):
        i = jnp.where(s < count_ref[0], pairs_ref[0, s], clusters)
        j = pairs_ref[1, s]
        total[i] = total[i] + join_rows(dot_nt(window[j], blocks_ref[s]))

    near_loop(count_ref, one)
    near = total[:clusters]
    out_ref[...] = near
    split = jnp.concatenate([split_rows(near[c]) for c in range(clusters)], axis=0)
    proj_ref[...] = project(split, basis_ref[...])


def rows_two_kernel(pairs_ref, count_ref, blocks_ref, field_ref, after_ref, begun_ref, back_ref, basis_ref,
                    right_ref, image_ref, out_ref, proj_ref, gram_ref, window, total):
    near_rows_kernel(pairs_ref, count_ref, blocks_ref, field_ref, after_ref, begun_ref, back_ref, basis_ref,
                     out_ref, proj_ref, window, total)
    gram_two(right_ref, image_ref, out_ref, gram_ref)


def merge_kernel(coupled_ref, out_ref, turned_ref):
    devices = out_ref.shape[0]
    for d in range(devices):
        near, away = coupled_ref[d], coupled_ref[devices + d]
        out_ref[d] = near + away.T
        turned_ref[d] = away + near.T


def far_sums(place, merged_ref, low_ref, high_ref, kept_ref, got_ref):
    devices = merged_ref.shape[0]
    sums = kept_ref[0]
    for piece in range(got_ref.shape[0]):
        sums = sums + got_ref[piece].astype(f32)
    steps = rounds(devices)
    for g in range(devices):
        proj = low_ref[g] if g < devices // 2 else high_ref[g - devices // 2]
        apart = functools.reduce(lambda x, y: x ^ y, [step for t, step in enumerate(steps) if (g >> t) & 1], 0)
        sums = sums + dot(proj, merged_ref[place[apart]])
    return split_rows(sums)


def across_clusters(sums, cross_ref):
    return join_rows(dot(sums, cross_ref[0])) + dot(sums[:R], cross_ref[1])


def turn_kernel(place, merged_ref, low_ref, high_ref, kept_ref, got_ref, near_proj_ref, cross_ref,
                turned_ref, sums_ref, proj_ref, payload_ref):
    sums = far_sums(place, merged_ref, low_ref, high_ref, kept_ref, got_ref)
    sums_ref[...] = sums
    proj = near_proj_ref[...] + across_clusters(sums, cross_ref)
    proj_ref[...] = proj
    proj = proj.astype(bf16)
    send(lambda d: dot(proj, turned_ref[d]), payload_ref, proj, turned_ref.shape[0], False)


def image_kernel(near_ref, sums_ref, basis_ref, image_ref, field_ref):
    far = expand(sums_ref[...], basis_ref[...])
    for c in range(near_ref.shape[0]):
        image = near_ref[c] + join_rows(far[c * 2 * R : (c + 1) * 2 * R])
        image_ref[c] = image
        field_ref[c] = split_rows(image)


def second_kernel(near_ref, sums_ref, basis_ref, image_ref):
    far = expand(sums_ref[...], basis_ref[...])
    for c in range(near_ref.shape[0]):
        image_ref[c] = near_ref[c] + join_rows(far[c * 2 * R : (c + 1) * 2 * R])


def gram_one_kernel(corner_ref, right_ref, image_ref, gram_ref):
    gram = corner_ref[...]
    zero = jnp.zeros((R, PANEL), f32)
    for c in range(image_ref.shape[0]):
        right, image = right_ref[:, c * PANEL : (c + 1) * PANEL], image_ref[c]
        gram = gram + exact_nt(image, jnp.concatenate([right, image, zero, zero], axis=0))
    gram_ref[...] = gram


def gram_two(right_ref, image_ref, near_ref, gram_ref):
    gram = jnp.zeros((R, 4 * R), f32)
    zero = jnp.zeros((R, PANEL), f32)
    for c in range(image_ref.shape[0]):
        right, near = right_ref[:, c * PANEL : (c + 1) * PANEL], near_ref[c]
        gram = gram + exact_nt(near, jnp.concatenate([right, image_ref[c], near, zero], axis=0))
    gram_ref[...] = gram


def tail_kernel(place, merged_ref, low_ref, high_ref, kept_ref, got_ref, near_proj_ref, cross_ref,
                right_proj_ref, image_proj_ref, early_ref, gram_ref, sums_ref, out_ref):
    sums = far_sums(place, merged_ref, low_ref, high_ref, kept_ref, got_ref)
    sums_ref[...] = sums
    half = near_proj_ref[...] + 0.5 * across_clusters(sums, cross_ref)
    sums = join_rows(sums.astype(f32))
    known = jnp.concatenate([right_proj_ref[...], image_proj_ref[...], half, jnp.zeros_like(half)], axis=0)
    added = exact_nt(sums, known)
    mirror = exact_nt(half, jnp.concatenate([jnp.zeros_like(sums)] * 2 + [sums, jnp.zeros_like(sums)], axis=0))
    late = gram_ref[...] + added + mirror
    lanes = lane_group(late.shape)
    out_ref[:R] = jnp.where(lanes == 3, pltpu.roll(late, 3 * R, 1), early_ref[...])
    rest = pltpu.roll(late, 3 * R, 1)
    half_rows = R // 2
    out_ref[R:] = jnp.where(lanes[:half_rows] < 2, rest[:half_rows], pltpu.roll(rest[half_rows:], 2 * R, 1))


TALL = 8


def lane(x, k):
    return jnp.broadcast_to(x[:, k : k + 1], x.shape)


def eliminate(wide, late, k):
    block, at = k // TALL, k % TALL
    rows = lax.broadcasted_iota(jnp.int32, wide[block].shape, 0)
    both = [wide] if late is None or block < len(wide) // 2 else [wide, late]
    columns = [[lane(x, k + j) for x in wide[block:]] for j in range(4)]
    m = [[columns[j][0][at + i : at + i + 1] for j in range(4)] for i in range(4)]
    scale = 1.0 / (m[0][0] * m[1][1] - m[0][1] * m[1][0])
    first = {j: (m[1][1] * m[0][j] - m[0][1] * m[1][j]) * scale for j in (2, 3)}
    second = {j: (m[0][0] * m[1][j] - m[1][0] * m[0][j]) * scale for j in (2, 3)}
    s = {(i, j): m[i][j] - (m[i][0] * first[j] + m[i][1] * second[j]) for i in (2, 3) for j in (2, 3)}
    after = 1.0 / (s[2, 2] * s[3, 3] - s[2, 3] * s[3, 2])
    ratio, last_ratio = m[1][0] / m[0][0], s[3, 2] / s[2, 2]
    for part in both:
        p = [part[block][at + i : at + i + 1] for i in range(4)]
        y0 = (m[1][1] * p[0] - m[0][1] * p[1]) * scale
        y1 = (m[0][0] * p[1] - m[1][0] * p[0]) * scale
        r2 = p[2] - (m[2][0] * y0 + m[2][1] * y1)
        r3 = p[3] - (m[3][0] * y0 + m[3][1] * y1)
        x2 = (s[3, 3] * r2 - s[2, 3] * r3) * after
        x3 = (s[2, 2] * r3 - s[3, 2] * r2) * after
        x0 = y0 - (first[2] * x2 + first[3] * x3)
        x1 = y1 - (second[2] * x2 + second[3] * x3)
        own = [p[0], p[1] - ratio * p[0], r2, r3 - last_ratio * r2]
        for i in range(block, len(wide)):
            c = [column[i - block] for column in columns]
            rest = part[i] - ((c[0] * x0 + c[1] * x1) + (c[2] * x2 + c[3] * x3))
            if i == block:
                rest = jnp.where(rows > at + 3, rest, part[i])
                for t in range(1, 4):
                    rest = jnp.where(rows == at + t, own[t], rest)
            part[i] = rest


def last_kernel(kept_ref, got_ref, right_ref, image_ref, second_ref, field_ref, residual_ref, hessenberg_ref):
    clusters = image_ref.shape[0]
    gram = kept_ref[...] + got_ref[...]
    top, folded = gram[:R], gram[R:]
    bottom = jnp.concatenate([folded[:, : 2 * R], folded[:, 2 * R :]], axis=0)
    lanes = lax.broadcasted_iota(jnp.int32, (2 * R, 4 * R), 1)
    rows = lax.broadcasted_iota(jnp.int32, (2 * R, 4 * R), 0)
    wide = jnp.zeros((R, R), f32)
    first_first, image_first = top[:, 2 * R : 3 * R], top[:, :R]
    image_image, second_first = top[:, R : 2 * R], top[:, 3 * R :]
    second_image, second_second = bottom[:, :R], bottom[:, R:]
    system = jnp.concatenate(
        [
            jnp.concatenate([image_image, second_image.T, image_first, wide], axis=1),
            jnp.concatenate([second_image, second_second, second_first, wide], axis=1),
        ],
        axis=0,
    )
    lower = jnp.concatenate(
        [
            jnp.concatenate([first_first, image_first.T, wide, wide], axis=1),
            jnp.concatenate([image_first, image_image, wide, wide], axis=1),
        ],
        axis=0,
    )
    lower = jnp.where(lanes - 2 * R == rows, 1.0, lower)
    system = jnp.where(lanes - 3 * R == rows, 1.0, system)
    late = jnp.where(lanes + R == rows, 1.0, 0.0)

    def blocks(x):
        return [x[i : i + TALL] for i in range(0, 2 * R, TALL)]

    system, lower, late = blocks(system), blocks(lower), blocks(late)
    for k in range(0, 2 * R, 4):
        eliminate(system, late, k)
        eliminate(lower, None, k)
    system, lower, late = (jnp.concatenate(x, axis=0) for x in (system, lower, late))

    def diagonal(x):
        return jnp.sum(jnp.where(lanes == rows, x, 0.0), axis=1, keepdims=True)

    lower = lower * lax.rsqrt(diagonal(lower))
    scaled = system[:, 2 * R : 3 * R] / diagonal(system)
    inverse = jnp.concatenate([system[:, 3 * R :], late[:, :R]], axis=1)
    weights = lax.dot_general(scaled, inverse, TN, precision=highest, preferred_element_type=f32)
    inverse_zero = lower[:R, 2 * R : 3 * R]
    hessenberg_ref[:, :R] = exact_nt(inverse_zero, lower[:R, R : 2 * R])
    hessenberg_ref[:, R:] = lax.dot_general(
        lower[R:, R : 2 * R], inverse_zero, NT, precision=highest, preferred_element_type=f32
    )
    none = jnp.zeros((R, R), f32)
    mix = jnp.concatenate(
        [jnp.concatenate([weights, none], axis=1), jnp.concatenate([none, weights], axis=1)], axis=0
    )
    mix_high = mix.astype(bf16)
    mix_both = jnp.concatenate([mix_high, (mix - mix_high.astype(f32)).astype(bf16)], axis=0)
    for c in range(clusters):
        here = slice(c * PANEL, (c + 1) * PANEL)
        right = right_ref[:, here]
        stacked = jnp.concatenate([right, image_ref[c], second_ref[c]], axis=0)
        high = stacked.astype(bf16)
        low = (stacked - high.astype(f32)).astype(bf16)
        both = dot(mix_both, high)
        value = both[: 2 * R] + both[2 * R :] + dot(mix_high, low)
        field_ref[:, here] = value[:R]
        residual_ref[:, here] = right - value[R:]


def body(right_side, near_pairs, near_count, near_blocks, far_pairs, coupling, cluster_basis, cluster_slot):
    devices = lax.axis_size("leaf")
    order, place = rounds(devices), places(devices)
    clusters = cluster_basis.shape[0]
    me = lax.axis_index("leaf").astype(jnp.int32).reshape(1)
    basis = cluster_basis.reshape(clusters * K, PANEL)
    sds = jax.ShapeDtypeStruct

    def across(x, b):
        return lax.ppermute(x, "leaf", [(i, i ^ b) for i in range(devices)])

    def shift(x, by):
        return lax.ppermute(x, "leaf", [(i, i + by) for i in range(devices) if 0 <= i + by < devices])

    panels = sds((clusters, R, PANEL), f32)
    narrow = sds((clusters, R, PANEL), bf16)
    split = sds((clusters, 2 * R, PANEL), bf16)
    rank_wide = sds((R, clusters * K), f32)
    rank_split = sds((2 * R, clusters * K), bf16)
    half = devices // 2
    merged_out = sds((devices, clusters * K, clusters * K), bf16)
    payload_out = sds((1 + half, R, clusters * K), bf16)
    kept_out = sds((half, R, clusters * K), f32)
    barrier = lax.optimization_barrier
    near_spaces = [SMEM, SMEM, VMEM, VMEM]

    def in_hbm(x):
        return pltpu.with_memory_space_constraint(x, pltpu.HBM)

    near_pairs, near_blocks, field, right_proj, coupled, payload = call(
        open_kernel,
        (sds(near_pairs.shape, jnp.int32), sds(near_blocks.shape, bf16), split, rank_wide,
         sds((2 * devices, clusters * K, clusters * K), bf16),
         sds((1 + devices, R, clusters * K), bf16)),
        (me, in_hbm(far_pairs), in_hbm(cluster_slot), in_hbm(coupling), in_hbm(right_side), in_hbm(basis),
         in_hbm(near_pairs), in_hbm(near_blocks)),
        [SMEM] + [pltpu.HBM] * 7,
        [
            pltpu.SMEM(far_pairs.shape, jnp.int32),
            pltpu.SMEM(cluster_slot.shape, jnp.int32),
            pltpu.SMEM((devices,), jnp.int32),
            pltpu.VMEM(coupling.shape, bf16),
            pltpu.VMEM(right_side.shape, f32),
            pltpu.VMEM(basis.shape, bf16),
            pltpu.VMEM((coupling.shape[0] * (K + 1), 128), f32),
            pltpu.SemaphoreType.DMA((7,)),
        ],
        placed=[SMEM] + [VMEM] * 5,
    )

    def exchange(make_field, beside, keep, payload, merged=None):
        first = merged is None
        for t, b in enumerate(order):
            if t > 0:
                held, half = gathered.shape[0], sums.shape[0] // 2
                payload = jnp.concatenate([gathered, sums[half:].astype(bf16)], axis=0)
                sums = sums[:half]
            else:
                gathered, held = payload[:1], 1
            if t == 2:
                payload, own = barrier((payload, own))
            if t == 3:
                payload, made = barrier((payload, made))
            got = across(payload, b)
            if t == 0:
                sums, cross, corner = keep(payload)
                image, field, got = make_field(got)
                after = shift(field, -1)
                own, following = call(
                    near_cols_kernel, (panels, narrow), (near_pairs, near_count, near_blocks, field), near_spaces,
                    [pltpu.VMEM((2 * clusters + 1, R, PANEL), f32)], moved=12 << 20,
                )
                back = shift(following, 1)
            if t == 1:
                made, got = beside(image, corner, got)
            if t == len(order) - 2:
                after, got = barrier((after, got))
            got_gathered, got_sums = got[:held], got[held:]
            if t < len(order) - 1:
                gathered = jnp.concatenate([gathered, got_gathered], axis=0)
                for piece in range(0, got_sums.shape[0], sums.shape[0]):
                    sums = sums + got_sums[piece : piece + sums.shape[0]].astype(f32)
        kernel, ins, outs = near_rows_kernel, (near_blocks, field, after, own, back, basis), (panels, rank_wide)
        if not first:
            kernel, ins, outs = rows_two_kernel, ins + (right_side, image), outs + (sds((R, 4 * R), f32),)
        near, near_proj, *gram = call(
            kernel, outs, (near_pairs, near_count) + ins, [SMEM] * 2 + [VMEM] * len(ins),
            [pltpu.VMEM((2 * clusters, 2 * R, PANEL), bf16), pltpu.VMEM((clusters + 1, R, PANEL), f32)],
            moved=12 << 20,
        )
        merged = made if first else merged
        return image, near, made, gram, cross, corner, (merged[0], gathered, got_gathered, sums, got_sums, near_proj, cross)

    def first_field(got):
        ready, got = barrier((field, got))
        return right_side, ready, got

    def keep_one(payload):
        return call(
            keep_one_kernel, (kept_out, sds((2, clusters * K, clusters * K), bf16), sds((R, 4 * R), f32)),
            (coupled, payload, basis, right_side), [VMEM] * 4,
        )

    def merging(image, corner, got):
        ready, got = barrier((coupled, got))
        return call(merge_kernel, (merged_out, merged_out), (ready,), [VMEM]), got

    def multiplying(image, corner, got):
        ready, got = barrier((image, got))
        return call(gram_one_kernel, sds((R, 4 * R), f32), (corner, right_side, ready), [VMEM] * 3), got

    unused, near, merged, unused, cross, corner, parts = exchange(first_field, merging, keep_one, payload)
    far, image_proj, payload = call(
        functools.partial(turn_kernel, place), (rank_split, rank_wide, payload_out), parts + (merged[1],), [VMEM] * 8
    )

    def second_field(got):
        ready, got = barrier((far, got))
        return *call(image_kernel, (panels, split), (near, ready, basis), [VMEM] * 3), got

    def keep_two(payload):
        return call(keep_two_kernel, kept_out, (merged[1], payload), [VMEM] * 2), cross, corner

    image, near_two, early, gram, unused, unused, parts = exchange(
        second_field, multiplying, keep_two, payload, merged
    )
    far, gram = call(
        functools.partial(tail_kernel, place), (rank_split, sds((R + R // 2, 4 * R), f32)),
        parts + (right_proj, image_proj, early, *gram), [VMEM] * 11,
    )
    got = None
    for t, b in enumerate(order):
        if t > 0:
            gram = gram + got
        if t == 2:
            gram, second = barrier((gram, second))
        got = across(gram, b)
        if t == 0:
            far, got = barrier((far, got))
            second = call(second_kernel, panels, (near_two, far, basis), [VMEM] * 3)
    wide = sds(right_side.shape, f32)
    solution_field, residual, hessenberg = call(
        last_kernel, (wide, wide, sds((R, 2 * R), f32)), (gram, got, right_side, image, second), [VMEM] * 5
    )
    return solution_field, residual, hessenberg.T


def solution(mesh):
    in_specs = (
        P(None, ("parts", "leaf")),
        P(None, ("parts", "leaf")),
        P(("parts", "leaf")),
        P(("parts", "leaf"), None, None),
        P(None, ("parts", "leaf")),
        P(("parts", "leaf"), None),
        P(("parts", "leaf"), None, None),
        P("parts"),
    )
    out_specs = (P(None, ("parts", "leaf")), P(None, ("parts", "leaf")), P("parts", None))
    return jax.shard_map(body, mesh=mesh, in_specs=in_specs, out_specs=out_specs, check_vma=False)
```

```python
import functools

import jax
import jax.numpy as jnp
from jax import lax
from jax.experimental import pallas as pl
from jax.experimental.pallas import tpu as pltpu
from jax.sharding import PartitionSpec as P

PANEL = 256
R = 32
K = 32
GROUP = 32
highest = lax.Precision.HIGHEST
VMEM = pltpu.VMEM
SMEM = pltpu.SMEM
TN = (((0,), (0,)), ((), ()))
NT = (((1,), (1,)), ((), ()))
f32 = jnp.float32
bf16 = jnp.bfloat16


def spec(space):
    return pl.BlockSpec(memory_space=space)


def call(kernel, outs, ins, spaces, scratch=(), limit=24, flops=10**8, moved=10**6, placed=None):
    return pl.pallas_call(
        kernel,
        out_shape=outs,
        in_specs=[spec(s) for s in spaces],
        out_specs=jax.tree.map(lambda _: spec(VMEM), outs) if placed is None else tuple(map(spec, placed)),
        scratch_shapes=list(scratch),
        compiler_params=pltpu.CompilerParams(vmem_limit_bytes=limit << 20),
        cost_estimate=pl.CostEstimate(flops=flops, bytes_accessed=moved, transcendentals=0),
    )(*ins)


def dot(x, y):
    return jnp.dot(x, y, preferred_element_type=f32)


def dot_nt(x, y):
    return lax.dot_general(x, y, NT, preferred_element_type=f32)


def exact_nt(x, y):
    return lax.dot_general(x, y, NT, precision=highest, preferred_element_type=f32)


def split_rows(x):
    high = x.astype(bf16)
    low = (x - high.astype(f32)).astype(bf16)
    return jnp.concatenate([high, low], axis=0)


def join_rows(x):
    return x[:R] + x[R:]


def lane_group(shape):
    return lax.broadcasted_iota(jnp.int32, shape, 1) // K


def project(fields, basis):
    clusters = fields.shape[0] // (2 * R)
    all_pairs = dot_nt(fields, basis)
    group = lane_group((2 * R, clusters * K))
    total = jnp.zeros((2 * R, clusters * K), f32)
    for c in range(clusters):
        total = total + jnp.where(group == c, all_pairs[c * 2 * R : (c + 1) * 2 * R], 0.0)
    return join_rows(total)


def expand(sums, basis):
    group = lane_group(sums.shape)
    zero = jnp.zeros_like(sums)
    spread = [jnp.where(group == c, sums, zero) for c in range(sums.shape[1] // K)]
    return dot(jnp.concatenate(spread, axis=0), basis)


def rounds(devices):
    bits = devices.bit_length() - 1
    return [1] + [(1 << b) | 1 for b in [bits - 1, 1] + list(range(bits - 2, 1, -1))]


def places(devices):
    steps = rounds(devices)
    place = [0] * devices
    for p in range(devices):
        apart = 0
        for t, step in enumerate(steps):
            if (p >> (len(steps) - 1 - t)) & 1:
                apart ^= step
        place[apart] = p
    return place


def couple(me, pairs_ref, slots_ref, table_ref, wide_ref, out_ref):
    clusters = out_ref.shape[2] // K
    devices = out_ref.shape[0] // 2
    pairs = pairs_ref.shape[1]
    group = lane_group((K, clusters * K))
    shift = clusters.bit_length() - 1
    assert clusters == 1 << shift
    steps = rounds(devices)
    for home in range(devices):
        apart = home ^ me
        parity = apart
        for b in range(1, len(steps)):
            parity = parity ^ (apart >> b)
        place = (parity & 1) << (len(steps) - 1)
        for t, step in enumerate(steps[1:], 1):
            bit = step.bit_length() - 1
            place = place + (((apart >> bit) & 1) << (len(steps) - 1 - t))
        table_ref[home] = place

    def one(f):
        first = slots_ref[pairs_ref[0, f]]
        second = slots_ref[pairs_ref[1, f]]
        first_home, second_home = first >> shift, second >> shift
        own = first_home == me
        where = jnp.where(own, devices, 0) + table_ref[jnp.where(own, second_home, first_home)]
        block = wide_ref[pl.ds(f, K, stride=pairs + 8), :]
        block = jnp.concatenate([block] * (clusters * K // block.shape[1]), axis=1)
        block = jnp.where(group == (second & (clusters - 1)), block, 0.0).astype(bf16)
        here = pl.ds(pl.multiple_of((first & (clusters - 1)) * K, K), K)
        out_ref[where, here, :] = out_ref[where, here, :] + block

    def some(step, carry):
        for u in range(16):
            one(step * 16 + u)
        return carry

    lax.fori_loop(0, pairs // 16, some, 0)


def open_kernel(me_ref, pairs_hbm, slots_hbm, coupling_hbm, right_hbm, basis_hbm, near_hbm, blocks_hbm,
                near_pairs_ref, blocks_ref, field_ref, near_proj_ref, coupled_ref, payload_ref,
                pairs_ref, slots_ref, table_ref, coupling_ref, right_ref, basis_ref, wide_ref, sems):
    clusters = field_ref.shape[0]
    moves = [(coupling_hbm, coupling_ref), (basis_hbm, basis_ref), (right_hbm, right_ref),
             (pairs_hbm, pairs_ref), (slots_hbm, slots_ref), (near_hbm, near_pairs_ref), (blocks_hbm, blocks_ref)]
    copies = [pltpu.make_async_copy(*move, sems.at[i]) for i, move in enumerate(moves)]
    for copy in copies:
        copy.start()
    coupled_ref[...] = jnp.zeros_like(coupled_ref)
    copies[0].wait()
    pairs = coupling_ref.shape[0]
    lanes_held = 128
    rows = lax.broadcasted_iota(jnp.int32, (lanes_held, lanes_held), 0)
    lanes = lax.broadcasted_iota(jnp.int32, (lanes_held, lanes_held), 1)
    tiles = coupling_ref.shape[1] // lanes_held
    flat = jnp.concatenate(
        [coupling_ref[:, t * lanes_held : (t + 1) * lanes_held] for t in range(tiles)], axis=0
    )
    each = lanes_held // K
    for u in range(each):
        spread = jnp.where((lanes % K == rows % K) & (rows // K == u), 1.0, 0.0).astype(bf16)
        value = dot(flat, spread)
        for t in range(tiles):
            begin = (t * each + u) * (pairs + 8)
            wide_ref[begin : begin + pairs] = value[t * pairs : (t + 1) * pairs]
    copies[1].wait()
    basis = basis_ref[...]
    copies[2].wait()
    for c in range(clusters):
        field_ref[c] = split_rows(right_ref[:, c * PANEL : (c + 1) * PANEL])
    proj = project(field_ref[...].reshape(clusters * 2 * R, PANEL), basis)
    near_proj_ref[...] = proj
    copies[3].wait()
    copies[4].wait()
    copies[5].wait()
    couple(me_ref[0], pairs_ref, slots_ref, table_ref, wide_ref, coupled_ref)
    proj = proj.astype(bf16)
    devices = coupled_ref.shape[0] // 2
    send(
        lambda d: dot(proj, coupled_ref[devices + d]) + dot_nt(proj, coupled_ref[d]),
        payload_ref, proj, devices, True,
    )
    copies[6].wait()


def send(products, payload_ref, proj, devices, both):
    payload_ref[0] = proj
    half = devices // 2
    for d in range(half, devices):
        value = products(d)
        high = value.astype(bf16)
        payload_ref[1 + d - half] = high
        if both:
            payload_ref[1 + d] = (value - high.astype(f32)).astype(bf16)


def keep_one_kernel(coupled_ref, payload_ref, basis_ref, right_ref, kept_ref, cross_ref, corner_ref):
    devices = coupled_ref.shape[0] // 2
    proj = payload_ref[0]
    for d in range(devices // 2):
        kept_ref[d] = dot(proj, coupled_ref[devices + d]) + dot_nt(proj, coupled_ref[d])
    basis = basis_ref[...]
    cross = dot_nt(basis, basis)
    same = lane_group(cross.shape) == lax.broadcasted_iota(jnp.int32, cross.shape, 0) // K
    cross = jnp.where(same, cross, 0.0)
    high = cross.astype(bf16)
    cross_ref[0] = high
    cross_ref[1] = (cross - high.astype(f32)).astype(bf16)
    corner = jnp.zeros((R, 4 * R), f32)
    zero = jnp.zeros((R, PANEL), f32)
    for c in range(right_ref.shape[1] // PANEL):
        right = right_ref[:, c * PANEL : (c + 1) * PANEL]
        corner = corner + exact_nt(right, jnp.concatenate([zero, zero, right, zero], axis=0))
    corner_ref[...] = corner


def keep_two_kernel(turned_ref, payload_ref, kept_ref):
    proj = payload_ref[0]
    for d in range(kept_ref.shape[0]):
        kept_ref[d] = dot(proj, turned_ref[d])


def near_loop(count_ref, one):
    def group(g, carry):
        for u in range(GROUP):
            one(g * GROUP + u)
        return carry

    lax.fori_loop(0, (count_ref[0] + GROUP - 1) // GROUP, group, 0)


def near_cols_kernel(pairs_ref, count_ref, blocks_ref, field_ref, own_ref, next_ref, total):
    clusters = field_ref.shape[0]
    total[...] = jnp.zeros_like(total)

    def one(s):
        i = pairs_ref[0, s]
        j = jnp.where(s < count_ref[0], pairs_ref[1, s], 2 * clusters)
        total[j] = total[j] + join_rows(dot(field_ref[i], blocks_ref[s]))

    near_loop(count_ref, one)
    own_ref[...] = total[:clusters]
    next_ref[...] = total[clusters : 2 * clusters].astype(bf16)


def near_rows_kernel(pairs_ref, count_ref, blocks_ref, field_ref, after_ref, begun_ref, back_ref, basis_ref,
                     out_ref, proj_ref, window, total):
    clusters = field_ref.shape[0]
    window[:clusters] = field_ref[...]
    window[clusters:] = after_ref[...]
    total[:clusters] = begun_ref[...] + back_ref[...].astype(f32)
    total[clusters] = jnp.zeros_like(total[clusters])

    def one(s):
        i = jnp.where(s < count_ref[0], pairs_ref[0, s], clusters)
        j = pairs_ref[1, s]
        total[i] = total[i] + join_rows(dot_nt(window[j], blocks_ref[s]))

    near_loop(count_ref, one)
    near = total[:clusters]
    out_ref[...] = near
    split = jnp.concatenate([split_rows(near[c]) for c in range(clusters)], axis=0)
    proj_ref[...] = project(split, basis_ref[...])


def rows_two_kernel(pairs_ref, count_ref, blocks_ref, field_ref, after_ref, begun_ref, back_ref, basis_ref,
                    right_ref, image_ref, out_ref, proj_ref, gram_ref, window, total):
    near_rows_kernel(pairs_ref, count_ref, blocks_ref, field_ref, after_ref, begun_ref, back_ref, basis_ref,
                     out_ref, proj_ref, window, total)
    gram_two(right_ref, image_ref, out_ref, gram_ref)


def merge_kernel(coupled_ref, out_ref, turned_ref):
    devices = out_ref.shape[0]
    for d in range(devices):
        near, away = coupled_ref[d], coupled_ref[devices + d]
        out_ref[d] = near + away.T
        turned_ref[d] = away + near.T


def far_sums(place, merged_ref, low_ref, high_ref, kept_ref, got_ref):
    devices = merged_ref.shape[0]
    sums = kept_ref[0]
    for piece in range(got_ref.shape[0]):
        sums = sums + got_ref[piece].astype(f32)
    steps = rounds(devices)
    for g in range(devices):
        proj = low_ref[g] if g < devices // 2 else high_ref[g - devices // 2]
        apart = functools.reduce(lambda x, y: x ^ y, [step for t, step in enumerate(steps) if (g >> t) & 1], 0)
        sums = sums + dot(proj, merged_ref[place[apart]])
    return split_rows(sums)


def across_clusters(sums, cross_ref):
    return join_rows(dot(sums, cross_ref[0])) + dot(sums[:R], cross_ref[1])


def turn_kernel(place, merged_ref, low_ref, high_ref, kept_ref, got_ref, near_proj_ref, cross_ref,
                turned_ref, sums_ref, proj_ref, payload_ref):
    sums = far_sums(place, merged_ref, low_ref, high_ref, kept_ref, got_ref)
    sums_ref[...] = sums
    proj = near_proj_ref[...] + across_clusters(sums, cross_ref)
    proj_ref[...] = proj
    proj = proj.astype(bf16)
    send(lambda d: dot(proj, turned_ref[d]), payload_ref, proj, turned_ref.shape[0], False)


def image_kernel(near_ref, sums_ref, basis_ref, image_ref, field_ref):
    far = expand(sums_ref[...], basis_ref[...])
    for c in range(near_ref.shape[0]):
        image = near_ref[c] + join_rows(far[c * 2 * R : (c + 1) * 2 * R])
        image_ref[c] = image
        field_ref[c] = split_rows(image)


def second_kernel(near_ref, sums_ref, basis_ref, image_ref):
    far = expand(sums_ref[...], basis_ref[...])
    for c in range(near_ref.shape[0]):
        image_ref[c] = near_ref[c] + join_rows(far[c * 2 * R : (c + 1) * 2 * R])


def gram_one_kernel(corner_ref, right_ref, image_ref, gram_ref):
    gram = corner_ref[...]
    zero = jnp.zeros((R, PANEL), f32)
    for c in range(image_ref.shape[0]):
        right, image = right_ref[:, c * PANEL : (c + 1) * PANEL], image_ref[c]
        gram = gram + exact_nt(image, jnp.concatenate([right, image, zero, zero], axis=0))
    gram_ref[...] = gram


def gram_two(right_ref, image_ref, near_ref, gram_ref):
    gram = jnp.zeros((R, 4 * R), f32)
    zero = jnp.zeros((R, PANEL), f32)
    for c in range(image_ref.shape[0]):
        right, near = right_ref[:, c * PANEL : (c + 1) * PANEL], near_ref[c]
        gram = gram + exact_nt(near, jnp.concatenate([right, image_ref[c], near, zero], axis=0))
    gram_ref[...] = gram


def tail_kernel(place, merged_ref, low_ref, high_ref, kept_ref, got_ref, near_proj_ref, cross_ref,
                right_proj_ref, image_proj_ref, early_ref, gram_ref, sums_ref, out_ref):
    sums = far_sums(place, merged_ref, low_ref, high_ref, kept_ref, got_ref)
    sums_ref[...] = sums
    half = near_proj_ref[...] + 0.5 * across_clusters(sums, cross_ref)
    sums = join_rows(sums.astype(f32))
    known = jnp.concatenate([right_proj_ref[...], image_proj_ref[...], half, jnp.zeros_like(half)], axis=0)
    added = exact_nt(sums, known)
    mirror = exact_nt(half, jnp.concatenate([jnp.zeros_like(sums)] * 2 + [sums, jnp.zeros_like(sums)], axis=0))
    late = gram_ref[...] + added + mirror
    lanes = lane_group(late.shape)
    out_ref[:R] = jnp.where(lanes == 3, pltpu.roll(late, 3 * R, 1), early_ref[...])
    rest = pltpu.roll(late, 3 * R, 1)
    half_rows = R // 2
    out_ref[R:] = jnp.where(lanes[:half_rows] < 2, rest[:half_rows], pltpu.roll(rest[half_rows:], 2 * R, 1))


TALL = 8


def lane(x, k):
    return jnp.broadcast_to(x[:, k : k + 1], x.shape)


def eliminate(wide, late, k):
    block, at = k // TALL, k % TALL
    rows = lax.broadcasted_iota(jnp.int32, wide[block].shape, 0)
    both = [wide] if late is None or block < len(wide) // 2 else [wide, late]
    columns = [[lane(x, k + j) for x in wide[block:]] for j in range(4)]
    m = [[columns[j][0][at + i : at + i + 1] for j in range(4)] for i in range(4)]
    scale = 1.0 / (m[0][0] * m[1][1] - m[0][1] * m[1][0])
    first = {j: (m[1][1] * m[0][j] - m[0][1] * m[1][j]) * scale for j in (2, 3)}
    second = {j: (m[0][0] * m[1][j] - m[1][0] * m[0][j]) * scale for j in (2, 3)}
    s = {(i, j): m[i][j] - (m[i][0] * first[j] + m[i][1] * second[j]) for i in (2, 3) for j in (2, 3)}
    after = 1.0 / (s[2, 2] * s[3, 3] - s[2, 3] * s[3, 2])
    ratio, last_ratio = m[1][0] / m[0][0], s[3, 2] / s[2, 2]
    for part in both:
        p = [part[block][at + i : at + i + 1] for i in range(4)]
        y0 = (m[1][1] * p[0] - m[0][1] * p[1]) * scale
        y1 = (m[0][0] * p[1] - m[1][0] * p[0]) * scale
        r2 = p[2] - (m[2][0] * y0 + m[2][1] * y1)
        r3 = p[3] - (m[3][0] * y0 + m[3][1] * y1)
        x2 = (s[3, 3] * r2 - s[2, 3] * r3) * after
        x3 = (s[2, 2] * r3 - s[3, 2] * r2) * after
        x0 = y0 - (first[2] * x2 + first[3] * x3)
        x1 = y1 - (second[2] * x2 + second[3] * x3)
        own = [p[0], p[1] - ratio * p[0], r2, r3 - last_ratio * r2]
        for i in range(block, len(wide)):
            c = [column[i - block] for column in columns]
            rest = part[i] - ((c[0] * x0 + c[1] * x1) + (c[2] * x2 + c[3] * x3))
            if i == block:
                rest = jnp.where(rows > at + 3, rest, part[i])
                for t in range(1, 4):
                    rest = jnp.where(rows == at + t, own[t], rest)
            part[i] = rest


def last_kernel(kept_ref, got_ref, right_ref, image_ref, second_ref, field_ref, residual_ref, hessenberg_ref):
    clusters = image_ref.shape[0]
    gram = kept_ref[...] + got_ref[...]
    top, folded = gram[:R], gram[R:]
    bottom = jnp.concatenate([folded[:, : 2 * R], folded[:, 2 * R :]], axis=0)
    lanes = lax.broadcasted_iota(jnp.int32, (2 * R, 4 * R), 1)
    rows = lax.broadcasted_iota(jnp.int32, (2 * R, 4 * R), 0)
    wide = jnp.zeros((R, R), f32)
    first_first, image_first = top[:, 2 * R : 3 * R], top[:, :R]
    image_image, second_first = top[:, R : 2 * R], top[:, 3 * R :]
    second_image, second_second = bottom[:, :R], bottom[:, R:]
    system = jnp.concatenate(
        [
            jnp.concatenate([image_image, second_image.T, image_first, wide], axis=1),
            jnp.concatenate([second_image, second_second, second_first, wide], axis=1),
        ],
        axis=0,
    )
    lower = jnp.concatenate(
        [
            jnp.concatenate([first_first, image_first.T, wide, wide], axis=1),
            jnp.concatenate([image_first, image_image, wide, wide], axis=1),
        ],
        axis=0,
    )
    lower = jnp.where(lanes - 2 * R == rows, 1.0, lower)
    system = jnp.where(lanes - 3 * R == rows, 1.0, system)
    late = jnp.where(lanes + R == rows, 1.0, 0.0)

    def blocks(x):
        return [x[i : i + TALL] for i in range(0, 2 * R, TALL)]

    system, lower, late = blocks(system), blocks(lower), blocks(late)
    for k in range(0, 2 * R, 4):
        eliminate(system, late, k)
        eliminate(lower, None, k)
    system, lower, late = (jnp.concatenate(x, axis=0) for x in (system, lower, late))

    def diagonal(x):
        return jnp.sum(jnp.where(lanes == rows, x, 0.0), axis=1, keepdims=True)

    lower = lower * lax.rsqrt(diagonal(lower))
    scaled = system[:, 2 * R : 3 * R] / diagonal(system)
    inverse = jnp.concatenate([system[:, 3 * R :], late[:, :R]], axis=1)
    weights = lax.dot_general(scaled, inverse, TN, precision=highest, preferred_element_type=f32)
    inverse_zero = lower[:R, 2 * R : 3 * R]
    hessenberg_ref[:, :R] = exact_nt(inverse_zero, lower[:R, R : 2 * R])
    hessenberg_ref[:, R:] = lax.dot_general(
        lower[R:, R : 2 * R], inverse_zero, NT, precision=highest, preferred_element_type=f32
    )
    none = jnp.zeros((R, R), f32)
    mix = jnp.concatenate(
        [jnp.concatenate([weights, none], axis=1), jnp.concatenate([none, weights], axis=1)], axis=0
    )
    mix_high = mix.astype(bf16)
    mix_both = jnp.concatenate([mix_high, (mix - mix_high.astype(f32)).astype(bf16)], axis=0)
    for c in range(clusters):
        here = slice(c * PANEL, (c + 1) * PANEL)
        right = right_ref[:, here]
        stacked = jnp.concatenate([right, image_ref[c], second_ref[c]], axis=0)
        high = stacked.astype(bf16)
        low = (stacked - high.astype(f32)).astype(bf16)
        both = dot(mix_both, high)
        value = both[: 2 * R] + both[2 * R :] + dot(mix_high, low)
        field_ref[:, here] = value[:R]
        residual_ref[:, here] = right - value[R:]


def body(right_side, near_pairs, near_count, near_blocks, far_pairs, coupling, cluster_basis, cluster_slot):
    devices = lax.axis_size("leaf")
    order, place = rounds(devices), places(devices)
    clusters = cluster_basis.shape[0]
    me = lax.axis_index("leaf").astype(jnp.int32).reshape(1)
    basis = cluster_basis.reshape(clusters * K, PANEL)
    sds = jax.ShapeDtypeStruct

    def across(x, b):
        return lax.ppermute(x, "leaf", [(i, i ^ b) for i in range(devices)])

    def shift(x, by):
        return lax.ppermute(x, "leaf", [(i, i + by) for i in range(devices) if 0 <= i + by < devices])

    panels = sds((clusters, R, PANEL), f32)
    narrow = sds((clusters, R, PANEL), bf16)
    split = sds((clusters, 2 * R, PANEL), bf16)
    rank_wide = sds((R, clusters * K), f32)
    rank_split = sds((2 * R, clusters * K), bf16)
    half = devices // 2
    merged_out = sds((devices, clusters * K, clusters * K), bf16)
    payload_out = sds((1 + half, R, clusters * K), bf16)
    kept_out = sds((half, R, clusters * K), f32)
    barrier = lax.optimization_barrier
    near_spaces = [SMEM, SMEM, VMEM, VMEM]

    def in_hbm(x):
        return pltpu.with_memory_space_constraint(x, pltpu.HBM)

    near_pairs, near_blocks, field, right_proj, coupled, payload = call(
        open_kernel,
        (sds(near_pairs.shape, jnp.int32), sds(near_blocks.shape, bf16), split, rank_wide,
         sds((2 * devices, clusters * K, clusters * K), bf16),
         sds((1 + devices, R, clusters * K), bf16)),
        (me, in_hbm(far_pairs), in_hbm(cluster_slot), in_hbm(coupling), in_hbm(right_side), in_hbm(basis),
         in_hbm(near_pairs), in_hbm(near_blocks)),
        [SMEM] + [pltpu.HBM] * 7,
        [
            pltpu.SMEM(far_pairs.shape, jnp.int32),
            pltpu.SMEM(cluster_slot.shape, jnp.int32),
            pltpu.SMEM((devices,), jnp.int32),
            pltpu.VMEM(coupling.shape, bf16),
            pltpu.VMEM(right_side.shape, f32),
            pltpu.VMEM(basis.shape, bf16),
            pltpu.VMEM(((coupling.shape[0] + 8) * (K + 1), 128), f32),
            pltpu.SemaphoreType.DMA((7,)),
        ],
        placed=[SMEM] + [VMEM] * 5,
    )

    def exchange(make_field, beside, keep, payload, merged=None):
        first = merged is None
        for t, b in enumerate(order):
            if t > 0:
                held, half = gathered.shape[0], sums.shape[0] // 2
                payload = jnp.concatenate([gathered, sums[half:].astype(bf16)], axis=0)
                sums = sums[:half]
            else:
                gathered, held = payload[:1], 1
            if t == 2:
                payload, own = barrier((payload, own))
            if t == 3:
                payload, made = barrier((payload, made))
            got = across(payload, b)
            if t == 0:
                sums, cross, corner = keep(payload)
                image, field, got = make_field(got)
                after = shift(field, -1)
                own, following = call(
                    near_cols_kernel, (panels, narrow), (near_pairs, near_count, near_blocks, field), near_spaces,
                    [pltpu.VMEM((2 * clusters + 1, R, PANEL), f32)], moved=12 << 20,
                )
                back = shift(following, 1)
            if t == 1:
                made, got = beside(image, corner, got)
            if t == len(order) - 2:
                after, got = barrier((after, got))
            got_gathered, got_sums = got[:held], got[held:]
            if t < len(order) - 1:
                gathered = jnp.concatenate([gathered, got_gathered], axis=0)
                for piece in range(0, got_sums.shape[0], sums.shape[0]):
                    sums = sums + got_sums[piece : piece + sums.shape[0]].astype(f32)
        kernel, ins, outs = near_rows_kernel, (near_blocks, field, after, own, back, basis), (panels, rank_wide)
        if not first:
            kernel, ins, outs = rows_two_kernel, ins + (right_side, image), outs + (sds((R, 4 * R), f32),)
        near, near_proj, *gram = call(
            kernel, outs, (near_pairs, near_count) + ins, [SMEM] * 2 + [VMEM] * len(ins),
            [pltpu.VMEM((2 * clusters, 2 * R, PANEL), bf16), pltpu.VMEM((clusters + 1, R, PANEL), f32)],
            moved=12 << 20,
        )
        merged = made if first else merged
        return image, near, made, gram, cross, corner, (merged[0], gathered, got_gathered, sums, got_sums, near_proj, cross)

    def first_field(got):
        ready, got = barrier((field, got))
        return right_side, ready, got

    def keep_one(payload):
        return call(
            keep_one_kernel, (kept_out, sds((2, clusters * K, clusters * K), bf16), sds((R, 4 * R), f32)),
            (coupled, payload, basis, right_side), [VMEM] * 4,
        )

    def merging(image, corner, got):
        ready, got = barrier((coupled, got))
        return call(merge_kernel, (merged_out, merged_out), (ready,), [VMEM]), got

    def multiplying(image, corner, got):
        ready, got = barrier((image, got))
        return call(gram_one_kernel, sds((R, 4 * R), f32), (corner, right_side, ready), [VMEM] * 3), got

    unused, near, merged, unused, cross, corner, parts = exchange(first_field, merging, keep_one, payload)
    far, image_proj, payload = call(
        functools.partial(turn_kernel, place), (rank_split, rank_wide, payload_out), parts + (merged[1],), [VMEM] * 8
    )

    def second_field(got):
        ready, got = barrier((far, got))
        return *call(image_kernel, (panels, split), (near, ready, basis), [VMEM] * 3), got

    def keep_two(payload):
        return call(keep_two_kernel, kept_out, (merged[1], payload), [VMEM] * 2), cross, corner

    image, near_two, early, gram, unused, unused, parts = exchange(
        second_field, multiplying, keep_two, payload, merged
    )
    far, gram = call(
        functools.partial(tail_kernel, place), (rank_split, sds((R + R // 2, 4 * R), f32)),
        parts + (right_proj, image_proj, early, *gram), [VMEM] * 11,
    )
    got = None
    for t, b in enumerate(order):
        if t > 0:
            gram = gram + got
        if t == 2:
            gram, second = barrier((gram, second))
        got = across(gram, b)
        if t == 0:
            far, got = barrier((far, got))
            second = call(second_kernel, panels, (near_two, far, basis), [VMEM] * 3)
    wide = sds(right_side.shape, f32)
    solution_field, residual, hessenberg = call(
        last_kernel, (wide, wide, sds((R, 2 * R), f32)), (gram, got, right_side, image, second), [VMEM] * 5
    )
    return solution_field, residual, hessenberg.T


def solution(mesh):
    in_specs = (
        P(None, ("parts", "leaf")),
        P(None, ("parts", "leaf")),
        P(("parts", "leaf")),
        P(("parts", "leaf"), None, None),
        P(None, ("parts", "leaf")),
        P(("parts", "leaf"), None),
        P(("parts", "leaf"), None, None),
        P("parts"),
    )
    out_specs = (P(None, ("parts", "leaf")), P(None, ("parts", "leaf")), P("parts", None))
    return jax.shard_map(body, mesh=mesh, in_specs=in_specs, out_specs=out_specs, check_vma=False)
```

```python
import functools

import jax
import jax.numpy as jnp
from jax import lax
from jax.experimental import pallas as pl
from jax.experimental.pallas import tpu as pltpu
from jax.sharding import PartitionSpec as P

PANEL = 256
R = 32
K = 32
GROUP = 32
highest = lax.Precision.HIGHEST
VMEM = pltpu.VMEM
SMEM = pltpu.SMEM
TN = (((0,), (0,)), ((), ()))
NT = (((1,), (1,)), ((), ()))
f32 = jnp.float32
bf16 = jnp.bfloat16


def spec(space):
    return pl.BlockSpec(memory_space=space)


def call(kernel, outs, ins, spaces, scratch=(), limit=24, flops=10**8, moved=10**6, placed=None):
    return pl.pallas_call(
        kernel,
        out_shape=outs,
        in_specs=[spec(s) for s in spaces],
        out_specs=jax.tree.map(lambda _: spec(VMEM), outs) if placed is None else tuple(map(spec, placed)),
        scratch_shapes=list(scratch),
        compiler_params=pltpu.CompilerParams(vmem_limit_bytes=limit << 20),
        cost_estimate=pl.CostEstimate(flops=flops, bytes_accessed=moved, transcendentals=0),
    )(*ins)


def dot(x, y):
    return jnp.dot(x, y, preferred_element_type=f32)


def dot_nt(x, y):
    return lax.dot_general(x, y, NT, preferred_element_type=f32)


def exact_nt(x, y):
    return lax.dot_general(x, y, NT, precision=highest, preferred_element_type=f32)


def split_rows(x):
    high = x.astype(bf16)
    low = (x - high.astype(f32)).astype(bf16)
    return jnp.concatenate([high, low], axis=0)


def join_rows(x):
    return x[:R] + x[R:]


def lane_group(shape):
    return lax.broadcasted_iota(jnp.int32, shape, 1) // K


def project(fields, basis):
    clusters = fields.shape[0] // (2 * R)
    all_pairs = dot_nt(fields, basis)
    group = lane_group((2 * R, clusters * K))
    total = jnp.zeros((2 * R, clusters * K), f32)
    for c in range(clusters):
        total = total + jnp.where(group == c, all_pairs[c * 2 * R : (c + 1) * 2 * R], 0.0)
    return join_rows(total)


def expand(sums, basis):
    group = lane_group(sums.shape)
    zero = jnp.zeros_like(sums)
    spread = [jnp.where(group == c, sums, zero) for c in range(sums.shape[1] // K)]
    return dot(jnp.concatenate(spread, axis=0), basis)


def rounds(devices):
    bits = devices.bit_length() - 1
    return [1] + [(1 << b) | 1 for b in [bits - 1, 1] + list(range(bits - 2, 1, -1))]


def places(devices):
    steps = rounds(devices)
    place = [0] * devices
    for p in range(devices):
        apart = 0
        for t, step in enumerate(steps):
            if (p >> (len(steps) - 1 - t)) & 1:
                apart ^= step
        place[apart] = p
    return place


def couple(me, pairs_ref, slots_ref, table_ref, wide_ref, out_ref):
    clusters = out_ref.shape[2] // K
    devices = out_ref.shape[0] // 2
    pairs = pairs_ref.shape[1]
    group = lane_group((K, clusters * K))
    shift = clusters.bit_length() - 1
    assert clusters == 1 << shift
    steps = rounds(devices)
    for home in range(devices):
        apart = home ^ me
        parity = apart
        for b in range(1, len(steps)):
            parity = parity ^ (apart >> b)
        place = (parity & 1) << (len(steps) - 1)
        for t, step in enumerate(steps[1:], 1):
            bit = step.bit_length() - 1
            place = place + (((apart >> bit) & 1) << (len(steps) - 1 - t))
        table_ref[home] = place

    def one(f):
        first = slots_ref[pairs_ref[0, f]]
        second = slots_ref[pairs_ref[1, f]]
        first_home, second_home = first >> shift, second >> shift
        own = first_home == me
        where = jnp.where(own, devices, 0) + table_ref[jnp.where(own, second_home, first_home)]
        block = wide_ref[pl.ds(f, K, stride=pairs + 8), :]
        block = jnp.concatenate([block] * (clusters * K // block.shape[1]), axis=1)
        block = jnp.where(group == (second & (clusters - 1)), block, 0.0).astype(bf16)
        here = pl.ds(pl.multiple_of((first & (clusters - 1)) * K, K), K)
        out_ref[where, here, :] = out_ref[where, here, :] + block

    def some(step, carry):
        for u in range(16):
            one(step * 16 + u)
        return carry

    lax.fori_loop(0, pairs // 16, some, 0)


def open_kernel(me_ref, pairs_hbm, slots_hbm, coupling_hbm, right_hbm, basis_hbm, near_hbm, blocks_hbm,
                near_pairs_ref, blocks_ref, field_ref, near_proj_ref, coupled_ref, payload_ref,
                pairs_ref, slots_ref, table_ref, coupling_ref, right_ref, basis_ref, wide_ref, sems):
    clusters = field_ref.shape[0]
    moves = [(coupling_hbm, coupling_ref), (basis_hbm, basis_ref), (right_hbm, right_ref),
             (pairs_hbm, pairs_ref), (slots_hbm, slots_ref), (near_hbm, near_pairs_ref), (blocks_hbm, blocks_ref)]
    copies = [pltpu.make_async_copy(*move, sems.at[i]) for i, move in enumerate(moves)]
    for copy in copies:
        copy.start()
    coupled_ref[...] = jnp.zeros_like(coupled_ref)
    copies[0].wait()
    pairs = coupling_ref.shape[0]
    lanes_held = 128
    rows = lax.broadcasted_iota(jnp.int32, (lanes_held, lanes_held), 0)
    lanes = lax.broadcasted_iota(jnp.int32, (lanes_held, lanes_held), 1)
    tiles = coupling_ref.shape[1] // lanes_held
    flat = jnp.concatenate(
        [coupling_ref[:, t * lanes_held : (t + 1) * lanes_held] for t in range(tiles)], axis=0
    )
    each = lanes_held // K
    for u in range(each):
        spread = jnp.where((lanes % K == rows % K) & (rows // K == u), 1.0, 0.0).astype(bf16)
        value = dot(flat, spread)
        for t in range(tiles):
            begin = (t * each + u) * (pairs + 8)
            wide_ref[begin : begin + pairs] = value[t * pairs : (t + 1) * pairs]
    copies[1].wait()
    basis = basis_ref[...]
    copies[2].wait()
    for c in range(clusters):
        field_ref[c] = split_rows(right_ref[:, c * PANEL : (c + 1) * PANEL])
    proj = project(field_ref[...].reshape(clusters * 2 * R, PANEL), basis)
    near_proj_ref[...] = proj
    copies[3].wait()
    copies[4].wait()
    copies[5].wait()
    couple(me_ref[0], pairs_ref, slots_ref, table_ref, wide_ref, coupled_ref)
    proj = proj.astype(bf16)
    devices = coupled_ref.shape[0] // 2
    send(
        lambda d: dot(proj, coupled_ref[devices + d]) + dot_nt(proj, coupled_ref[d]),
        payload_ref, proj, devices, True,
    )
    copies[6].wait()


def send(products, payload_ref, proj, devices, both):
    payload_ref[0] = proj
    half = devices // 2
    for d in range(half, devices):
        value = products(d)
        high = value.astype(bf16)
        payload_ref[1 + d - half] = high
        if both:
            payload_ref[1 + d] = (value - high.astype(f32)).astype(bf16)


def keep_one_kernel(coupled_ref, payload_ref, basis_ref, right_ref, kept_ref, cross_ref, corner_ref):
    devices = coupled_ref.shape[0] // 2
    proj = payload_ref[0]
    for d in range(devices // 2):
        kept_ref[d] = dot(proj, coupled_ref[devices + d]) + dot_nt(proj, coupled_ref[d])
    basis = basis_ref[...]
    cross = dot_nt(basis, basis)
    same = lane_group(cross.shape) == lax.broadcasted_iota(jnp.int32, cross.shape, 0) // K
    cross = jnp.where(same, cross, 0.0)
    high = cross.astype(bf16)
    cross_ref[0] = high
    cross_ref[1] = (cross - high.astype(f32)).astype(bf16)
    corner = jnp.zeros((R, 4 * R), f32)
    zero = jnp.zeros((R, PANEL), f32)
    for c in range(right_ref.shape[1] // PANEL):
        right = right_ref[:, c * PANEL : (c + 1) * PANEL]
        corner = corner + exact_nt(right, jnp.concatenate([zero, zero, right, zero], axis=0))
    corner_ref[...] = corner


def keep_two_kernel(turned_ref, payload_ref, kept_ref):
    proj = payload_ref[0]
    for d in range(kept_ref.shape[0]):
        kept_ref[d] = dot(proj, turned_ref[d])


def near_loop(count_ref, one):
    def group(g, carry):
        for u in range(GROUP):
            one(g * GROUP + u)
        return carry

    lax.fori_loop(0, (count_ref[0] + GROUP - 1) // GROUP, group, 0)


def near_cols_kernel(pairs_ref, count_ref, blocks_ref, field_ref, own_ref, next_ref, total):
    clusters = field_ref.shape[0]
    total[...] = jnp.zeros_like(total)

    def one(s):
        i = pairs_ref[0, s]
        j = jnp.where(s < count_ref[0], pairs_ref[1, s], 2 * clusters)
        total[j] = total[j] + join_rows(dot(field_ref[i], blocks_ref[s]))

    near_loop(count_ref, one)
    own_ref[...] = total[:clusters]
    next_ref[...] = total[clusters : 2 * clusters].astype(bf16)


def near_rows_kernel(pairs_ref, count_ref, blocks_ref, field_ref, after_ref, begun_ref, back_ref, basis_ref,
                     out_ref, proj_ref, window, total):
    clusters = field_ref.shape[0]
    window[:clusters] = field_ref[...]
    window[clusters:] = after_ref[...]
    total[:clusters] = begun_ref[...] + back_ref[...].astype(f32)
    total[clusters] = jnp.zeros_like(total[clusters])

    def one(s):
        i = jnp.where(s < count_ref[0], pairs_ref[0, s], clusters)
        j = pairs_ref[1, s]
        total[i] = total[i] + join_rows(dot_nt(window[j], blocks_ref[s]))

    near_loop(count_ref, one)
    near = total[:clusters]
    out_ref[...] = near
    split = jnp.concatenate([split_rows(near[c]) for c in range(clusters)], axis=0)
    proj_ref[...] = project(split, basis_ref[...])


def rows_two_kernel(pairs_ref, count_ref, blocks_ref, field_ref, after_ref, begun_ref, back_ref, basis_ref,
                    right_ref, image_ref, out_ref, proj_ref, gram_ref, window, total):
    near_rows_kernel(pairs_ref, count_ref, blocks_ref, field_ref, after_ref, begun_ref, back_ref, basis_ref,
                     out_ref, proj_ref, window, total)
    gram_two(right_ref, image_ref, out_ref, gram_ref)


def merge_kernel(coupled_ref, out_ref, turned_ref):
    devices = out_ref.shape[0]
    for d in range(devices):
        near, away = coupled_ref[d], coupled_ref[devices + d]
        out_ref[d] = near + away.T
        turned_ref[d] = away + near.T


def far_sums(place, merged_ref, low_ref, high_ref, kept_ref, got_ref):
    devices = merged_ref.shape[0]
    sums = kept_ref[0]
    for piece in range(got_ref.shape[0]):
        sums = sums + got_ref[piece].astype(f32)
    steps = rounds(devices)
    for g in range(devices):
        proj = low_ref[g] if g < devices // 2 else high_ref[g - devices // 2]
        apart = functools.reduce(lambda x, y: x ^ y, [step for t, step in enumerate(steps) if (g >> t) & 1], 0)
        sums = sums + dot(proj, merged_ref[place[apart]])
    return split_rows(sums)


def across_clusters(sums, cross_ref):
    return join_rows(dot(sums, cross_ref[0])) + dot(sums[:R], cross_ref[1])


def turn_kernel(place, merged_ref, low_ref, high_ref, kept_ref, got_ref, near_proj_ref, cross_ref,
                turned_ref, sums_ref, proj_ref, payload_ref):
    sums = far_sums(place, merged_ref, low_ref, high_ref, kept_ref, got_ref)
    sums_ref[...] = sums
    proj = near_proj_ref[...] + across_clusters(sums, cross_ref)
    proj_ref[...] = proj
    proj = proj.astype(bf16)
    send(lambda d: dot(proj, turned_ref[d]), payload_ref, proj, turned_ref.shape[0], False)


def image_kernel(near_ref, sums_ref, basis_ref, image_ref, field_ref):
    far = expand(sums_ref[...], basis_ref[...])
    for c in range(near_ref.shape[0]):
        image = near_ref[c] + join_rows(far[c * 2 * R : (c + 1) * 2 * R])
        image_ref[c] = image
        field_ref[c] = split_rows(image)


def second_kernel(near_ref, sums_ref, basis_ref, image_ref):
    far = expand(sums_ref[...], basis_ref[...])
    for c in range(near_ref.shape[0]):
        image_ref[c] = near_ref[c] + join_rows(far[c * 2 * R : (c + 1) * 2 * R])


def gram_one_kernel(corner_ref, right_ref, image_ref, gram_ref):
    gram = corner_ref[...]
    zero = jnp.zeros((R, PANEL), f32)
    for c in range(image_ref.shape[0]):
        right, image = right_ref[:, c * PANEL : (c + 1) * PANEL], image_ref[c]
        gram = gram + exact_nt(image, jnp.concatenate([right, image, zero, zero], axis=0))
    gram_ref[...] = gram


def gram_two(right_ref, image_ref, near_ref, gram_ref):
    gram = jnp.zeros((R, 4 * R), f32)
    zero = jnp.zeros((R, PANEL), f32)
    for c in range(image_ref.shape[0]):
        right, near = right_ref[:, c * PANEL : (c + 1) * PANEL], near_ref[c]
        gram = gram + exact_nt(near, jnp.concatenate([right, image_ref[c], near, zero], axis=0))
    gram_ref[...] = gram


def tail_kernel(place, merged_ref, low_ref, high_ref, kept_ref, got_ref, near_proj_ref, cross_ref,
                right_proj_ref, image_proj_ref, early_ref, gram_ref, sums_ref, out_ref):
    sums = far_sums(place, merged_ref, low_ref, high_ref, kept_ref, got_ref)
    sums_ref[...] = sums
    half = near_proj_ref[...] + 0.5 * across_clusters(sums, cross_ref)
    sums = join_rows(sums.astype(f32))
    known = jnp.concatenate([right_proj_ref[...], image_proj_ref[...], half, jnp.zeros_like(half)], axis=0)
    added = exact_nt(sums, known)
    mirror = exact_nt(half, jnp.concatenate([jnp.zeros_like(sums)] * 2 + [sums, jnp.zeros_like(sums)], axis=0))
    late = gram_ref[...] + added + mirror
    lanes = lane_group(late.shape)
    out_ref[:R] = jnp.where(lanes == 3, pltpu.roll(late, 3 * R, 1), early_ref[...])
    rest = pltpu.roll(late, 3 * R, 1)
    half_rows = R // 2
    out_ref[R:] = jnp.where(lanes[:half_rows] < 2, rest[:half_rows], pltpu.roll(rest[half_rows:], 2 * R, 1))


TALL = 8


def lane(x, k):
    return jnp.broadcast_to(x[:, k : k + 1], x.shape)


def eliminate(wide, late, k):
    block, at = k // TALL, k % TALL
    rows = lax.broadcasted_iota(jnp.int32, wide[block].shape, 0)
    both = [wide] if late is None or block < len(wide) // 2 else [wide, late]
    columns = [[lane(x, k + j) for x in wide[block:]] for j in range(4)]
    m = [[columns[j][0][at + i : at + i + 1] for j in range(4)] for i in range(4)]
    scale = 1.0 / (m[0][0] * m[1][1] - m[0][1] * m[1][0])
    first = {j: (m[1][1] * m[0][j] - m[0][1] * m[1][j]) * scale for j in (2, 3)}
    second = {j: (m[0][0] * m[1][j] - m[1][0] * m[0][j]) * scale for j in (2, 3)}
    s = {(i, j): m[i][j] - (m[i][0] * first[j] + m[i][1] * second[j]) for i in (2, 3) for j in (2, 3)}
    after = 1.0 / (s[2, 2] * s[3, 3] - s[2, 3] * s[3, 2])
    ratio, last_ratio = m[1][0] / m[0][0], s[3, 2] / s[2, 2]
    for part in both:
        p = [part[block][at + i : at + i + 1] for i in range(4)]
        y0 = (m[1][1] * p[0] - m[0][1] * p[1]) * scale
        y1 = (m[0][0] * p[1] - m[1][0] * p[0]) * scale
        r2 = p[2] - (m[2][0] * y0 + m[2][1] * y1)
        r3 = p[3] - (m[3][0] * y0 + m[3][1] * y1)
        x2 = (s[3, 3] * r2 - s[2, 3] * r3) * after
        x3 = (s[2, 2] * r3 - s[3, 2] * r2) * after
        x0 = y0 - (first[2] * x2 + first[3] * x3)
        x1 = y1 - (second[2] * x2 + second[3] * x3)
        own = [p[0], p[1] - ratio * p[0], r2, r3 - last_ratio * r2]
        for i in range(block, len(wide)):
            c = [column[i - block] for column in columns]
            rest = part[i] - ((c[0] * x0 + c[1] * x1) + (c[2] * x2 + c[3] * x3))
            if i == block:
                rest = jnp.where(rows > at + 3, rest, part[i])
                for t in range(1, 4):
                    rest = jnp.where(rows == at + t, own[t], rest)
            part[i] = rest


def last_kernel(kept_ref, got_ref, right_ref, image_ref, second_ref, field_ref, residual_ref, hessenberg_ref):
    clusters = image_ref.shape[0]
    gram = kept_ref[...] + got_ref[...]
    top, folded = gram[:R], gram[R:]
    bottom = jnp.concatenate([folded[:, : 2 * R], folded[:, 2 * R :]], axis=0)
    lanes = lax.broadcasted_iota(jnp.int32, (2 * R, 4 * R), 1)
    rows = lax.broadcasted_iota(jnp.int32, (2 * R, 4 * R), 0)
    wide = jnp.zeros((R, R), f32)
    first_first, image_first = top[:, 2 * R : 3 * R], top[:, :R]
    image_image, second_first = top[:, R : 2 * R], top[:, 3 * R :]
    second_image, second_second = bottom[:, :R], bottom[:, R:]
    on_diagonal = lax.broadcasted_iota(jnp.int32, (R, R), 0) == lax.broadcasted_iota(jnp.int32, (R, R), 1)

    def shrink(x):
        trace = jnp.sum(jnp.where(on_diagonal, x, 0.0), axis=0, keepdims=True)
        return lax.rsqrt(jnp.sum(trace, axis=1, keepdims=True) / R)

    at_first, at_image, at_second = shrink(first_first), shrink(image_image), shrink(second_second)
    stretch = at_first / at_image
    first_first, image_first = first_first * at_first * at_first, image_first * at_image * at_first
    image_image, second_second = image_image * at_image * at_image, second_second * at_second * at_second
    second_image, second_first = second_image * at_second * at_image, second_first * at_second * at_first
    system = jnp.concatenate(
        [
            jnp.concatenate([image_image, second_image.T, image_first, wide], axis=1),
            jnp.concatenate([second_image, second_second, second_first, wide], axis=1),
        ],
        axis=0,
    )
    lower = jnp.concatenate(
        [
            jnp.concatenate([first_first, image_first.T, wide, wide], axis=1),
            jnp.concatenate([image_first, image_image, wide, wide], axis=1),
        ],
        axis=0,
    )
    lower = jnp.where(lanes - 2 * R == rows, 1.0, lower)
    system = jnp.where(lanes - 3 * R == rows, 1.0, system)
    late = jnp.where(lanes + R == rows, 1.0, 0.0)

    def blocks(x):
        return [x[i : i + TALL] for i in range(0, 2 * R, TALL)]

    system, lower, late = blocks(system), blocks(lower), blocks(late)
    for k in range(0, 2 * R, 4):
        eliminate(system, late, k)
        eliminate(lower, None, k)
    system, lower, late = (jnp.concatenate(x, axis=0) for x in (system, lower, late))

    def diagonal(x):
        return jnp.sum(jnp.where(lanes == rows, x, 0.0), axis=1, keepdims=True)

    lower = lower * lax.rsqrt(diagonal(lower))
    scaled = system[:, 2 * R : 3 * R] / diagonal(system)
    inverse = jnp.concatenate([system[:, 3 * R :], late[:, :R]], axis=1)
    weights = lax.dot_general(scaled, inverse, TN, precision=highest, preferred_element_type=f32)
    weights = weights * jnp.where(lanes[:R, : 2 * R] < R, at_image, at_second) / at_first
    inverse_zero = lower[:R, 2 * R : 3 * R]
    hessenberg_ref[:, :R] = stretch * exact_nt(inverse_zero, lower[:R, R : 2 * R])
    hessenberg_ref[:, R:] = stretch * lax.dot_general(
        lower[R:, R : 2 * R], inverse_zero, NT, precision=highest, preferred_element_type=f32
    )
    none = jnp.zeros((R, R), f32)
    mix = jnp.concatenate(
        [jnp.concatenate([weights, none], axis=1), jnp.concatenate([none, weights], axis=1)], axis=0
    )
    mix_high = mix.astype(bf16)
    mix_both = jnp.concatenate([mix_high, (mix - mix_high.astype(f32)).astype(bf16)], axis=0)
    for c in range(clusters):
        here = slice(c * PANEL, (c + 1) * PANEL)
        right = right_ref[:, here]
        stacked = jnp.concatenate([right, image_ref[c], second_ref[c]], axis=0)
        high = stacked.astype(bf16)
        low = (stacked - high.astype(f32)).astype(bf16)
        both = dot(mix_both, high)
        value = both[: 2 * R] + both[2 * R :] + dot(mix_high, low)
        field_ref[:, here] = value[:R]
        residual_ref[:, here] = right - value[R:]


def body(right_side, near_pairs, near_count, near_blocks, far_pairs, coupling, cluster_basis, cluster_slot):
    devices = lax.axis_size("leaf")
    order, place = rounds(devices), places(devices)
    clusters = cluster_basis.shape[0]
    me = lax.axis_index("leaf").astype(jnp.int32).reshape(1)
    basis = cluster_basis.reshape(clusters * K, PANEL)
    sds = jax.ShapeDtypeStruct

    def across(x, b):
        return lax.ppermute(x, "leaf", [(i, i ^ b) for i in range(devices)])

    def shift(x, by):
        return lax.ppermute(x, "leaf", [(i, i + by) for i in range(devices) if 0 <= i + by < devices])

    panels = sds((clusters, R, PANEL), f32)
    narrow = sds((clusters, R, PANEL), bf16)
    split = sds((clusters, 2 * R, PANEL), bf16)
    rank_wide = sds((R, clusters * K), f32)
    rank_split = sds((2 * R, clusters * K), bf16)
    half = devices // 2
    merged_out = sds((devices, clusters * K, clusters * K), bf16)
    payload_out = sds((1 + half, R, clusters * K), bf16)
    kept_out = sds((half, R, clusters * K), f32)
    barrier = lax.optimization_barrier
    near_spaces = [SMEM, SMEM, VMEM, VMEM]

    def in_hbm(x):
        return pltpu.with_memory_space_constraint(x, pltpu.HBM)

    near_pairs, near_blocks, field, right_proj, coupled, payload = call(
        open_kernel,
        (sds(near_pairs.shape, jnp.int32), sds(near_blocks.shape, bf16), split, rank_wide,
         sds((2 * devices, clusters * K, clusters * K), bf16),
         sds((1 + devices, R, clusters * K), bf16)),
        (me, in_hbm(far_pairs), in_hbm(cluster_slot), in_hbm(coupling), in_hbm(right_side), in_hbm(basis),
         in_hbm(near_pairs), in_hbm(near_blocks)),
        [SMEM] + [pltpu.HBM] * 7,
        [
            pltpu.SMEM(far_pairs.shape, jnp.int32),
            pltpu.SMEM(cluster_slot.shape, jnp.int32),
            pltpu.SMEM((devices,), jnp.int32),
            pltpu.VMEM(coupling.shape, bf16),
            pltpu.VMEM(right_side.shape, f32),
            pltpu.VMEM(basis.shape, bf16),
            pltpu.VMEM(((coupling.shape[0] + 8) * (K + 1), 128), f32),
            pltpu.SemaphoreType.DMA((7,)),
        ],
        placed=[SMEM] + [VMEM] * 5,
    )

    def exchange(make_field, beside, keep, payload, merged=None):
        first = merged is None
        for t, b in enumerate(order):
            if t > 0:
                held, half = gathered.shape[0], sums.shape[0] // 2
                payload = jnp.concatenate([gathered, sums[half:].astype(bf16)], axis=0)
                sums = sums[:half]
            else:
                gathered, held = payload[:1], 1
            if t == 2:
                payload, own = barrier((payload, own))
            if t == 3:
                payload, made = barrier((payload, made))
            got = across(payload, b)
            if t == 0:
                sums, cross, corner = keep(payload)
                image, field, got = make_field(got)
                after = shift(field, -1)
                own, following = call(
                    near_cols_kernel, (panels, narrow), (near_pairs, near_count, near_blocks, field), near_spaces,
                    [pltpu.VMEM((2 * clusters + 1, R, PANEL), f32)], moved=12 << 20,
                )
                back = shift(following, 1)
            if t == 1:
                made, got = beside(image, corner, got)
            if t == len(order) - 2:
                after, got = barrier((after, got))
            got_gathered, got_sums = got[:held], got[held:]
            if t < len(order) - 1:
                gathered = jnp.concatenate([gathered, got_gathered], axis=0)
                for piece in range(0, got_sums.shape[0], sums.shape[0]):
                    sums = sums + got_sums[piece : piece + sums.shape[0]].astype(f32)
        kernel, ins, outs = near_rows_kernel, (near_blocks, field, after, own, back, basis), (panels, rank_wide)
        if not first:
            kernel, ins, outs = rows_two_kernel, ins + (right_side, image), outs + (sds((R, 4 * R), f32),)
        near, near_proj, *gram = call(
            kernel, outs, (near_pairs, near_count) + ins, [SMEM] * 2 + [VMEM] * len(ins),
            [pltpu.VMEM((2 * clusters, 2 * R, PANEL), bf16), pltpu.VMEM((clusters + 1, R, PANEL), f32)],
            moved=12 << 20,
        )
        merged = made if first else merged
        return image, near, made, gram, cross, corner, (merged[0], gathered, got_gathered, sums, got_sums, near_proj, cross)

    def first_field(got):
        ready, got = barrier((field, got))
        return right_side, ready, got

    def keep_one(payload):
        return call(
            keep_one_kernel, (kept_out, sds((2, clusters * K, clusters * K), bf16), sds((R, 4 * R), f32)),
            (coupled, payload, basis, right_side), [VMEM] * 4,
        )

    def merging(image, corner, got):
        ready, got = barrier((coupled, got))
        return call(merge_kernel, (merged_out, merged_out), (ready,), [VMEM]), got

    def multiplying(image, corner, got):
        ready, got = barrier((image, got))
        return call(gram_one_kernel, sds((R, 4 * R), f32), (corner, right_side, ready), [VMEM] * 3), got

    unused, near, merged, unused, cross, corner, parts = exchange(first_field, merging, keep_one, payload)
    far, image_proj, payload = call(
        functools.partial(turn_kernel, place), (rank_split, rank_wide, payload_out), parts + (merged[1],), [VMEM] * 8
    )

    def second_field(got):
        ready, got = barrier((far, got))
        return *call(image_kernel, (panels, split), (near, ready, basis), [VMEM] * 3), got

    def keep_two(payload):
        return call(keep_two_kernel, kept_out, (merged[1], payload), [VMEM] * 2), cross, corner

    image, near_two, early, gram, unused, unused, parts = exchange(
        second_field, multiplying, keep_two, payload, merged
    )
    far, gram = call(
        functools.partial(tail_kernel, place), (rank_split, sds((R + R // 2, 4 * R), f32)),
        parts + (right_proj, image_proj, early, *gram), [VMEM] * 11,
    )
    got = None
    for t, b in enumerate(order):
        if t > 0:
            gram = gram + got
        if t == 2:
            gram, second = barrier((gram, second))
        got = across(gram, b)
        if t == 0:
            far, got = barrier((far, got))
            second = call(second_kernel, panels, (near_two, far, basis), [VMEM] * 3)
    wide = sds(right_side.shape, f32)
    solution_field, residual, hessenberg = call(
        last_kernel, (wide, wide, sds((R, 2 * R), f32)), (gram, got, right_side, image, second), [VMEM] * 5
    )
    return solution_field, residual, hessenberg.T


def solution(mesh):
    in_specs = (
        P(None, ("parts", "leaf")),
        P(None, ("parts", "leaf")),
        P(("parts", "leaf")),
        P(("parts", "leaf"), None, None),
        P(None, ("parts", "leaf")),
        P(("parts", "leaf"), None),
        P(("parts", "leaf"), None, None),
        P("parts"),
    )
    out_specs = (P(None, ("parts", "leaf")), P(None, ("parts", "leaf")), P("parts", None))
    return jax.shard_map(body, mesh=mesh, in_specs=in_specs, out_specs=out_specs, check_vma=False)
```

```python
import functools

import jax
import jax.numpy as jnp
from jax import lax
from jax.experimental import pallas as pl
from jax.experimental.pallas import tpu as pltpu
from jax.sharding import PartitionSpec as P

PANEL = 256
R = 32
K = 32
GROUP = 32
highest = lax.Precision.HIGHEST
VMEM = pltpu.VMEM
SMEM = pltpu.SMEM
TN = (((0,), (0,)), ((), ()))
NT = (((1,), (1,)), ((), ()))
f32 = jnp.float32
bf16 = jnp.bfloat16


def spec(space):
    return pl.BlockSpec(memory_space=space)


def call(kernel, outs, ins, spaces, scratch=(), limit=24, flops=10**8, moved=10**6, placed=None):
    return pl.pallas_call(
        kernel,
        out_shape=outs,
        in_specs=[spec(s) for s in spaces],
        out_specs=jax.tree.map(lambda _: spec(VMEM), outs) if placed is None else tuple(map(spec, placed)),
        scratch_shapes=list(scratch),
        compiler_params=pltpu.CompilerParams(vmem_limit_bytes=limit << 20),
        cost_estimate=pl.CostEstimate(flops=flops, bytes_accessed=moved, transcendentals=0),
    )(*ins)


def dot(x, y):
    return jnp.dot(x, y, preferred_element_type=f32)


def dot_nt(x, y):
    return lax.dot_general(x, y, NT, preferred_element_type=f32)


def exact_nt(x, y):
    return lax.dot_general(x, y, NT, precision=highest, preferred_element_type=f32)


def split_rows(x):
    high = x.astype(bf16)
    low = (x - high.astype(f32)).astype(bf16)
    return jnp.concatenate([high, low], axis=0)


def join_rows(x):
    return x[:R] + x[R:]


def split_nt(x, high, low):
    return join_rows(dot_nt(x, high)) + dot_nt(x[:R], low)


def stack(*halves):
    zero = jnp.zeros((R, halves[0 if halves[0] is not None else 2].shape[1]), bf16)
    return (
        jnp.concatenate([zero if x is None else x[:R] for x in halves], axis=0),
        jnp.concatenate([zero if x is None else x[R:] for x in halves], axis=0),
    )


def lane_group(shape):
    return lax.broadcasted_iota(jnp.int32, shape, 1) // K


def project(fields, basis):
    clusters = fields.shape[0] // (2 * R)
    all_pairs = dot_nt(fields, basis)
    group = lane_group((2 * R, clusters * K))
    total = jnp.zeros((2 * R, clusters * K), f32)
    for c in range(clusters):
        total = total + jnp.where(group == c, all_pairs[c * 2 * R : (c + 1) * 2 * R], 0.0)
    return join_rows(total)


def expand(sums, basis):
    group = lane_group(sums.shape)
    zero = jnp.zeros_like(sums)
    spread = [jnp.where(group == c, sums, zero) for c in range(sums.shape[1] // K)]
    return dot(jnp.concatenate(spread, axis=0), basis)


def rounds(devices):
    bits = devices.bit_length() - 1
    return [1] + [(1 << b) | 1 for b in [bits - 1, 1] + list(range(bits - 2, 1, -1))]


def places(devices):
    steps = rounds(devices)
    place = [0] * devices
    for p in range(devices):
        apart = 0
        for t, step in enumerate(steps):
            if (p >> (len(steps) - 1 - t)) & 1:
                apart ^= step
        place[apart] = p
    return place


def couple(me, pairs_ref, slots_ref, table_ref, wide_ref, out_ref):
    clusters = out_ref.shape[2] // K
    devices = out_ref.shape[0] // 2
    pairs = pairs_ref.shape[1]
    group = lane_group((K, clusters * K))
    shift = clusters.bit_length() - 1
    assert clusters == 1 << shift
    steps = rounds(devices)
    for home in range(devices):
        apart = home ^ me
        parity = apart
        for b in range(1, len(steps)):
            parity = parity ^ (apart >> b)
        place = (parity & 1) << (len(steps) - 1)
        for t, step in enumerate(steps[1:], 1):
            bit = step.bit_length() - 1
            place = place + (((apart >> bit) & 1) << (len(steps) - 1 - t))
        table_ref[home] = place

    def one(f):
        first = slots_ref[pairs_ref[0, f]]
        second = slots_ref[pairs_ref[1, f]]
        first_home, second_home = first >> shift, second >> shift
        own = first_home == me
        where = jnp.where(own, devices, 0) + table_ref[jnp.where(own, second_home, first_home)]
        block = wide_ref[pl.ds(f, K, stride=pairs + 8), :]
        block = jnp.concatenate([block] * (clusters * K // block.shape[1]), axis=1)
        block = jnp.where(group == (second & (clusters - 1)), block, 0.0).astype(bf16)
        here = pl.ds(pl.multiple_of((first & (clusters - 1)) * K, K), K)
        out_ref[where, here, :] = out_ref[where, here, :] + block

    def some(step, carry):
        for u in range(16):
            one(step * 16 + u)
        return carry

    lax.fori_loop(0, pairs // 16, some, 0)


def open_kernel(me_ref, pairs_hbm, slots_hbm, coupling_hbm, right_hbm, basis_hbm, near_hbm, blocks_hbm,
                near_pairs_ref, blocks_ref, field_ref, near_proj_ref, coupled_ref, payload_ref,
                pairs_ref, slots_ref, table_ref, coupling_ref, right_ref, basis_ref, wide_ref, sems):
    clusters = field_ref.shape[0]
    moves = [(coupling_hbm, coupling_ref), (basis_hbm, basis_ref), (right_hbm, right_ref),
             (pairs_hbm, pairs_ref), (slots_hbm, slots_ref), (near_hbm, near_pairs_ref), (blocks_hbm, blocks_ref)]
    copies = [pltpu.make_async_copy(*move, sems.at[i]) for i, move in enumerate(moves)]
    for copy in copies:
        copy.start()
    coupled_ref[...] = jnp.zeros_like(coupled_ref)
    copies[0].wait()
    pairs = coupling_ref.shape[0]
    lanes_held = 128
    rows = lax.broadcasted_iota(jnp.int32, (lanes_held, lanes_held), 0)
    lanes = lax.broadcasted_iota(jnp.int32, (lanes_held, lanes_held), 1)
    tiles = coupling_ref.shape[1] // lanes_held
    flat = jnp.concatenate(
        [coupling_ref[:, t * lanes_held : (t + 1) * lanes_held] for t in range(tiles)], axis=0
    )
    each = lanes_held // K
    for u in range(each):
        spread = jnp.where((lanes % K == rows % K) & (rows // K == u), 1.0, 0.0).astype(bf16)
        value = dot(flat, spread)
        for t in range(tiles):
            begin = (t * each + u) * (pairs + 8)
            wide_ref[begin : begin + pairs] = value[t * pairs : (t + 1) * pairs]
    copies[1].wait()
    basis = basis_ref[...]
    copies[2].wait()
    for c in range(clusters):
        field_ref[c] = split_rows(right_ref[:, c * PANEL : (c + 1) * PANEL])
    proj = project(field_ref[...].reshape(clusters * 2 * R, PANEL), basis)
    near_proj_ref[...] = proj
    copies[3].wait()
    copies[4].wait()
    copies[5].wait()
    couple(me_ref[0], pairs_ref, slots_ref, table_ref, wide_ref, coupled_ref)
    proj = proj.astype(bf16)
    devices = coupled_ref.shape[0] // 2
    send(
        lambda d: dot(proj, coupled_ref[devices + d]) + dot_nt(proj, coupled_ref[d]),
        payload_ref, proj, devices, True,
    )
    copies[6].wait()


def send(products, payload_ref, proj, devices, both):
    payload_ref[0] = proj
    half = devices // 2
    for d in range(half, devices):
        value = products(d)
        high = value.astype(bf16)
        payload_ref[1 + d - half] = high
        if both:
            payload_ref[1 + d] = (value - high.astype(f32)).astype(bf16)


def keep_one_kernel(coupled_ref, payload_ref, basis_ref, field_ref, kept_ref, cross_ref, corner_ref):
    devices = coupled_ref.shape[0] // 2
    proj = payload_ref[0]
    for d in range(devices // 2):
        kept_ref[d] = dot(proj, coupled_ref[devices + d]) + dot_nt(proj, coupled_ref[d])
    basis = basis_ref[...]
    cross = dot_nt(basis, basis)
    same = lane_group(cross.shape) == lax.broadcasted_iota(jnp.int32, cross.shape, 0) // K
    cross = jnp.where(same, cross, 0.0)
    high = cross.astype(bf16)
    cross_ref[0] = high
    cross_ref[1] = (cross - high.astype(f32)).astype(bf16)
    corner = jnp.zeros((R, 4 * R), f32)
    for c in range(field_ref.shape[0]):
        right = field_ref[c]
        corner = corner + split_nt(right, *stack(None, None, right, None))
    corner_ref[...] = corner


def keep_two_kernel(turned_ref, payload_ref, kept_ref):
    proj = payload_ref[0]
    for d in range(kept_ref.shape[0]):
        kept_ref[d] = dot(proj, turned_ref[d])


def near_loop(count_ref, one):
    def group(g, carry):
        for u in range(GROUP):
            one(g * GROUP + u)
        return carry

    lax.fori_loop(0, (count_ref[0] + GROUP - 1) // GROUP, group, 0)


def near_cols_kernel(pairs_ref, count_ref, blocks_ref, field_ref, own_ref, next_ref, total):
    clusters = field_ref.shape[0]
    total[...] = jnp.zeros_like(total)

    def one(s):
        i = pairs_ref[0, s]
        j = jnp.where(s < count_ref[0], pairs_ref[1, s], 2 * clusters)
        total[j] = total[j] + join_rows(dot(field_ref[i], blocks_ref[s]))

    near_loop(count_ref, one)
    own_ref[...] = total[:clusters]
    next_ref[...] = total[clusters : 2 * clusters].astype(bf16)


def near_rows(pairs_ref, count_ref, blocks_ref, field_ref, after_ref, begun_ref, back_ref, basis_ref,
                     out_ref, proj_ref, window, total):
    clusters = field_ref.shape[0]
    window[:clusters] = field_ref[...]
    window[clusters:] = after_ref[...]
    total[:clusters] = begun_ref[...] + back_ref[...].astype(f32)
    total[clusters] = jnp.zeros_like(total[clusters])

    def one(s):
        i = jnp.where(s < count_ref[0], pairs_ref[0, s], clusters)
        j = pairs_ref[1, s]
        total[i] = total[i] + join_rows(dot_nt(window[j], blocks_ref[s]))

    near_loop(count_ref, one)
    near = total[:clusters]
    out_ref[...] = near
    split = jnp.concatenate([split_rows(near[c]) for c in range(clusters)], axis=0)
    proj_ref[...] = project(split, basis_ref[...])
    return split


def rows_one_kernel(*refs):
    near_rows(*refs)


def rows_two_kernel(pairs_ref, count_ref, blocks_ref, field_ref, after_ref, begun_ref, back_ref, basis_ref,
                    right_ref, out_ref, proj_ref, gram_ref, window, total):
    split = near_rows(pairs_ref, count_ref, blocks_ref, field_ref, after_ref, begun_ref, back_ref, basis_ref,
                      out_ref, proj_ref, window, total)
    gram = jnp.zeros((R, 4 * R), f32)
    for c in range(field_ref.shape[0]):
        near = split[c * 2 * R : (c + 1) * 2 * R]
        gram = gram + split_nt(near, *stack(right_ref[c], field_ref[c], near, None))
    gram_ref[...] = gram


def merge_kernel(coupled_ref, out_ref, turned_ref):
    devices = out_ref.shape[0]
    for d in range(devices):
        near, away = coupled_ref[d], coupled_ref[devices + d]
        out_ref[d] = near + away.T
        turned_ref[d] = away + near.T


def far_sums(place, merged_ref, low_ref, high_ref, kept_ref, got_ref):
    devices = merged_ref.shape[0]
    sums = kept_ref[0]
    for piece in range(got_ref.shape[0]):
        sums = sums + got_ref[piece].astype(f32)
    steps = rounds(devices)
    for g in range(devices):
        proj = low_ref[g] if g < devices // 2 else high_ref[g - devices // 2]
        apart = functools.reduce(lambda x, y: x ^ y, [step for t, step in enumerate(steps) if (g >> t) & 1], 0)
        sums = sums + dot(proj, merged_ref[place[apart]])
    return split_rows(sums)


def across_clusters(sums, cross_ref):
    return join_rows(dot(sums, cross_ref[0])) + dot(sums[:R], cross_ref[1])


def turn_kernel(place, merged_ref, low_ref, high_ref, kept_ref, got_ref, near_proj_ref, cross_ref,
                turned_ref, sums_ref, proj_ref, payload_ref):
    sums = far_sums(place, merged_ref, low_ref, high_ref, kept_ref, got_ref)
    sums_ref[...] = sums
    proj = near_proj_ref[...] + across_clusters(sums, cross_ref)
    proj_ref[...] = proj
    proj = proj.astype(bf16)
    send(lambda d: dot(proj, turned_ref[d]), payload_ref, proj, turned_ref.shape[0], False)


def image_kernel(near_ref, sums_ref, basis_ref, image_ref, field_ref):
    far = expand(sums_ref[...], basis_ref[...])
    for c in range(near_ref.shape[0]):
        image = near_ref[c] + join_rows(far[c * 2 * R : (c + 1) * 2 * R])
        image_ref[c] = image
        field_ref[c] = split_rows(image)


def second_kernel(near_ref, sums_ref, basis_ref, image_ref):
    far = expand(sums_ref[...], basis_ref[...])
    for c in range(near_ref.shape[0]):
        image_ref[c] = near_ref[c] + join_rows(far[c * 2 * R : (c + 1) * 2 * R])


def gram_one_kernel(corner_ref, right_ref, image_ref, gram_ref):
    gram = corner_ref[...]
    for c in range(image_ref.shape[0]):
        gram = gram + split_nt(image_ref[c], *stack(right_ref[c], image_ref[c], None, None))
    gram_ref[...] = gram


def tail_kernel(place, merged_ref, low_ref, high_ref, kept_ref, got_ref, near_proj_ref, cross_ref,
                right_proj_ref, image_proj_ref, early_ref, gram_ref, sums_ref, out_ref):
    sums = far_sums(place, merged_ref, low_ref, high_ref, kept_ref, got_ref)
    sums_ref[...] = sums
    half = near_proj_ref[...] + 0.5 * across_clusters(sums, cross_ref)
    known = jnp.concatenate([right_proj_ref[...], image_proj_ref[...], half, jnp.zeros_like(half)], axis=0)
    high = known.astype(bf16)
    added = split_nt(sums, high, (known - high.astype(f32)).astype(bf16))
    mirror = jnp.where(lane_group(added.shape) == 2, jnp.concatenate([added[:, 2 * R : 3 * R].T] * 4, axis=1), 0.0)
    late = gram_ref[...] + added + mirror
    lanes = lane_group(late.shape)
    out_ref[:R] = jnp.where(lanes == 3, pltpu.roll(late, 3 * R, 1), early_ref[...])
    rest = pltpu.roll(late, 3 * R, 1)
    half_rows = R // 2
    out_ref[R:] = jnp.where(lanes[:half_rows] < 2, rest[:half_rows], pltpu.roll(rest[half_rows:], 2 * R, 1))


TALL = 8


def lane(x, k):
    return jnp.broadcast_to(x[:, k : k + 1], x.shape)


def eliminate(wide, late, k):
    block, at = k // TALL, k % TALL
    rows = lax.broadcasted_iota(jnp.int32, wide[block].shape, 0)
    both = [wide] if late is None or block < len(wide) // 2 else [wide, late]
    columns = [[lane(x, k + j) for x in wide[block:]] for j in range(4)]
    m = [[columns[j][0][at + i : at + i + 1] for j in range(4)] for i in range(4)]
    scale = 1.0 / (m[0][0] * m[1][1] - m[0][1] * m[1][0])
    first = {j: (m[1][1] * m[0][j] - m[0][1] * m[1][j]) * scale for j in (2, 3)}
    second = {j: (m[0][0] * m[1][j] - m[1][0] * m[0][j]) * scale for j in (2, 3)}
    s = {(i, j): m[i][j] - (m[i][0] * first[j] + m[i][1] * second[j]) for i in (2, 3) for j in (2, 3)}
    after = 1.0 / (s[2, 2] * s[3, 3] - s[2, 3] * s[3, 2])
    ratio, last_ratio = m[1][0] / m[0][0], s[3, 2] / s[2, 2]
    for part in both:
        p = [part[block][at + i : at + i + 1] for i in range(4)]
        y0 = (m[1][1] * p[0] - m[0][1] * p[1]) * scale
        y1 = (m[0][0] * p[1] - m[1][0] * p[0]) * scale
        r2 = p[2] - (m[2][0] * y0 + m[2][1] * y1)
        r3 = p[3] - (m[3][0] * y0 + m[3][1] * y1)
        x2 = (s[3, 3] * r2 - s[2, 3] * r3) * after
        x3 = (s[2, 2] * r3 - s[3, 2] * r2) * after
        x0 = y0 - (first[2] * x2 + first[3] * x3)
        x1 = y1 - (second[2] * x2 + second[3] * x3)
        own = [p[0], p[1] - ratio * p[0], r2, r3 - last_ratio * r2]
        for i in range(block, len(wide)):
            c = [column[i - block] for column in columns]
            rest = part[i] - ((c[0] * x0 + c[1] * x1) + (c[2] * x2 + c[3] * x3))
            if i == block:
                rest = jnp.where(rows > at + 3, rest, part[i])
                for t in range(1, 4):
                    rest = jnp.where(rows == at + t, own[t], rest)
            part[i] = rest


def last_kernel(kept_ref, got_ref, right_ref, image_ref, second_ref, field_ref, residual_ref, hessenberg_ref):
    clusters = image_ref.shape[0]
    gram = kept_ref[...] + got_ref[...]
    top, folded = gram[:R], gram[R:]
    bottom = jnp.concatenate([folded[:, : 2 * R], folded[:, 2 * R :]], axis=0)
    lanes = lax.broadcasted_iota(jnp.int32, (2 * R, 4 * R), 1)
    rows = lax.broadcasted_iota(jnp.int32, (2 * R, 4 * R), 0)
    wide = jnp.zeros((R, R), f32)
    first_first, image_first = top[:, 2 * R : 3 * R], top[:, :R]
    image_image, second_first = top[:, R : 2 * R], top[:, 3 * R :]
    second_image, second_second = bottom[:, :R], bottom[:, R:]
    on_diagonal = lax.broadcasted_iota(jnp.int32, (R, R), 0) == lax.broadcasted_iota(jnp.int32, (R, R), 1)

    def shrink(x):
        trace = jnp.sum(jnp.where(on_diagonal, x, 0.0), axis=0, keepdims=True)
        return lax.rsqrt(jnp.sum(trace, axis=1, keepdims=True) / R)

    at_first, at_image, at_second = shrink(first_first), shrink(image_image), shrink(second_second)
    stretch = at_first / at_image
    first_first, image_first = first_first * at_first * at_first, image_first * at_image * at_first
    image_image, second_second = image_image * at_image * at_image, second_second * at_second * at_second
    second_image, second_first = second_image * at_second * at_image, second_first * at_second * at_first
    system = jnp.concatenate(
        [
            jnp.concatenate([image_image, second_image.T, image_first, wide], axis=1),
            jnp.concatenate([second_image, second_second, second_first, wide], axis=1),
        ],
        axis=0,
    )
    lower = jnp.concatenate(
        [
            jnp.concatenate([first_first, image_first.T, wide, wide], axis=1),
            jnp.concatenate([image_first, image_image, wide, wide], axis=1),
        ],
        axis=0,
    )
    lower = jnp.where(lanes - 2 * R == rows, 1.0, lower)
    system = jnp.where(lanes - 3 * R == rows, 1.0, system)
    late = jnp.where(lanes + R == rows, 1.0, 0.0)

    def blocks(x):
        return [x[i : i + TALL] for i in range(0, 2 * R, TALL)]

    system, lower, late = blocks(system), blocks(lower), blocks(late)
    for k in range(0, 2 * R, 4):
        eliminate(system, late, k)
        eliminate(lower, None, k)
    system, lower, late = (jnp.concatenate(x, axis=0) for x in (system, lower, late))

    def diagonal(x):
        return jnp.sum(jnp.where(lanes == rows, x, 0.0), axis=1, keepdims=True)

    lower = lower * lax.rsqrt(diagonal(lower))
    scaled = system[:, 2 * R : 3 * R] / diagonal(system)
    inverse = jnp.concatenate([system[:, 3 * R :], late[:, :R]], axis=1)
    weights = lax.dot_general(scaled, inverse, TN, precision=highest, preferred_element_type=f32)
    weights = weights * jnp.where(lanes[:R, : 2 * R] < R, at_image, at_second) / at_first
    inverse_zero = lower[:R, 2 * R : 3 * R]
    hessenberg_ref[:, :R] = stretch * exact_nt(inverse_zero, lower[:R, R : 2 * R])
    hessenberg_ref[:, R:] = stretch * lax.dot_general(
        lower[R:, R : 2 * R], inverse_zero, NT, precision=highest, preferred_element_type=f32
    )
    none = jnp.zeros((R, R), f32)
    mix = jnp.concatenate(
        [jnp.concatenate([weights, none], axis=1), jnp.concatenate([none, weights], axis=1)], axis=0
    )
    mix_high = mix.astype(bf16)
    mix_both = jnp.concatenate([mix_high, (mix - mix_high.astype(f32)).astype(bf16)], axis=0)
    for c in range(clusters):
        here = slice(c * PANEL, (c + 1) * PANEL)
        right = right_ref[:, here]
        stacked = jnp.concatenate([right, image_ref[c], second_ref[c]], axis=0)
        high = stacked.astype(bf16)
        low = (stacked - high.astype(f32)).astype(bf16)
        both = dot(mix_both, high)
        value = both[: 2 * R] + both[2 * R :] + dot(mix_high, low)
        field_ref[:, here] = value[:R]
        residual_ref[:, here] = right - value[R:]


def body(right_side, near_pairs, near_count, near_blocks, far_pairs, coupling, cluster_basis, cluster_slot):
    devices = lax.axis_size("leaf")
    order, place = rounds(devices), places(devices)
    clusters = cluster_basis.shape[0]
    me = lax.axis_index("leaf").astype(jnp.int32).reshape(1)
    basis = cluster_basis.reshape(clusters * K, PANEL)
    sds = jax.ShapeDtypeStruct

    def across(x, b):
        return lax.ppermute(x, "leaf", [(i, i ^ b) for i in range(devices)])

    def shift(x, by):
        return lax.ppermute(x, "leaf", [(i, i + by) for i in range(devices) if 0 <= i + by < devices])

    panels = sds((clusters, R, PANEL), f32)
    narrow = sds((clusters, R, PANEL), bf16)
    split = sds((clusters, 2 * R, PANEL), bf16)
    rank_wide = sds((R, clusters * K), f32)
    rank_split = sds((2 * R, clusters * K), bf16)
    half = devices // 2
    merged_out = sds((devices, clusters * K, clusters * K), bf16)
    payload_out = sds((1 + half, R, clusters * K), bf16)
    kept_out = sds((half, R, clusters * K), f32)
    barrier = lax.optimization_barrier
    near_spaces = [SMEM, SMEM, VMEM, VMEM]

    def in_hbm(x):
        return pltpu.with_memory_space_constraint(x, pltpu.HBM)

    near_pairs, near_blocks, field, right_proj, coupled, payload = call(
        open_kernel,
        (sds(near_pairs.shape, jnp.int32), sds(near_blocks.shape, bf16), split, rank_wide,
         sds((2 * devices, clusters * K, clusters * K), bf16),
         sds((1 + devices, R, clusters * K), bf16)),
        (me, in_hbm(far_pairs), in_hbm(cluster_slot), in_hbm(coupling), in_hbm(right_side), in_hbm(basis),
         in_hbm(near_pairs), in_hbm(near_blocks)),
        [SMEM] + [pltpu.HBM] * 7,
        [
            pltpu.SMEM(far_pairs.shape, jnp.int32),
            pltpu.SMEM(cluster_slot.shape, jnp.int32),
            pltpu.SMEM((devices,), jnp.int32),
            pltpu.VMEM(coupling.shape, bf16),
            pltpu.VMEM(right_side.shape, f32),
            pltpu.VMEM(basis.shape, bf16),
            pltpu.VMEM(((coupling.shape[0] + 8) * (K + 1), 128), f32),
            pltpu.SemaphoreType.DMA((7,)),
        ],
        placed=[SMEM] + [VMEM] * 5,
    )

    right_field = field

    def exchange(make_field, beside, keep, payload, merged=None):
        first = merged is None
        for t, b in enumerate(order):
            if t > 0:
                held, half = gathered.shape[0], sums.shape[0] // 2
                payload = jnp.concatenate([gathered, sums[half:].astype(bf16)], axis=0)
                sums = sums[:half]
            else:
                gathered, held = payload[:1], 1
            if t == 2:
                payload, own = barrier((payload, own))
            if t == 3:
                payload, made = barrier((payload, made))
            got = across(payload, b)
            if t == 0:
                sums, cross, corner = keep(payload)
                image, field, got = make_field(got)
                after = shift(field, -1)
                own, following = call(
                    near_cols_kernel, (panels, narrow), (near_pairs, near_count, near_blocks, field), near_spaces,
                    [pltpu.VMEM((2 * clusters + 1, R, PANEL), f32)], moved=12 << 20,
                )
                back = shift(following, 1)
            if t == 1:
                made, got = beside(field, corner, got)
            if t == len(order) - 2:
                after, got = barrier((after, got))
            got_gathered, got_sums = got[:held], got[held:]
            if t < len(order) - 1:
                gathered = jnp.concatenate([gathered, got_gathered], axis=0)
                for piece in range(0, got_sums.shape[0], sums.shape[0]):
                    sums = sums + got_sums[piece : piece + sums.shape[0]].astype(f32)
        kernel, ins, outs = rows_one_kernel, (near_blocks, field, after, own, back, basis), (panels, rank_wide)
        if not first:
            kernel, ins, outs = rows_two_kernel, ins + (right_field,), outs + (sds((R, 4 * R), f32),)
        near, near_proj, *gram = call(
            kernel, outs, (near_pairs, near_count) + ins, [SMEM] * 2 + [VMEM] * len(ins),
            [pltpu.VMEM((2 * clusters, 2 * R, PANEL), bf16), pltpu.VMEM((clusters + 1, R, PANEL), f32)],
            moved=12 << 20,
        )
        merged = made if first else merged
        return image, near, made, gram, cross, corner, (merged[0], gathered, got_gathered, sums, got_sums, near_proj, cross)

    def first_field(got):
        ready, got = barrier((field, got))
        return right_side, ready, got

    def keep_one(payload):
        return call(
            keep_one_kernel, (kept_out, sds((2, clusters * K, clusters * K), bf16), sds((R, 4 * R), f32)),
            (coupled, payload, basis, right_field), [VMEM] * 4,
        )

    def merging(image, corner, got):
        ready, got = barrier((coupled, got))
        return call(merge_kernel, (merged_out, merged_out), (ready,), [VMEM]), got

    def multiplying(image, corner, got):
        ready, got = barrier((image, got))
        return call(gram_one_kernel, sds((R, 4 * R), f32), (corner, right_field, ready), [VMEM] * 3), got

    unused, near, merged, unused, cross, corner, parts = exchange(first_field, merging, keep_one, payload)
    far, image_proj, payload = call(
        functools.partial(turn_kernel, place), (rank_split, rank_wide, payload_out), parts + (merged[1],), [VMEM] * 8
    )

    def second_field(got):
        ready, got = barrier((far, got))
        return *call(image_kernel, (panels, split), (near, ready, basis), [VMEM] * 3), got

    def keep_two(payload):
        return call(keep_two_kernel, kept_out, (merged[1], payload), [VMEM] * 2), cross, corner

    image, near_two, early, gram, unused, unused, parts = exchange(
        second_field, multiplying, keep_two, payload, merged
    )
    far, gram = call(
        functools.partial(tail_kernel, place), (rank_split, sds((R + R // 2, 4 * R), f32)),
        parts + (right_proj, image_proj, early, *gram), [VMEM] * 11,
    )
    got = None
    for t, b in enumerate(order):
        if t > 0:
            gram = gram + got
        if t == 2:
            gram, second = barrier((gram, second))
        got = across(gram, b)
        if t == 0:
            far, got = barrier((far, got))
            second = call(second_kernel, panels, (near_two, far, basis), [VMEM] * 3)
    wide = sds(right_side.shape, f32)
    solution_field, residual, hessenberg = call(
        last_kernel, (wide, wide, sds((R, 2 * R), f32)), (gram, got, right_side, image, second), [VMEM] * 5
    )
    return solution_field, residual, hessenberg.T


def solution(mesh):
    in_specs = (
        P(None, ("parts", "leaf")),
        P(None, ("parts", "leaf")),
        P(("parts", "leaf")),
        P(("parts", "leaf"), None, None),
        P(None, ("parts", "leaf")),
        P(("parts", "leaf"), None),
        P(("parts", "leaf"), None, None),
        P("parts"),
    )
    out_specs = (P(None, ("parts", "leaf")), P(None, ("parts", "leaf")), P("parts", None))
    return jax.shard_map(body, mesh=mesh, in_specs=in_specs, out_specs=out_specs, check_vma=False)
```

```python
import functools

import jax
import jax.numpy as jnp
from jax import lax
from jax.experimental import pallas as pl
from jax.experimental.pallas import tpu as pltpu
from jax.sharding import PartitionSpec as P

PANEL = 256
R = 32
K = 32
GROUP = 32
highest = lax.Precision.HIGHEST
VMEM = pltpu.VMEM
SMEM = pltpu.SMEM
TN = (((0,), (0,)), ((), ()))
NT = (((1,), (1,)), ((), ()))
f32 = jnp.float32
bf16 = jnp.bfloat16


def spec(space):
    return pl.BlockSpec(memory_space=space)


def call(kernel, outs, ins, spaces, scratch=(), limit=24, flops=10**8, moved=10**6, placed=None):
    return pl.pallas_call(
        kernel,
        out_shape=outs,
        in_specs=[spec(s) for s in spaces],
        out_specs=jax.tree.map(lambda _: spec(VMEM), outs) if placed is None else tuple(map(spec, placed)),
        scratch_shapes=list(scratch),
        compiler_params=pltpu.CompilerParams(vmem_limit_bytes=limit << 20),
        cost_estimate=pl.CostEstimate(flops=flops, bytes_accessed=moved, transcendentals=0),
    )(*ins)


def dot(x, y):
    return jnp.dot(x, y, preferred_element_type=f32)


def dot_nt(x, y):
    return lax.dot_general(x, y, NT, preferred_element_type=f32)


def exact_nt(x, y):
    return lax.dot_general(x, y, NT, precision=highest, preferred_element_type=f32)


def split_rows(x):
    high = x.astype(bf16)
    low = (x - high.astype(f32)).astype(bf16)
    return jnp.concatenate([high, low], axis=0)


def join_rows(x):
    return x[:R] + x[R:]


def split_nt(x, high, low):
    return join_rows(dot_nt(x, high)) + dot_nt(x[:R], low)


def stack(*halves):
    zero = jnp.zeros((R, halves[0 if halves[0] is not None else 2].shape[1]), bf16)
    return (
        jnp.concatenate([zero if x is None else x[:R] for x in halves], axis=0),
        jnp.concatenate([zero if x is None else x[R:] for x in halves], axis=0),
    )


def lane_group(shape):
    return lax.broadcasted_iota(jnp.int32, shape, 1) // K


def project(fields, basis):
    clusters = fields.shape[0] // (2 * R)
    all_pairs = dot_nt(fields, basis)
    group = lane_group((2 * R, clusters * K))
    total = jnp.zeros((2 * R, clusters * K), f32)
    for c in range(clusters):
        total = total + jnp.where(group == c, all_pairs[c * 2 * R : (c + 1) * 2 * R], 0.0)
    return join_rows(total)


def expand(sums, basis):
    group = lane_group(sums.shape)
    zero = jnp.zeros_like(sums)
    spread = [jnp.where(group == c, sums, zero) for c in range(sums.shape[1] // K)]
    return dot(jnp.concatenate(spread, axis=0), basis)


def rounds(devices):
    bits = devices.bit_length() - 1
    return [1] + [(1 << b) | 1 for b in [bits - 1, 1] + list(range(bits - 2, 1, -1))]


def places(devices):
    steps = rounds(devices)
    place = [0] * devices
    for p in range(devices):
        apart = 0
        for t, step in enumerate(steps):
            if (p >> (len(steps) - 1 - t)) & 1:
                apart ^= step
        place[apart] = p
    return place


def couple(me, pairs_ref, slots_ref, table_ref, wide_ref, out_ref):
    clusters = out_ref.shape[2] // K
    devices = out_ref.shape[0] // 2
    pairs = pairs_ref.shape[1]
    group = lane_group((K, clusters * K))
    shift = clusters.bit_length() - 1
    assert clusters == 1 << shift
    steps = rounds(devices)
    for home in range(devices):
        apart = home ^ me
        parity = apart
        for b in range(1, len(steps)):
            parity = parity ^ (apart >> b)
        place = (parity & 1) << (len(steps) - 1)
        for t, step in enumerate(steps[1:], 1):
            bit = step.bit_length() - 1
            place = place + (((apart >> bit) & 1) << (len(steps) - 1 - t))
        table_ref[home] = place

    def one(f):
        first = slots_ref[pairs_ref[0, f]]
        second = slots_ref[pairs_ref[1, f]]
        first_home, second_home = first >> shift, second >> shift
        own = first_home == me
        where = jnp.where(own, devices, 0) + table_ref[jnp.where(own, second_home, first_home)]
        block = wide_ref[pl.ds(f, K, stride=pairs + 8), :]
        block = jnp.concatenate([block] * (clusters * K // block.shape[1]), axis=1)
        block = jnp.where(group == (second & (clusters - 1)), block, 0.0).astype(bf16)
        here = pl.ds(pl.multiple_of((first & (clusters - 1)) * K, K), K)
        out_ref[where, here, :] = out_ref[where, here, :] + block

    def some(step, carry):
        for u in range(16):
            one(step * 16 + u)
        return carry

    lax.fori_loop(0, pairs // 16, some, 0)


def open_kernel(me_ref, pairs_hbm, slots_hbm, coupling_hbm, right_hbm, basis_hbm, near_hbm, blocks_hbm,
                near_pairs_ref, blocks_ref, field_ref, near_proj_ref, coupled_ref, payload_ref,
                pairs_ref, slots_ref, table_ref, coupling_ref, right_ref, basis_ref, wide_ref, sems):
    clusters = field_ref.shape[0]
    moves = [(coupling_hbm, coupling_ref), (basis_hbm, basis_ref), (right_hbm, right_ref),
             (pairs_hbm, pairs_ref), (slots_hbm, slots_ref), (near_hbm, near_pairs_ref), (blocks_hbm, blocks_ref)]
    copies = [pltpu.make_async_copy(*move, sems.at[i]) for i, move in enumerate(moves)]
    for copy in copies:
        copy.start()
    coupled_ref[...] = jnp.zeros_like(coupled_ref)
    copies[0].wait()
    pairs = coupling_ref.shape[0]
    lanes_held = 128
    rows = lax.broadcasted_iota(jnp.int32, (lanes_held, lanes_held), 0)
    lanes = lax.broadcasted_iota(jnp.int32, (lanes_held, lanes_held), 1)
    tiles = coupling_ref.shape[1] // lanes_held
    flat = jnp.concatenate(
        [coupling_ref[:, t * lanes_held : (t + 1) * lanes_held] for t in range(tiles)], axis=0
    )
    each = lanes_held // K
    for u in range(each):
        spread = jnp.where((lanes % K == rows % K) & (rows // K == u), 1.0, 0.0).astype(bf16)
        value = dot(flat, spread)
        for t in range(tiles):
            begin = (t * each + u) * (pairs + 8)
            wide_ref[begin : begin + pairs] = value[t * pairs : (t + 1) * pairs]
    copies[1].wait()
    basis = basis_ref[...]
    copies[2].wait()
    for c in range(clusters):
        field_ref[c] = split_rows(right_ref[:, c * PANEL : (c + 1) * PANEL])
    proj = project(field_ref[...].reshape(clusters * 2 * R, PANEL), basis)
    near_proj_ref[...] = proj
    copies[3].wait()
    copies[4].wait()
    copies[5].wait()
    couple(me_ref[0], pairs_ref, slots_ref, table_ref, wide_ref, coupled_ref)
    proj = proj.astype(bf16)
    devices = coupled_ref.shape[0] // 2
    send(
        lambda d: dot(proj, coupled_ref[devices + d]) + dot_nt(proj, coupled_ref[d]),
        payload_ref, proj, devices, True,
    )
    copies[6].wait()


def send(products, payload_ref, proj, devices, both):
    payload_ref[0] = proj
    half = devices // 2
    for d in range(half, devices):
        value = products(d)
        high = value.astype(bf16)
        payload_ref[1 + d - half] = high
        if both:
            payload_ref[1 + d] = (value - high.astype(f32)).astype(bf16)


def keep_one_kernel(coupled_ref, payload_ref, basis_ref, field_ref, kept_ref, cross_ref, corner_ref):
    devices = coupled_ref.shape[0] // 2
    proj = payload_ref[0]
    for d in range(devices // 2):
        kept_ref[d] = dot(proj, coupled_ref[devices + d]) + dot_nt(proj, coupled_ref[d])
    basis = basis_ref[...]
    cross = dot_nt(basis, basis)
    same = lane_group(cross.shape) == lax.broadcasted_iota(jnp.int32, cross.shape, 0) // K
    cross = jnp.where(same, cross, 0.0)
    high = cross.astype(bf16)
    cross_ref[0] = high
    cross_ref[1] = (cross - high.astype(f32)).astype(bf16)
    corner = jnp.zeros((R, 4 * R), f32)
    for c in range(field_ref.shape[0]):
        right = field_ref[c]
        corner = corner + split_nt(right, *stack(None, None, right, None))
    corner_ref[...] = corner


def keep_two_kernel(turned_ref, payload_ref, kept_ref):
    proj = payload_ref[0]
    for d in range(kept_ref.shape[0]):
        kept_ref[d] = dot(proj, turned_ref[d])


def near_loop(count_ref, one, many=GROUP):
    def group(g, carry):
        for u in range(many):
            one(g * many + u)
        return carry

    lax.fori_loop(0, (count_ref[0] + many - 1) // many, group, 0)


def near_cols_kernel(pairs_ref, count_ref, blocks_ref, field_ref, own_ref, next_ref, total):
    clusters = field_ref.shape[0]
    total[...] = jnp.zeros_like(total)

    def one(s):
        i = pairs_ref[0, s]
        j = jnp.where(s < count_ref[0], pairs_ref[1, s], 2 * clusters)
        total[j] = total[j] + join_rows(dot(field_ref[i], blocks_ref[s]))

    near_loop(count_ref, one)
    own_ref[...] = total[:clusters]
    next_ref[...] = total[clusters : 2 * clusters].astype(bf16)


def near_rows(pairs_ref, count_ref, blocks_ref, field_ref, after_ref, begun_ref, back_ref, basis_ref,
                     out_ref, proj_ref, window, total):
    clusters = field_ref.shape[0]
    window[:clusters] = field_ref[...]
    window[clusters:] = after_ref[...]
    total[:clusters] = begun_ref[...] + back_ref[...].astype(f32)
    total[clusters] = jnp.zeros_like(total[clusters])

    def one(s):
        i = jnp.where(s < count_ref[0], pairs_ref[0, s], clusters)
        j = pairs_ref[1, s]
        total[i] = total[i] + join_rows(dot_nt(window[j], blocks_ref[s]))

    near_loop(count_ref, one, blocks_ref.shape[0])
    near = total[:clusters]
    out_ref[...] = near
    split = jnp.concatenate([split_rows(near[c]) for c in range(clusters)], axis=0)
    proj_ref[...] = project(split, basis_ref[...])
    return split


def rows_one_kernel(*refs):
    near_rows(*refs)


def rows_two_kernel(pairs_ref, count_ref, blocks_ref, field_ref, after_ref, begun_ref, back_ref, basis_ref,
                    right_ref, out_ref, proj_ref, gram_ref, window, total):
    split = near_rows(pairs_ref, count_ref, blocks_ref, field_ref, after_ref, begun_ref, back_ref, basis_ref,
                      out_ref, proj_ref, window, total)
    gram = jnp.zeros((R, 4 * R), f32)
    for c in range(field_ref.shape[0]):
        near = split[c * 2 * R : (c + 1) * 2 * R]
        gram = gram + split_nt(near, *stack(right_ref[c], field_ref[c], near, None))
    gram_ref[...] = gram


def merge_kernel(coupled_ref, out_ref, turned_ref):
    devices = out_ref.shape[0]
    for d in range(devices):
        near, away = coupled_ref[d], coupled_ref[devices + d]
        out_ref[d] = near + away.T
        turned_ref[d] = away + near.T


def far_sums(place, merged_ref, low_ref, high_ref, kept_ref, got_ref):
    devices = merged_ref.shape[0]
    sums = kept_ref[0]
    for piece in range(got_ref.shape[0]):
        sums = sums + got_ref[piece].astype(f32)
    steps = rounds(devices)
    for g in range(devices):
        proj = low_ref[g] if g < devices // 2 else high_ref[g - devices // 2]
        apart = functools.reduce(lambda x, y: x ^ y, [step for t, step in enumerate(steps) if (g >> t) & 1], 0)
        sums = sums + dot(proj, merged_ref[place[apart]])
    return split_rows(sums)


def across_clusters(sums, cross_ref):
    return join_rows(dot(sums, cross_ref[0])) + dot(sums[:R], cross_ref[1])


def turn_kernel(place, merged_ref, low_ref, high_ref, kept_ref, got_ref, near_proj_ref, cross_ref,
                turned_ref, sums_ref, proj_ref, payload_ref):
    sums = far_sums(place, merged_ref, low_ref, high_ref, kept_ref, got_ref)
    sums_ref[...] = sums
    proj = near_proj_ref[...] + across_clusters(sums, cross_ref)
    proj_ref[...] = proj
    proj = proj.astype(bf16)
    send(lambda d: dot(proj, turned_ref[d]), payload_ref, proj, turned_ref.shape[0], False)


def image_kernel(near_ref, sums_ref, basis_ref, image_ref, field_ref):
    far = expand(sums_ref[...], basis_ref[...])
    for c in range(near_ref.shape[0]):
        image = near_ref[c] + join_rows(far[c * 2 * R : (c + 1) * 2 * R])
        image_ref[c] = image
        field_ref[c] = split_rows(image)


def second_kernel(near_ref, sums_ref, basis_ref, image_ref):
    far = expand(sums_ref[...], basis_ref[...])
    for c in range(near_ref.shape[0]):
        image_ref[c] = near_ref[c] + join_rows(far[c * 2 * R : (c + 1) * 2 * R])


def gram_one_kernel(corner_ref, right_ref, image_ref, gram_ref):
    gram = corner_ref[...]
    for c in range(image_ref.shape[0]):
        gram = gram + split_nt(image_ref[c], *stack(right_ref[c], image_ref[c], None, None))
    gram_ref[...] = gram


def tail_kernel(place, merged_ref, low_ref, high_ref, kept_ref, got_ref, near_proj_ref, cross_ref,
                right_proj_ref, image_proj_ref, early_ref, gram_ref, sums_ref, out_ref):
    sums = far_sums(place, merged_ref, low_ref, high_ref, kept_ref, got_ref)
    sums_ref[...] = sums
    half = near_proj_ref[...] + 0.5 * across_clusters(sums, cross_ref)
    known = jnp.concatenate([right_proj_ref[...], image_proj_ref[...], half, jnp.zeros_like(half)], axis=0)
    high = known.astype(bf16)
    added = split_nt(sums, high, (known - high.astype(f32)).astype(bf16))
    mirror = jnp.where(lane_group(added.shape) == 2, jnp.concatenate([added[:, 2 * R : 3 * R].T] * 4, axis=1), 0.0)
    late = gram_ref[...] + added + mirror
    lanes = lane_group(late.shape)
    out_ref[:R] = jnp.where(lanes == 3, pltpu.roll(late, 3 * R, 1), early_ref[...])
    rest = pltpu.roll(late, 3 * R, 1)
    half_rows = R // 2
    out_ref[R:] = jnp.where(lanes[:half_rows] < 2, rest[:half_rows], pltpu.roll(rest[half_rows:], 2 * R, 1))


TALL = 8


def lane(x, k):
    return jnp.broadcast_to(x[:, k : k + 1], x.shape)


def eliminate(wide, late, k):
    block, at = k // TALL, k % TALL
    rows = lax.broadcasted_iota(jnp.int32, wide[block].shape, 0)
    both = [wide] if late is None or block < len(wide) // 2 else [wide, late]
    columns = [[lane(x, k + j) for x in wide[block:]] for j in range(4)]
    m = [[columns[j][0][at + i : at + i + 1] for j in range(4)] for i in range(4)]
    scale = 1.0 / (m[0][0] * m[1][1] - m[0][1] * m[1][0])
    first = {j: (m[1][1] * m[0][j] - m[0][1] * m[1][j]) * scale for j in (2, 3)}
    second = {j: (m[0][0] * m[1][j] - m[1][0] * m[0][j]) * scale for j in (2, 3)}
    s = {(i, j): m[i][j] - (m[i][0] * first[j] + m[i][1] * second[j]) for i in (2, 3) for j in (2, 3)}
    after = 1.0 / (s[2, 2] * s[3, 3] - s[2, 3] * s[3, 2])
    ratio, last_ratio = m[1][0] / m[0][0], s[3, 2] / s[2, 2]
    for part in both:
        p = [part[block][at + i : at + i + 1] for i in range(4)]
        y0 = (m[1][1] * p[0] - m[0][1] * p[1]) * scale
        y1 = (m[0][0] * p[1] - m[1][0] * p[0]) * scale
        r2 = p[2] - (m[2][0] * y0 + m[2][1] * y1)
        r3 = p[3] - (m[3][0] * y0 + m[3][1] * y1)
        x2 = (s[3, 3] * r2 - s[2, 3] * r3) * after
        x3 = (s[2, 2] * r3 - s[3, 2] * r2) * after
        x0 = y0 - (first[2] * x2 + first[3] * x3)
        x1 = y1 - (second[2] * x2 + second[3] * x3)
        own = [p[0], p[1] - ratio * p[0], r2, r3 - last_ratio * r2]
        for i in range(block, len(wide)):
            c = [column[i - block] for column in columns]
            rest = part[i] - ((c[0] * x0 + c[1] * x1) + (c[2] * x2 + c[3] * x3))
            if i == block:
                rest = jnp.where(rows > at + 3, rest, part[i])
                for t in range(1, 4):
                    rest = jnp.where(rows == at + t, own[t], rest)
            part[i] = rest


def last_kernel(kept_ref, got_ref, right_ref, image_ref, second_ref, field_ref, residual_ref, hessenberg_ref):
    clusters = image_ref.shape[0]
    gram = kept_ref[...] + got_ref[...]
    top, folded = gram[:R], gram[R:]
    bottom = jnp.concatenate([folded[:, : 2 * R], folded[:, 2 * R :]], axis=0)
    lanes = lax.broadcasted_iota(jnp.int32, (2 * R, 4 * R), 1)
    rows = lax.broadcasted_iota(jnp.int32, (2 * R, 4 * R), 0)
    wide = jnp.zeros((R, R), f32)
    first_first, image_first = top[:, 2 * R : 3 * R], top[:, :R]
    image_image, second_first = top[:, R : 2 * R], top[:, 3 * R :]
    second_image, second_second = bottom[:, :R], bottom[:, R:]
    on_diagonal = lax.broadcasted_iota(jnp.int32, (R, R), 0) == lax.broadcasted_iota(jnp.int32, (R, R), 1)

    def shrink(x):
        trace = jnp.sum(jnp.where(on_diagonal, x, 0.0), axis=0, keepdims=True)
        return lax.rsqrt(jnp.sum(trace, axis=1, keepdims=True) / R)

    at_first, at_image, at_second = shrink(first_first), shrink(image_image), shrink(second_second)
    stretch = at_first / at_image
    first_first, image_first = first_first * at_first * at_first, image_first * at_image * at_first
    image_image, second_second = image_image * at_image * at_image, second_second * at_second * at_second
    second_image, second_first = second_image * at_second * at_image, second_first * at_second * at_first
    system = jnp.concatenate(
        [
            jnp.concatenate([image_image, second_image.T, image_first, wide], axis=1),
            jnp.concatenate([second_image, second_second, second_first, wide], axis=1),
        ],
        axis=0,
    )
    lower = jnp.concatenate(
        [
            jnp.concatenate([first_first, image_first.T, wide, wide], axis=1),
            jnp.concatenate([image_first, image_image, wide, wide], axis=1),
        ],
        axis=0,
    )
    lower = jnp.where(lanes - 2 * R == rows, 1.0, lower)
    system = jnp.where(lanes - 3 * R == rows, 1.0, system)
    late = jnp.where(lanes + R == rows, 1.0, 0.0)

    def blocks(x):
        return [x[i : i + TALL] for i in range(0, 2 * R, TALL)]

    system, lower, late = blocks(system), blocks(lower), blocks(late)
    for k in range(0, 2 * R, 4):
        eliminate(system, late, k)
        eliminate(lower, None, k)
    system, lower, late = (jnp.concatenate(x, axis=0) for x in (system, lower, late))

    def diagonal(x):
        return jnp.sum(jnp.where(lanes == rows, x, 0.0), axis=1, keepdims=True)

    lower = lower * lax.rsqrt(diagonal(lower))
    scaled = system[:, 2 * R : 3 * R] / diagonal(system)
    inverse = jnp.concatenate([system[:, 3 * R :], late[:, :R]], axis=1)
    weights = lax.dot_general(scaled, inverse, TN, precision=highest, preferred_element_type=f32)
    weights = weights * jnp.where(lanes[:R, : 2 * R] < R, at_image, at_second) / at_first
    inverse_zero = lower[:R, 2 * R : 3 * R]
    hessenberg_ref[:, :R] = stretch * exact_nt(inverse_zero, lower[:R, R : 2 * R])
    hessenberg_ref[:, R:] = stretch * lax.dot_general(
        lower[R:, R : 2 * R], inverse_zero, NT, precision=highest, preferred_element_type=f32
    )
    none = jnp.zeros((R, R), f32)
    mix = jnp.concatenate(
        [jnp.concatenate([weights, none], axis=1), jnp.concatenate([none, weights], axis=1)], axis=0
    )
    mix_high = mix.astype(bf16)
    mix_both = jnp.concatenate([mix_high, (mix - mix_high.astype(f32)).astype(bf16)], axis=0)
    for c in range(clusters):
        here = slice(c * PANEL, (c + 1) * PANEL)
        right = right_ref[:, here]
        stacked = jnp.concatenate([right, image_ref[c], second_ref[c]], axis=0)
        high = stacked.astype(bf16)
        low = (stacked - high.astype(f32)).astype(bf16)
        both = dot(mix_both, high)
        value = both[: 2 * R] + both[2 * R :] + dot(mix_high, low)
        field_ref[:, here] = value[:R]
        residual_ref[:, here] = right - value[R:]


def body(right_side, near_pairs, near_count, near_blocks, far_pairs, coupling, cluster_basis, cluster_slot):
    devices = lax.axis_size("leaf")
    order, place = rounds(devices), places(devices)
    clusters = cluster_basis.shape[0]
    me = lax.axis_index("leaf").astype(jnp.int32).reshape(1)
    basis = cluster_basis.reshape(clusters * K, PANEL)
    sds = jax.ShapeDtypeStruct

    def across(x, b):
        return lax.ppermute(x, "leaf", [(i, i ^ b) for i in range(devices)])

    def shift(x, by):
        return lax.ppermute(x, "leaf", [(i, i + by) for i in range(devices) if 0 <= i + by < devices])

    panels = sds((clusters, R, PANEL), f32)
    narrow = sds((clusters, R, PANEL), bf16)
    split = sds((clusters, 2 * R, PANEL), bf16)
    rank_wide = sds((R, clusters * K), f32)
    rank_split = sds((2 * R, clusters * K), bf16)
    half = devices // 2
    merged_out = sds((devices, clusters * K, clusters * K), bf16)
    payload_out = sds((1 + half, R, clusters * K), bf16)
    kept_out = sds((half, R, clusters * K), f32)
    barrier = lax.optimization_barrier
    near_spaces = [SMEM, SMEM, VMEM, VMEM]

    def in_hbm(x):
        return pltpu.with_memory_space_constraint(x, pltpu.HBM)

    near_pairs, near_blocks, field, right_proj, coupled, payload = call(
        open_kernel,
        (sds(near_pairs.shape, jnp.int32), sds(near_blocks.shape, bf16), split, rank_wide,
         sds((2 * devices, clusters * K, clusters * K), bf16),
         sds((1 + devices, R, clusters * K), bf16)),
        (me, in_hbm(far_pairs), in_hbm(cluster_slot), in_hbm(coupling), in_hbm(right_side), in_hbm(basis),
         in_hbm(near_pairs), in_hbm(near_blocks)),
        [SMEM] + [pltpu.HBM] * 7,
        [
            pltpu.SMEM(far_pairs.shape, jnp.int32),
            pltpu.SMEM(cluster_slot.shape, jnp.int32),
            pltpu.SMEM((devices,), jnp.int32),
            pltpu.VMEM(coupling.shape, bf16),
            pltpu.VMEM(right_side.shape, f32),
            pltpu.VMEM(basis.shape, bf16),
            pltpu.VMEM(((coupling.shape[0] + 8) * (K + 1), 128), f32),
            pltpu.SemaphoreType.DMA((7,)),
        ],
        placed=[SMEM] + [VMEM] * 5,
    )

    right_field = field

    def exchange(make_field, beside, keep, payload, merged=None):
        first = merged is None
        for t, b in enumerate(order):
            if t > 0:
                held, half = gathered.shape[0], sums.shape[0] // 2
                payload = jnp.concatenate([gathered, sums[half:].astype(bf16)], axis=0)
                sums = sums[:half]
            else:
                gathered, held = payload[:1], 1
            if t == 2:
                payload, own = barrier((payload, own))
            if t == 3:
                payload, made = barrier((payload, made))
            got = across(payload, b)
            if t == 0:
                sums, cross, corner = keep(payload)
                image, field, got = make_field(got)
                after = shift(field, -1)
                own, following = call(
                    near_cols_kernel, (panels, narrow), (near_pairs, near_count, near_blocks, field), near_spaces,
                    [pltpu.VMEM((2 * clusters + 1, R, PANEL), f32)], moved=12 << 20,
                )
                back = shift(following, 1)
            if t == 1:
                made, got = beside(field, corner, got)
            if t == len(order) - 2:
                after, got = barrier((after, got))
            got_gathered, got_sums = got[:held], got[held:]
            if t < len(order) - 1:
                gathered = jnp.concatenate([gathered, got_gathered], axis=0)
                for piece in range(0, got_sums.shape[0], sums.shape[0]):
                    sums = sums + got_sums[piece : piece + sums.shape[0]].astype(f32)
        kernel, ins, outs = rows_one_kernel, (near_blocks, field, after, own, back, basis), (panels, rank_wide)
        if not first:
            kernel, ins, outs = rows_two_kernel, ins + (right_field,), outs + (sds((R, 4 * R), f32),)
        near, near_proj, *gram = call(
            kernel, outs, (near_pairs, near_count) + ins, [SMEM] * 2 + [VMEM] * len(ins),
            [pltpu.VMEM((2 * clusters, 2 * R, PANEL), bf16), pltpu.VMEM((clusters + 1, R, PANEL), f32)],
            moved=12 << 20,
        )
        merged = made if first else merged
        return image, near, made, gram, cross, corner, (merged[0], gathered, got_gathered, sums, got_sums, near_proj, cross)

    def first_field(got):
        ready, got = barrier((field, got))
        return right_side, ready, got

    def keep_one(payload):
        return call(
            keep_one_kernel, (kept_out, sds((2, clusters * K, clusters * K), bf16), sds((R, 4 * R), f32)),
            (coupled, payload, basis, right_field), [VMEM] * 4,
        )

    def merging(image, corner, got):
        ready, got = barrier((coupled, got))
        return call(merge_kernel, (merged_out, merged_out), (ready,), [VMEM]), got

    def multiplying(image, corner, got):
        ready, got = barrier((image, got))
        return call(gram_one_kernel, sds((R, 4 * R), f32), (corner, right_field, ready), [VMEM] * 3), got

    unused, near, merged, unused, cross, corner, parts = exchange(first_field, merging, keep_one, payload)
    far, image_proj, payload = call(
        functools.partial(turn_kernel, place), (rank_split, rank_wide, payload_out), parts + (merged[1],), [VMEM] * 8
    )

    def second_field(got):
        ready, got = barrier((far, got))
        return *call(image_kernel, (panels, split), (near, ready, basis), [VMEM] * 3), got

    def keep_two(payload):
        return call(keep_two_kernel, kept_out, (merged[1], payload), [VMEM] * 2), cross, corner

    image, near_two, early, gram, unused, unused, parts = exchange(
        second_field, multiplying, keep_two, payload, merged
    )
    far, gram = call(
        functools.partial(tail_kernel, place), (rank_split, sds((R + R // 2, 4 * R), f32)),
        parts + (right_proj, image_proj, early, *gram), [VMEM] * 11,
    )
    got = None
    for t, b in enumerate(order):
        if t > 0:
            gram = gram + got
        if t == 2:
            gram, second = barrier((gram, second))
        got = across(gram, b)
        if t == 0:
            far, got = barrier((far, got))
            second = call(second_kernel, panels, (near_two, far, basis), [VMEM] * 3)
    wide = sds(right_side.shape, f32)
    solution_field, residual, hessenberg = call(
        last_kernel, (wide, wide, sds((R, 2 * R), f32)), (gram, got, right_side, image, second), [VMEM] * 5
    )
    return solution_field, residual, hessenberg.T


def solution(mesh):
    in_specs = (
        P(None, ("parts", "leaf")),
        P(None, ("parts", "leaf")),
        P(("parts", "leaf")),
        P(("parts", "leaf"), None, None),
        P(None, ("parts", "leaf")),
        P(("parts", "leaf"), None),
        P(("parts", "leaf"), None, None),
        P("parts"),
    )
    out_specs = (P(None, ("parts", "leaf")), P(None, ("parts", "leaf")), P("parts", None))
    return jax.shard_map(body, mesh=mesh, in_specs=in_specs, out_specs=out_specs, check_vma=False)
```

```python
import functools

import jax
import jax.numpy as jnp
from jax import lax
from jax.experimental import pallas as pl
from jax.experimental.pallas import tpu as pltpu
from jax.sharding import PartitionSpec as P

PANEL = 256
R = 32
K = 32
GROUP = 32
highest = lax.Precision.HIGHEST
VMEM = pltpu.VMEM
SMEM = pltpu.SMEM
TN = (((0,), (0,)), ((), ()))
NT = (((1,), (1,)), ((), ()))
f32 = jnp.float32
bf16 = jnp.bfloat16


def spec(space):
    return pl.BlockSpec(memory_space=space)


def call(kernel, outs, ins, spaces, scratch=(), limit=24, flops=10**8, moved=10**6, placed=None):
    return pl.pallas_call(
        kernel,
        out_shape=outs,
        in_specs=[spec(s) for s in spaces],
        out_specs=jax.tree.map(lambda _: spec(VMEM), outs) if placed is None else tuple(map(spec, placed)),
        scratch_shapes=list(scratch),
        compiler_params=pltpu.CompilerParams(vmem_limit_bytes=limit << 20),
        cost_estimate=pl.CostEstimate(flops=flops, bytes_accessed=moved, transcendentals=0),
    )(*ins)


def dot(x, y):
    return jnp.dot(x, y, preferred_element_type=f32)


def dot_nt(x, y):
    return lax.dot_general(x, y, NT, preferred_element_type=f32)


def exact_nt(x, y):
    return lax.dot_general(x, y, NT, precision=highest, preferred_element_type=f32)


def split_rows(x):
    high = x.astype(bf16)
    low = (x - high.astype(f32)).astype(bf16)
    return jnp.concatenate([high, low], axis=0)


def join_rows(x):
    return x[:R] + x[R:]


def split_nt(x, high, low):
    return join_rows(dot_nt(x, high)) + dot_nt(x[:R], low)


def stack(*halves):
    zero = jnp.zeros((R, halves[0 if halves[0] is not None else 2].shape[1]), bf16)
    return (
        jnp.concatenate([zero if x is None else x[:R] for x in halves], axis=0),
        jnp.concatenate([zero if x is None else x[R:] for x in halves], axis=0),
    )


def lane_group(shape):
    return lax.broadcasted_iota(jnp.int32, shape, 1) // K


def project(fields, basis):
    clusters = fields.shape[0] // (2 * R)
    all_pairs = dot_nt(fields, basis)
    group = lane_group((2 * R, clusters * K))
    total = jnp.zeros((2 * R, clusters * K), f32)
    for c in range(clusters):
        total = total + jnp.where(group == c, all_pairs[c * 2 * R : (c + 1) * 2 * R], 0.0)
    return join_rows(total)


def expand(sums, basis):
    group = lane_group(sums.shape)
    zero = jnp.zeros_like(sums)
    spread = [jnp.where(group == c, sums, zero) for c in range(sums.shape[1] // K)]
    return dot(jnp.concatenate(spread, axis=0), basis)


def rounds(devices):
    bits = devices.bit_length() - 1
    return [1] + [(1 << b) | 1 for b in [bits - 1, 1] + list(range(bits - 2, 1, -1))]


def places(devices):
    steps = rounds(devices)
    place = [0] * devices
    for p in range(devices):
        apart = 0
        for t, step in enumerate(steps):
            if (p >> (len(steps) - 1 - t)) & 1:
                apart ^= step
        place[apart] = p
    return place


def couple(me, pairs_ref, slots_ref, table_ref, wide_ref, out_ref):
    clusters = out_ref.shape[2] // K
    devices = out_ref.shape[0] // 2
    pairs = pairs_ref.shape[1]
    group = lane_group((K, clusters * K))
    shift = clusters.bit_length() - 1
    assert clusters == 1 << shift
    steps = rounds(devices)
    for home in range(devices):
        apart = home ^ me
        parity = apart
        for b in range(1, len(steps)):
            parity = parity ^ (apart >> b)
        place = (parity & 1) << (len(steps) - 1)
        for t, step in enumerate(steps[1:], 1):
            bit = step.bit_length() - 1
            place = place + (((apart >> bit) & 1) << (len(steps) - 1 - t))
        table_ref[home] = place

    def one(f):
        first = slots_ref[pairs_ref[0, f]]
        second = slots_ref[pairs_ref[1, f]]
        first_home, second_home = first >> shift, second >> shift
        own = first_home == me
        where = jnp.where(own, devices, 0) + table_ref[jnp.where(own, second_home, first_home)]
        block = wide_ref[pl.ds(f, K, stride=pairs + 8), :]
        block = jnp.concatenate([block] * (clusters * K // block.shape[1]), axis=1)
        block = jnp.where(group == (second & (clusters - 1)), block, 0.0).astype(bf16)
        here = pl.ds(pl.multiple_of((first & (clusters - 1)) * K, K), K)
        out_ref[where, here, :] = out_ref[where, here, :] + block

    def some(step, carry):
        for u in range(32):
            one(step * 32 + u)
        return carry

    lax.fori_loop(0, pairs // 32, some, 0)


def open_kernel(me_ref, pairs_hbm, slots_hbm, coupling_hbm, right_hbm, basis_hbm, near_hbm, blocks_hbm,
                near_pairs_ref, blocks_ref, field_ref, near_proj_ref, coupled_ref, payload_ref,
                pairs_ref, slots_ref, table_ref, coupling_ref, right_ref, basis_ref, wide_ref, sems):
    clusters = field_ref.shape[0]
    moves = [(coupling_hbm, coupling_ref), (basis_hbm, basis_ref), (right_hbm, right_ref),
             (pairs_hbm, pairs_ref), (slots_hbm, slots_ref), (near_hbm, near_pairs_ref), (blocks_hbm, blocks_ref)]
    copies = [pltpu.make_async_copy(*move, sems.at[i]) for i, move in enumerate(moves)]
    for copy in copies:
        copy.start()
    coupled_ref[...] = jnp.zeros_like(coupled_ref)
    copies[0].wait()
    pairs = coupling_ref.shape[0]
    lanes_held = 128
    rows = lax.broadcasted_iota(jnp.int32, (lanes_held, lanes_held), 0)
    lanes = lax.broadcasted_iota(jnp.int32, (lanes_held, lanes_held), 1)
    tiles = coupling_ref.shape[1] // lanes_held
    flat = jnp.concatenate(
        [coupling_ref[:, t * lanes_held : (t + 1) * lanes_held] for t in range(tiles)], axis=0
    )
    each = lanes_held // K
    for u in range(each):
        spread = jnp.where((lanes % K == rows % K) & (rows // K == u), 1.0, 0.0).astype(bf16)
        value = dot(flat, spread)
        for t in range(tiles):
            begin = (t * each + u) * (pairs + 8)
            wide_ref[begin : begin + pairs] = value[t * pairs : (t + 1) * pairs]
    copies[1].wait()
    basis = basis_ref[...]
    copies[2].wait()
    for c in range(clusters):
        field_ref[c] = split_rows(right_ref[:, c * PANEL : (c + 1) * PANEL])
    proj = project(field_ref[...].reshape(clusters * 2 * R, PANEL), basis)
    near_proj_ref[...] = proj
    copies[3].wait()
    copies[4].wait()
    copies[5].wait()
    couple(me_ref[0], pairs_ref, slots_ref, table_ref, wide_ref, coupled_ref)
    proj = proj.astype(bf16)
    devices = coupled_ref.shape[0] // 2
    send(
        lambda d: dot(proj, coupled_ref[devices + d]) + dot_nt(proj, coupled_ref[d]),
        payload_ref, proj, devices, True,
    )
    copies[6].wait()


def send(products, payload_ref, proj, devices, both):
    payload_ref[0] = proj
    half = devices // 2
    for d in range(half, devices):
        value = products(d)
        high = value.astype(bf16)
        payload_ref[1 + d - half] = high
        if both:
            payload_ref[1 + d] = (value - high.astype(f32)).astype(bf16)


def keep_one_kernel(coupled_ref, payload_ref, basis_ref, field_ref, kept_ref, cross_ref, corner_ref):
    devices = coupled_ref.shape[0] // 2
    proj = payload_ref[0]
    for d in range(devices // 2):
        kept_ref[d] = dot(proj, coupled_ref[devices + d]) + dot_nt(proj, coupled_ref[d])
    basis = basis_ref[...]
    cross = dot_nt(basis, basis)
    same = lane_group(cross.shape) == lax.broadcasted_iota(jnp.int32, cross.shape, 0) // K
    cross = jnp.where(same, cross, 0.0)
    high = cross.astype(bf16)
    cross_ref[0] = high
    cross_ref[1] = (cross - high.astype(f32)).astype(bf16)
    corner = jnp.zeros((R, 4 * R), f32)
    for c in range(field_ref.shape[0]):
        right = field_ref[c]
        corner = corner + split_nt(right, *stack(None, None, right, None))
    corner_ref[...] = corner


def keep_two_kernel(turned_ref, payload_ref, kept_ref):
    proj = payload_ref[0]
    for d in range(kept_ref.shape[0]):
        kept_ref[d] = dot(proj, turned_ref[d])


def near_loop(count_ref, one, many=GROUP):
    def group(g, carry):
        for u in range(many):
            one(g * many + u)
        return carry

    lax.fori_loop(0, (count_ref[0] + many - 1) // many, group, 0)


def near_cols_kernel(pairs_ref, count_ref, blocks_ref, field_ref, own_ref, next_ref, total):
    clusters = field_ref.shape[0]
    total[...] = jnp.zeros_like(total)

    def one(s):
        i = pairs_ref[0, s]
        j = jnp.where(s < count_ref[0], pairs_ref[1, s], 2 * clusters)
        total[j] = total[j] + join_rows(dot(field_ref[i], blocks_ref[s]))

    near_loop(count_ref, one)
    own_ref[...] = total[:clusters]
    next_ref[...] = total[clusters : 2 * clusters].astype(bf16)


def near_rows(pairs_ref, count_ref, blocks_ref, field_ref, after_ref, begun_ref, back_ref, basis_ref,
                     out_ref, proj_ref, window, total):
    clusters = field_ref.shape[0]
    window[:clusters] = field_ref[...]
    window[clusters:] = after_ref[...]
    total[:clusters] = begun_ref[...] + back_ref[...].astype(f32)
    total[clusters] = jnp.zeros_like(total[clusters])

    def one(s):
        i = jnp.where(s < count_ref[0], pairs_ref[0, s], clusters)
        j = pairs_ref[1, s]
        total[i] = total[i] + join_rows(dot_nt(window[j], blocks_ref[s]))

    near_loop(count_ref, one, blocks_ref.shape[0])
    near = total[:clusters]
    out_ref[...] = near
    split = jnp.concatenate([split_rows(near[c]) for c in range(clusters)], axis=0)
    proj_ref[...] = project(split, basis_ref[...])
    return split


def rows_one_kernel(*refs):
    near_rows(*refs)


def rows_two_kernel(pairs_ref, count_ref, blocks_ref, field_ref, after_ref, begun_ref, back_ref, basis_ref,
                    right_ref, out_ref, proj_ref, gram_ref, window, total):
    split = near_rows(pairs_ref, count_ref, blocks_ref, field_ref, after_ref, begun_ref, back_ref, basis_ref,
                      out_ref, proj_ref, window, total)
    gram = jnp.zeros((R, 4 * R), f32)
    for c in range(field_ref.shape[0]):
        near = split[c * 2 * R : (c + 1) * 2 * R]
        gram = gram + split_nt(near, *stack(right_ref[c], field_ref[c], near, None))
    gram_ref[...] = gram


def merge_kernel(coupled_ref, out_ref, turned_ref):
    devices = out_ref.shape[0]
    for d in range(devices):
        near, away = coupled_ref[d], coupled_ref[devices + d]
        out_ref[d] = near + away.T
        turned_ref[d] = away + near.T


def far_sums(place, merged_ref, low_ref, high_ref, kept_ref, got_ref):
    devices = merged_ref.shape[0]
    sums = kept_ref[0]
    for piece in range(got_ref.shape[0]):
        sums = sums + got_ref[piece].astype(f32)
    steps = rounds(devices)
    for g in range(devices):
        proj = low_ref[g] if g < devices // 2 else high_ref[g - devices // 2]
        apart = functools.reduce(lambda x, y: x ^ y, [step for t, step in enumerate(steps) if (g >> t) & 1], 0)
        sums = sums + dot(proj, merged_ref[place[apart]])
    return split_rows(sums)


def across_clusters(sums, cross_ref):
    return join_rows(dot(sums, cross_ref[0])) + dot(sums[:R], cross_ref[1])


def turn_kernel(place, merged_ref, low_ref, high_ref, kept_ref, got_ref, near_proj_ref, cross_ref,
                turned_ref, sums_ref, proj_ref, payload_ref):
    sums = far_sums(place, merged_ref, low_ref, high_ref, kept_ref, got_ref)
    sums_ref[...] = sums
    proj = near_proj_ref[...] + across_clusters(sums, cross_ref)
    proj_ref[...] = proj
    proj = proj.astype(bf16)
    send(lambda d: dot(proj, turned_ref[d]), payload_ref, proj, turned_ref.shape[0], False)


def image_kernel(near_ref, sums_ref, basis_ref, image_ref, field_ref):
    far = expand(sums_ref[...], basis_ref[...])
    for c in range(near_ref.shape[0]):
        image = near_ref[c] + join_rows(far[c * 2 * R : (c + 1) * 2 * R])
        image_ref[c] = image
        field_ref[c] = split_rows(image)


def second_kernel(near_ref, sums_ref, basis_ref, image_ref):
    far = expand(sums_ref[...], basis_ref[...])
    for c in range(near_ref.shape[0]):
        image_ref[c] = near_ref[c] + join_rows(far[c * 2 * R : (c + 1) * 2 * R])


def gram_one_kernel(corner_ref, right_ref, image_ref, gram_ref):
    gram = corner_ref[...]
    for c in range(image_ref.shape[0]):
        gram = gram + split_nt(image_ref[c], *stack(right_ref[c], image_ref[c], None, None))
    gram_ref[...] = gram


def tail_kernel(place, merged_ref, low_ref, high_ref, kept_ref, got_ref, near_proj_ref, cross_ref,
                right_proj_ref, image_proj_ref, early_ref, gram_ref, sums_ref, out_ref):
    sums = far_sums(place, merged_ref, low_ref, high_ref, kept_ref, got_ref)
    sums_ref[...] = sums
    half = near_proj_ref[...] + 0.5 * across_clusters(sums, cross_ref)
    known = jnp.concatenate([right_proj_ref[...], image_proj_ref[...], half, jnp.zeros_like(half)], axis=0)
    high = known.astype(bf16)
    added = split_nt(sums, high, (known - high.astype(f32)).astype(bf16))
    mirror = jnp.where(lane_group(added.shape) == 2, jnp.concatenate([added[:, 2 * R : 3 * R].T] * 4, axis=1), 0.0)
    late = gram_ref[...] + added + mirror
    lanes = lane_group(late.shape)
    out_ref[:R] = jnp.where(lanes == 3, pltpu.roll(late, 3 * R, 1), early_ref[...])
    rest = pltpu.roll(late, 3 * R, 1)
    half_rows = R // 2
    out_ref[R:] = jnp.where(lanes[:half_rows] < 2, rest[:half_rows], pltpu.roll(rest[half_rows:], 2 * R, 1))


TALL = 8


def lane(x, k):
    return jnp.broadcast_to(x[:, k : k + 1], x.shape)


def eliminate(wide, late, k):
    block, at = k // TALL, k % TALL
    rows = lax.broadcasted_iota(jnp.int32, wide[block].shape, 0)
    both = [wide] if late is None or block < len(wide) // 2 else [wide, late]
    columns = [[lane(x, k + j) for x in wide[block:]] for j in range(4)]
    m = [[columns[j][0][at + i : at + i + 1] for j in range(4)] for i in range(4)]
    scale = 1.0 / (m[0][0] * m[1][1] - m[0][1] * m[1][0])
    upper = {j: m[1][1] * m[0][j] - m[0][1] * m[1][j] for j in (2, 3)}
    under = {j: m[0][0] * m[1][j] - m[1][0] * m[0][j] for j in (2, 3)}
    s = {
        (i, j): m[i][j] - (m[i][0] * upper[j] + m[i][1] * under[j]) * scale for i in (2, 3) for j in (2, 3)
    }
    after = 1.0 / (s[2, 2] * s[3, 3] - s[2, 3] * s[3, 2])
    ratio, last_ratio = m[1][0] / m[0][0], s[3, 2] / s[2, 2]
    for part in both:
        p = [part[block][at + i : at + i + 1] for i in range(4)]
        y0, y1 = m[1][1] * p[0] - m[0][1] * p[1], m[0][0] * p[1] - m[1][0] * p[0]
        r2 = p[2] - (m[2][0] * y0 + m[2][1] * y1) * scale
        r3 = p[3] - (m[3][0] * y0 + m[3][1] * y1) * scale
        y0, y1 = y0 * scale, y1 * scale
        x2, x3 = s[3, 3] * r2 - s[2, 3] * r3, s[2, 2] * r3 - s[3, 2] * r2
        x0 = (upper[2] * x2 + upper[3] * x3) * scale
        x1 = (under[2] * x2 + under[3] * x3) * scale
        own = [p[0], p[1] - ratio * p[0], r2, r3 - last_ratio * r2]
        for i in range(block, len(wide)):
            c = [column[i - block] for column in columns]
            begun = part[i] - (c[0] * y0 + c[1] * y1)
            rest = begun - ((c[2] * x2 + c[3] * x3) - (c[0] * x0 + c[1] * x1)) * after
            if i == block:
                rest = jnp.where(rows > at + 3, rest, part[i])
                for t in range(1, 4):
                    rest = jnp.where(rows == at + t, own[t], rest)
            part[i] = rest


def last_kernel(kept_ref, got_ref, right_ref, image_ref, second_ref, field_ref, residual_ref, hessenberg_ref):
    clusters = image_ref.shape[0]
    gram = kept_ref[...] + got_ref[...]
    top, folded = gram[:R], gram[R:]
    bottom = jnp.concatenate([folded[:, : 2 * R], folded[:, 2 * R :]], axis=0)
    lanes = lax.broadcasted_iota(jnp.int32, (2 * R, 4 * R), 1)
    rows = lax.broadcasted_iota(jnp.int32, (2 * R, 4 * R), 0)
    wide = jnp.zeros((R, R), f32)
    first_first, image_first = top[:, 2 * R : 3 * R], top[:, :R]
    image_image, second_first = top[:, R : 2 * R], top[:, 3 * R :]
    second_image, second_second = bottom[:, :R], bottom[:, R:]
    on_diagonal = lax.broadcasted_iota(jnp.int32, (R, R), 0) == lax.broadcasted_iota(jnp.int32, (R, R), 1)

    def shrink(x):
        trace = jnp.sum(jnp.where(on_diagonal, x, 0.0), axis=0, keepdims=True)
        return lax.rsqrt(jnp.sum(trace, axis=1, keepdims=True) / R)

    at_first, at_image, at_second = shrink(first_first), shrink(image_image), shrink(second_second)
    stretch = at_first / at_image
    first_first, image_first = first_first * at_first * at_first, image_first * at_image * at_first
    image_image, second_second = image_image * at_image * at_image, second_second * at_second * at_second
    second_image, second_first = second_image * at_second * at_image, second_first * at_second * at_first
    system = jnp.concatenate(
        [
            jnp.concatenate([image_image, second_image.T, image_first, wide], axis=1),
            jnp.concatenate([second_image, second_second, second_first, wide], axis=1),
        ],
        axis=0,
    )
    lower = jnp.concatenate(
        [
            jnp.concatenate([first_first, image_first.T, wide, wide], axis=1),
            jnp.concatenate([image_first, image_image, wide, wide], axis=1),
        ],
        axis=0,
    )
    lower = jnp.where(lanes - 2 * R == rows, 1.0, lower)
    system = jnp.where(lanes - 3 * R == rows, 1.0, system)
    late = jnp.where(lanes + R == rows, 1.0, 0.0)

    def blocks(x):
        return [x[i : i + TALL] for i in range(0, 2 * R, TALL)]

    system, lower, late = blocks(system), blocks(lower), blocks(late)
    for k in range(0, 2 * R, 4):
        eliminate(system, late, k)
        eliminate(lower, None, k)
    system, lower, late = (jnp.concatenate(x, axis=0) for x in (system, lower, late))

    def diagonal(x):
        return jnp.sum(jnp.where(lanes == rows, x, 0.0), axis=1, keepdims=True)

    lower = lower * lax.rsqrt(diagonal(lower))
    scaled = system[:, 2 * R : 3 * R] / diagonal(system)
    inverse = jnp.concatenate([system[:, 3 * R :], late[:, :R]], axis=1)
    weights = lax.dot_general(scaled, inverse, TN, precision=highest, preferred_element_type=f32)
    weights = weights * jnp.where(lanes[:R, : 2 * R] < R, at_image, at_second) / at_first
    inverse_zero = lower[:R, 2 * R : 3 * R]
    hessenberg_ref[:, :R] = stretch * exact_nt(inverse_zero, lower[:R, R : 2 * R])
    hessenberg_ref[:, R:] = stretch * lax.dot_general(
        lower[R:, R : 2 * R], inverse_zero, NT, precision=highest, preferred_element_type=f32
    )
    none = jnp.zeros((R, R), f32)
    mix = jnp.concatenate(
        [jnp.concatenate([weights, none], axis=1), jnp.concatenate([none, weights], axis=1)], axis=0
    )
    mix_high = mix.astype(bf16)
    mix_both = jnp.concatenate([mix_high, (mix - mix_high.astype(f32)).astype(bf16)], axis=0)
    for c in range(clusters):
        here = slice(c * PANEL, (c + 1) * PANEL)
        right = right_ref[:, here]
        stacked = jnp.concatenate([right, image_ref[c], second_ref[c]], axis=0)
        high = stacked.astype(bf16)
        low = (stacked - high.astype(f32)).astype(bf16)
        both = dot(mix_both, high)
        value = both[: 2 * R] + both[2 * R :] + dot(mix_high, low)
        field_ref[:, here] = value[:R]
        residual_ref[:, here] = right - value[R:]


def body(right_side, near_pairs, near_count, near_blocks, far_pairs, coupling, cluster_basis, cluster_slot):
    devices = lax.axis_size("leaf")
    order, place = rounds(devices), places(devices)
    clusters = cluster_basis.shape[0]
    me = lax.axis_index("leaf").astype(jnp.int32).reshape(1)
    basis = cluster_basis.reshape(clusters * K, PANEL)
    sds = jax.ShapeDtypeStruct

    def across(x, b):
        return lax.ppermute(x, "leaf", [(i, i ^ b) for i in range(devices)])

    def shift(x, by):
        return lax.ppermute(x, "leaf", [(i, i + by) for i in range(devices) if 0 <= i + by < devices])

    panels = sds((clusters, R, PANEL), f32)
    narrow = sds((clusters, R, PANEL), bf16)
    split = sds((clusters, 2 * R, PANEL), bf16)
    rank_wide = sds((R, clusters * K), f32)
    rank_split = sds((2 * R, clusters * K), bf16)
    half = devices // 2
    merged_out = sds((devices, clusters * K, clusters * K), bf16)
    payload_out = sds((1 + half, R, clusters * K), bf16)
    kept_out = sds((half, R, clusters * K), f32)
    barrier = lax.optimization_barrier
    near_spaces = [SMEM, SMEM, VMEM, VMEM]

    def in_hbm(x):
        return pltpu.with_memory_space_constraint(x, pltpu.HBM)

    near_pairs, near_blocks, field, right_proj, coupled, payload = call(
        open_kernel,
        (sds(near_pairs.shape, jnp.int32), sds(near_blocks.shape, bf16), split, rank_wide,
         sds((2 * devices, clusters * K, clusters * K), bf16),
         sds((1 + devices, R, clusters * K), bf16)),
        (me, in_hbm(far_pairs), in_hbm(cluster_slot), in_hbm(coupling), in_hbm(right_side), in_hbm(basis),
         in_hbm(near_pairs), in_hbm(near_blocks)),
        [SMEM] + [pltpu.HBM] * 7,
        [
            pltpu.SMEM(far_pairs.shape, jnp.int32),
            pltpu.SMEM(cluster_slot.shape, jnp.int32),
            pltpu.SMEM((devices,), jnp.int32),
            pltpu.VMEM(coupling.shape, bf16),
            pltpu.VMEM(right_side.shape, f32),
            pltpu.VMEM(basis.shape, bf16),
            pltpu.VMEM(((coupling.shape[0] + 8) * (K + 1), 128), f32),
            pltpu.SemaphoreType.DMA((7,)),
        ],
        placed=[SMEM] + [VMEM] * 5,
    )

    right_field = field

    def exchange(make_field, beside, keep, payload, merged=None):
        first = merged is None
        for t, b in enumerate(order):
            if t > 0:
                held, half = gathered.shape[0], sums.shape[0] // 2
                payload = jnp.concatenate([gathered, sums[half:].astype(bf16)], axis=0)
                sums = sums[:half]
            else:
                gathered, held = payload[:1], 1
            if t == 2:
                payload, own = barrier((payload, own))
            if t == 3:
                payload, made = barrier((payload, made))
            got = across(payload, b)
            if t == 0:
                sums, cross, corner = keep(payload)
                image, field, got = make_field(got)
                after = shift(field, -1)
                own, following = call(
                    near_cols_kernel, (panels, narrow), (near_pairs, near_count, near_blocks, field), near_spaces,
                    [pltpu.VMEM((2 * clusters + 1, R, PANEL), f32)], moved=12 << 20,
                )
                back = shift(following, 1)
            if t == 1:
                made, got = beside(field, corner, got)
            if t == len(order) - 2:
                after, got = barrier((after, got))
            got_gathered, got_sums = got[:held], got[held:]
            if t < len(order) - 1:
                gathered = jnp.concatenate([gathered, got_gathered], axis=0)
                for piece in range(0, got_sums.shape[0], sums.shape[0]):
                    sums = sums + got_sums[piece : piece + sums.shape[0]].astype(f32)
        kernel, ins, outs = rows_one_kernel, (near_blocks, field, after, own, back, basis), (panels, rank_wide)
        if not first:
            kernel, ins, outs = rows_two_kernel, ins + (right_field,), outs + (sds((R, 4 * R), f32),)
        near, near_proj, *gram = call(
            kernel, outs, (near_pairs, near_count) + ins, [SMEM] * 2 + [VMEM] * len(ins),
            [pltpu.VMEM((2 * clusters, 2 * R, PANEL), bf16), pltpu.VMEM((clusters + 1, R, PANEL), f32)],
            moved=12 << 20,
        )
        merged = made if first else merged
        return image, near, made, gram, cross, corner, (merged[0], gathered, got_gathered, sums, got_sums, near_proj, cross)

    def first_field(got):
        ready, got = barrier((field, got))
        return right_side, ready, got

    def keep_one(payload):
        return call(
            keep_one_kernel, (kept_out, sds((2, clusters * K, clusters * K), bf16), sds((R, 4 * R), f32)),
            (coupled, payload, basis, right_field), [VMEM] * 4,
        )

    def merging(image, corner, got):
        ready, got = barrier((coupled, got))
        return call(merge_kernel, (merged_out, merged_out), (ready,), [VMEM]), got

    def multiplying(image, corner, got):
        ready, got = barrier((image, got))
        return call(gram_one_kernel, sds((R, 4 * R), f32), (corner, right_field, ready), [VMEM] * 3), got

    unused, near, merged, unused, cross, corner, parts = exchange(first_field, merging, keep_one, payload)
    far, image_proj, payload = call(
        functools.partial(turn_kernel, place), (rank_split, rank_wide, payload_out), parts + (merged[1],), [VMEM] * 8
    )

    def second_field(got):
        ready, got = barrier((far, got))
        return *call(image_kernel, (panels, split), (near, ready, basis), [VMEM] * 3), got

    def keep_two(payload):
        return call(keep_two_kernel, kept_out, (merged[1], payload), [VMEM] * 2), cross, corner

    image, near_two, early, gram, unused, unused, parts = exchange(
        second_field, multiplying, keep_two, payload, merged
    )
    far, gram = call(
        functools.partial(tail_kernel, place), (rank_split, sds((R + R // 2, 4 * R), f32)),
        parts + (right_proj, image_proj, early, *gram), [VMEM] * 11,
    )
    got = None
    for t, b in enumerate(order):
        if t > 0:
            gram = gram + got
        if t == 2:
            gram, second = barrier((gram, second))
        got = across(gram, b)
        if t == 0:
            far, got = barrier((far, got))
            second = call(second_kernel, panels, (near_two, far, basis), [VMEM] * 3)
    wide = sds(right_side.shape, f32)
    solution_field, residual, hessenberg = call(
        last_kernel, (wide, wide, sds((R, 2 * R), f32)), (gram, got, right_side, image, second), [VMEM] * 5
    )
    return solution_field, residual, hessenberg.T


def solution(mesh):
    in_specs = (
        P(None, ("parts", "leaf")),
        P(None, ("parts", "leaf")),
        P(("parts", "leaf")),
        P(("parts", "leaf"), None, None),
        P(None, ("parts", "leaf")),
        P(("parts", "leaf"), None),
        P(("parts", "leaf"), None, None),
        P("parts"),
    )
    out_specs = (P(None, ("parts", "leaf")), P(None, ("parts", "leaf")), P("parts", None))
    return jax.shard_map(body, mesh=mesh, in_specs=in_specs, out_specs=out_specs, check_vma=False)
```
